128 devices in a mesh: dp: 8 (over y_hi, x), field: 16 (over y_lo, z, core).
Axes of the slice: x: 4, y: 4 (y_hi: 2, y_lo: 2; y = y_hi * 2 + y_lo), z: 4, core: 2. Of those that a mesh axis runs over, the one named last changes fastest.
Arguments:
- emb: bfloat16 [1024, 512, 192], P('dp', 'field'), may hold values from -6 to 6
- comp: bfloat16 [512, 128], P('field'), may hold values from -0.15625 to 0.15625
- cot: bfloat16 [1024, 512, 128], P('dp', 'field'), may hold values from -6 to 6
- pairs: int32 [1152, 2], P('field'), may hold values from 0 to 15, as said below
- counts: int32 [16], P('field'), may hold values from 1 to 72, as said below
Outputs:
- mixed: bfloat16 [1024, 512, 128], P('dp', 'field')
- emb_grad: bfloat16 [1024, 512, 192], P('dp', 'field')
- weight_grad: float32 [512, 128], P('field')
The draws below stay inside these ranges and needn't reach their ends.
Inputs may be any that keep to these rules, and one draw needn't show every extreme that they name: `pairs`: each row names two field tiles, the first at most the second; rows may repeat. Field index f uses its first counts[f] rows; the counts sum to 384; the largest is exactly 72.
All inputs are finite; a program needn't handle non-finite values.
Results may differ from the reference program's by a relative error of at most 0.011.
Values may be sent and summed in bfloat16 or wider, within the bound.
No kernel may reach another device: no remote copies, remote signals or barrier semaphores. Data moves between devices by JAX's collectives and lax.ppermute only.
A program may use at most 192 MiB of HBM per device.

```python
import jax
import jax.numpy as jnp
from jax import lax

D = 192
K = 128
TILE = 32
SLOTS = 72
MEAN_LIVE = 24
N_EMB = 512
SAMPLES = 1024
N_FIELD = 16


def draw_pairs(key, part):
    key = jax.random.fold_in(key, 11)
    both = jax.random.randint(key, (N_FIELD * SLOTS, 2), 0, N_FIELD)
    return jnp.stack([jnp.min(both, axis=1), jnp.max(both, axis=1)], axis=1).astype(jnp.int32)


def draw_counts(key, part):
    key = jax.random.fold_in(key, 23)
    first_key, second_key = jax.random.split(key)
    others = N_FIELD - 1
    remain = MEAN_LIVE * N_FIELD - SLOTS
    base = remain // others
    extra = remain - base * others
    order = jnp.arange(others)
    offsets = jax.random.randint(first_key, (others,), 0, base)
    paired = offsets[order // 2 * 2]
    signs = jnp.where(order % 2 == 0, 1, -1)
    single = (order == others - 1) & (others % 2 == 1)
    values = base + jnp.where(single, 0, signs * paired) + (order < extra).astype(jnp.int32)
    values = jnp.concatenate([jnp.full((1,), SLOTS, jnp.int32), values.astype(jnp.int32)])
    perm = jax.random.permutation(second_key, N_FIELD)
    return jnp.zeros((N_FIELD,), jnp.int32).at[perm].set(values).astype(jnp.int32)


def block_scale(own_key, dims, cuts, least, high):
    gain = 1.0
    for position, blocks in cuts:
        heights = jax.random.uniform(jax.random.fold_in(jax.random.fold_in(own_key, 6), position), (blocks,), jnp.float32, least / len(cuts), high / len(cuts))
        gain = gain * jnp.repeat(jnp.exp(heights), dims[position] // blocks).reshape((-1,) + (1,) * (len(dims) - 1 - position))
    return gain


def noise(own_key, shape, width, bound, pieces=(), kind=jnp.bfloat16):
    factor_of = block_scale(own_key, shape, pieces, -0.22, 0.18) if pieces else 1.0
    array = jax.random.normal(own_key, shape, jnp.float32) * width * factor_of
    return jnp.minimum(jnp.maximum(array, -bound), bound).astype(kind)


def setup_inputs(seed: int = 0) -> dict:
    streams_of = jax.random.split(jax.random.key(seed), 6)
    emb = noise(streams_of[0], (SAMPLES, N_EMB, D), 1.0, 6.0, ((0, 8), (1, 16)))
    comp = noise(streams_of[1], (N_EMB, K), (2 * MEAN_LIVE * TILE) ** -0.5, 0.15625, ((0, 16),))
    cot = noise(streams_of[2], (SAMPLES, N_EMB, K), 1.0, 6.0, ((0, 8), (1, 16)))
    pairs = draw_pairs(jax.random.fold_in(streams_of[5], 71), 0)
    counts = draw_counts(jax.random.fold_in(streams_of[5], 71), 0)
    return dict(emb=emb, comp=comp, cot=cot, pairs=pairs, counts=counts)


def tile_mask(pairs, counts):
    slots = pairs.shape[0] // N_FIELD
    live = (jnp.arange(slots)[None, :] < counts[:, None]).reshape(-1).astype(jnp.float32)
    first = jax.nn.one_hot(pairs[:, 0], N_FIELD, dtype=jnp.float32) * live[:, None]
    second = jax.nn.one_hot(pairs[:, 1], N_FIELD, dtype=jnp.float32)
    table = jnp.dot(first.T, second, precision=lax.Precision.HIGHEST)
    mult = table + table.T - jnp.diag(jnp.diag(table))
    return jnp.repeat(jnp.repeat(mult, TILE, axis=0), TILE, axis=1)


def reference(emb, comp, cot, pairs, counts):
    scale = D ** -0.5
    mask = tile_mask(pairs, counts)
    weights = comp.astype(jnp.float32)

    def one_sample(items):
        feats, grads = items
        gram = (scale * jnp.dot(feats, feats.T, preferred_element_type=jnp.float32)).astype(jnp.bfloat16)
        masked = mask * gram.astype(jnp.float32)
        output = jnp.dot(masked, weights, precision=lax.Precision.HIGHEST)
        hmat = jnp.dot(grads, comp.T, preferred_element_type=jnp.float32)
        sym = (scale * (hmat + hmat.T)).astype(jnp.bfloat16)
        dfeat = jnp.dot(mask * sym.astype(jnp.float32), feats.astype(jnp.float32), precision=lax.Precision.HIGHEST)
        dweight = jnp.dot(masked.T, grads.astype(jnp.float32), precision=lax.Precision.HIGHEST)
        return output.astype(jnp.bfloat16), dfeat.astype(jnp.bfloat16), dweight

    def step(total, items):
        output, dfeat, dweight = one_sample(items)
        return total + dweight, (output, dfeat)

    start = jnp.zeros((N_EMB, K), jnp.float32)
    total, (mixed, emb_grad) = lax.scan(step, start, (emb, cot))
    return mixed, emb_grad, total / SAMPLES
```

```python
import functools

import jax
import jax.numpy as jnp
from jax import lax
from jax.experimental import pallas as pl
from jax.experimental.pallas import tpu as pltpu
from jax.sharding import PartitionSpec as P

LANES = 128
VMEM_LIMIT = 56 * 1024 * 1024


def identity():
    shape = (LANES, LANES)
    same = lax.broadcasted_iota(jnp.int32, shape, 0) == lax.broadcasted_iota(jnp.int32, shape, 1)
    return jnp.where(same, 1.0, 0.0).astype(jnp.bfloat16)


def pack_kernel(emb_ref, cot_ref, comp_ref, pairs_ref, counts_ref, out_ref, turned):
    tile, width, samples = emb_ref.shape
    fields = out_ref.shape[0]
    per_peer = samples // fields
    half = tile // 2
    rows = 2 * tile + half
    f32, bf16 = jnp.float32, jnp.bfloat16
    eye = identity()
    turn = (((1,), (1,)), ((), ()))
    for r in range(tile + half):
        if r < tile:
            block = emb_ref[r, :LANES]
        else:
            block = jnp.concatenate([emb_ref[r - tile, LANES:], emb_ref[r - half, LANES:]], axis=0)
        turned[r * samples : (r + 1) * samples] = lax.dot_general(
            eye, block, turn, preferred_element_type=f32
        )

    slots = pairs_ref.shape[1]
    number = lax.broadcasted_iota(jnp.int32, (LANES, slots), 0)
    live = lax.broadcasted_iota(jnp.int32, (LANES, slots), 1) < counts_ref[0]
    first = jnp.where((pairs_ref[0:1] == number) & live, 1.0, 0.0).astype(bf16)
    second = jnp.where(pairs_ref[1:2] == number, 1.0, 0.0).astype(bf16)
    table = lax.dot_general(first, second, turn, preferred_element_type=f32)[:16].astype(bf16)

    def peer(p, carry):
        for s in range(per_peer):
            number = p * per_peer + s
            both = turned[pl.ds(number, tile + half, stride=samples), :].astype(bf16)
            base = s * rows
            out_ref[p, base : base + tile] = both[:tile]
            out_ref[p, base + tile : base + 2 * tile] = cot_ref[number]
            out_ref[p, base + 2 * tile : base + rows] = both[tile:]
        base = per_peer * rows
        out_ref[p, base : base + tile] = comp_ref[...]
        out_ref[p, base + tile : base + tile + 16] = table
        return carry

    lax.fori_loop(0, fields, peer, 0)


def block_kernel(per_peer, scale, x_ref, y_ref, emb, sides, other, mask, grad):
    fields = x_ref.shape[0]
    tile = 32
    half, rest = tile // 2, emb.shape[1] - LANES
    rows = 2 * tile + half
    embeds = fields * tile
    f32, bf16 = jnp.float32, jnp.bfloat16
    base = per_peer * rows

    table = jnp.zeros((16, LANES), f32)
    for f in range(fields):
        table += x_ref[f, base + tile : base + tile + 16].astype(f32)
    square = jnp.concatenate([table, jnp.zeros((LANES - 16, LANES), f32)], axis=0)
    on_diag = lax.broadcasted_iota(jnp.int32, square.shape, 0) == lax.broadcasted_iota(
        jnp.int32, square.shape, 1
    )
    mult = (square + square.T - jnp.where(on_diag, square, 0.0)) * scale
    for a in range(fields):
        row = jnp.concatenate(
            [jnp.broadcast_to(mult[a : a + 1, b : b + 1], (1, tile)) for b in range(fields)], axis=1
        )
        mask[a * tile : (a + 1) * tile] = jnp.broadcast_to(row, (tile, embeds))

    weights = x_ref[:, base : base + tile].reshape(embeds, LANES)
    sides[:, :LANES] = weights
    other[:, LANES:] = weights
    grad[...] = jnp.zeros_like(grad)
    lane = lax.broadcasted_iota(jnp.int32, (fields, half, LANES), 2)

    def sample(s, carry):
        start = pl.multiple_of(s * rows, 16)
        emb[:, :LANES] = x_ref[:, pl.ds(start, tile)].reshape(embeds, LANES)
        cot = x_ref[:, pl.ds(start + tile, tile)].reshape(embeds, LANES)
        sides[:, LANES:] = cot
        other[:, :LANES] = cot
        tail = x_ref[:, pl.ds(start + 2 * tile, half)]
        upper = jnp.concatenate([tail[:, :, rest:], tail[:, :, :rest]], axis=2)
        both = jnp.concatenate([tail, upper], axis=1).reshape(embeds, LANES)
        emb[:, LANES:] = both[:, :rest]
        feats = emb[...]
        gram = lax.dot_general(feats, feats, (((1,), (1,)), ((), ())), preferred_element_type=f32)
        masked = (mask[...] * gram).astype(bf16)
        both = jnp.dot(masked, sides[...], preferred_element_type=f32)
        grad[...] += both[:, LANES:]
        y_ref[:, pl.ds(start, tile)] = both[:, :LANES].astype(bf16).reshape(fields, tile, LANES)
        hmat = lax.dot_general(
            other[...], sides[...], (((1,), (1,)), ((), ())), preferred_element_type=f32
        )
        sym = (mask[...] * hmat).astype(bf16)
        dfeat = jnp.dot(sym, feats, preferred_element_type=f32).astype(bf16)
        y_ref[:, pl.ds(start + tile, tile)] = dfeat[:, :LANES].reshape(fields, tile, LANES)
        last = dfeat[:, LANES:].reshape(fields, tile, rest)
        y_ref[:, pl.ds(start + 2 * tile, half)] = jnp.concatenate(
            [last[:, :half], last[:, half:]], axis=2
        )
        return carry

    lax.fori_loop(0, per_peer, sample, 0)
    y_ref[:, base : base + tile] = grad[...].astype(bf16).reshape(fields, tile, LANES)


def unpack_kernel(y_ref, mixed_ref, dfeat_ref, turned):
    tile, width, samples = dfeat_ref.shape
    fields = y_ref.shape[0]
    per_peer = samples // fields
    half, rest = tile // 2, width - LANES
    rows = 2 * tile + half
    f32, bf16 = jnp.float32, jnp.bfloat16

    def peer(p, carry):
        for s in range(per_peer):
            number = p * per_peer + s
            base = s * rows
            mixed_ref[number] = y_ref[p, base : base + tile]
            turned[pl.ds(number, tile + half, stride=samples), :] = y_ref[
                p, base + tile : base + rows
            ].astype(f32)
        return carry

    lax.fori_loop(0, fields, peer, 0)
    eye = identity()
    for r in range(tile + half):
        block = turned[r * samples : (r + 1) * samples].astype(bf16)
        block = lax.dot_general(
            block, eye, (((0,), (0,)), ((), ())), preferred_element_type=f32
        ).astype(bf16)
        if r < tile:
            dfeat_ref[r, :LANES] = block
        else:
            dfeat_ref[r - tile, LANES:] = block[:rest]
            dfeat_ref[r - half, LANES:] = block[rest:]


def dp_sum(x):
    size = lax.axis_size("dp")
    total = x
    for k in range(1, size):
        total = total + lax.ppermute(x, "dp", [(i, i ^ k) for i in range(size)])
    return total


def per_device(emb, comp, cot, pairs, counts):
    samp_rows, tile, width = emb.shape
    fields = lax.axis_size("field")
    per_peer = samp_rows // fields
    embeds = tile * fields
    packed = tile + tile // 2
    rows = packed + tile
    f32, bf16 = jnp.float32, jnp.bfloat16
    params = pltpu.CompilerParams(vmem_limit_bytes=VMEM_LIMIT)
    vmem = pl.BlockSpec(memory_space=pltpu.VMEM)
    sent = per_peer * rows + tile + 16
    back = per_peer * rows + tile
    x = pl.pallas_call(
        pack_kernel,
        out_shape=jax.ShapeDtypeStruct((fields, sent, LANES), bf16),
        in_specs=[vmem, vmem, vmem, vmem, pl.BlockSpec(memory_space=pltpu.SMEM)],
        out_specs=vmem,
        scratch_shapes=[pltpu.VMEM((packed * samp_rows, LANES), f32)],
        compiler_params=params,
    )(jnp.transpose(emb, (1, 2, 0)), cot, comp, pairs.T, counts)
    x = lax.all_to_all(x, "field", 0, 0)
    y = pl.pallas_call(
        functools.partial(block_kernel, per_peer, width ** (-0.5)),
        out_shape=jax.ShapeDtypeStruct((fields, back, LANES), bf16),
        in_specs=[vmem],
        out_specs=vmem,
        scratch_shapes=[
            pltpu.VMEM((embeds, width), bf16),
            pltpu.VMEM((embeds, 2 * LANES), bf16),
            pltpu.VMEM((embeds, 2 * LANES), bf16),
            pltpu.VMEM((embeds, embeds), f32),
            pltpu.VMEM((embeds, LANES), f32),
        ],
        compiler_params=params,
    )(x)
    y = lax.all_to_all(y, "field", 0, 0)
    grad = dp_sum(jnp.sum(y[:, per_peer * rows :].astype(f32), axis=0))
    mixed, emb_grad = pl.pallas_call(
        unpack_kernel,
        out_shape=(
            jax.ShapeDtypeStruct((samp_rows, tile, LANES), bf16),
            jax.ShapeDtypeStruct((tile, width, samp_rows), bf16),
        ),
        in_specs=[vmem],
        out_specs=(vmem, vmem),
        scratch_shapes=[pltpu.VMEM((packed * samp_rows, LANES), f32)],
        compiler_params=params,
        cost_estimate=pl.CostEstimate(flops=10**9, bytes_accessed=6 * 10**6, transcendentals=0),
    )(y)
    weight_grad = grad / (samp_rows * lax.axis_size("dp"))
    return mixed, jnp.transpose(emb_grad, (2, 0, 1)), weight_grad


def solution(mesh):
    in_specs = (
        P("dp", "field", None),
        P("field", None),
        P("dp", "field", None),
        P("field", None),
        P("field"),
    )
    out_specs = (P("dp", "field", None), P("dp", "field", None), P("field", None))
    return jax.shard_map(
        per_device, mesh=mesh, in_specs=in_specs, out_specs=out_specs, check_vma=False
    )
```

```python
import functools

import jax
import jax.numpy as jnp
from jax import lax
from jax.experimental import pallas as pl
from jax.experimental.pallas import tpu as pltpu
from jax.sharding import PartitionSpec as P

LANES = 128
CHUNKS = 1
TABLE = 16
TURN = (((1,), (1,)), ((), ()))
MIB = 1024 * 1024


def pack_kernel(chunk, emb_ref, cot_ref, *refs):
    *extras, out_ref, turned = refs
    tile, width, samples = emb_ref.shape
    fields = out_ref.shape[0]
    step = samples // CHUNKS
    each = step // fields
    half = tile // 2
    rows = 2 * tile + half
    f32, bf16 = jnp.float32, jnp.bfloat16
    lanes = slice(chunk * step, (chunk + 1) * step)
    for r in range(tile + half):
        if r < tile:
            block = emb_ref[r, :LANES]
        else:
            block = jnp.concatenate([emb_ref[r - tile, LANES:], emb_ref[r - half, LANES:]], axis=0)
        turned[r * step : (r + 1) * step] = block.astype(f32).T[lanes]

    def peer(p, carry):
        for j in range(each):
            number = p * each + j
            both = turned[pl.ds(number, tile + half, stride=step), :].astype(bf16)
            base = j * rows
            out_ref[p, base : base + tile] = both[:tile]
            out_ref[p, base + tile : base + 2 * tile] = cot_ref[number]
            out_ref[p, base + 2 * tile : base + rows] = both[tile:]
        return carry

    lax.fori_loop(0, fields, peer, 0)
    if chunk == 0:
        comp_ref, pairs_ref, counts_ref = extras
        slots = pairs_ref.shape[1]
        number = lax.broadcasted_iota(jnp.int32, (LANES, slots), 0)
        live = lax.broadcasted_iota(jnp.int32, (LANES, slots), 1) < counts_ref[0]
        first = jnp.where((pairs_ref[0:1] == number) & live, 1.0, 0.0).astype(bf16)
        second = jnp.where(pairs_ref[1:2] == number, 1.0, 0.0).astype(bf16)
        table = lax.dot_general(first, second, TURN, preferred_element_type=f32)
        base = each * rows
        for p in range(fields):
            out_ref[p, base : base + tile] = comp_ref[...]
            out_ref[p, base + tile : base + tile + TABLE] = table[:TABLE].astype(bf16)


def pair_mask(x_ref, base, scale, mask, tile):
    fields = x_ref.shape[0]
    f32 = jnp.float32
    table = jnp.zeros((TABLE, LANES), f32)
    for f in range(fields):
        table += x_ref[f, base : base + TABLE].astype(f32)
    square = jnp.concatenate([table, jnp.zeros((LANES - TABLE, LANES), f32)], axis=0)
    on_diag = lax.broadcasted_iota(jnp.int32, square.shape, 0) == lax.broadcasted_iota(
        jnp.int32, square.shape, 1
    )
    mult = (square + square.T - jnp.where(on_diag, square, 0.0)) * scale
    for a in range(fields):
        row = jnp.concatenate(
            [jnp.broadcast_to(mult[a : a + 1, b : b + 1], (1, tile)) for b in range(fields)], axis=1
        )
        mask[a * tile : (a + 1) * tile] = jnp.broadcast_to(row, (tile, row.shape[1]))


def block_kernel(chunk, scale, tile, width, x_ref, *refs):
    fields = x_ref.shape[0]
    half, rest = tile // 2, width - LANES
    rows = 2 * tile + half
    embeds = fields * tile
    f32, bf16 = jnp.float32, jnp.bfloat16
    emb, sides, other = refs[-3:]
    if chunk == 0:
        y_ref, mask, weights, grad = refs[:-3]
        each = (x_ref.shape[1] - tile - TABLE) // rows
        base = each * rows
        pair_mask(x_ref, base + tile, scale, mask, tile)
        weights[...] = x_ref[:, base : base + tile].reshape(embeds, LANES)
        grad[...] = jnp.zeros_like(grad)
    else:
        mask, weights, grad, y_ref = refs[:-3]
        each = x_ref.shape[1] // rows
    sides[:, :LANES] = weights[...]
    other[:, LANES:] = weights[...]

    def sample(j, total):
        start = pl.multiple_of(j * rows, 16)
        emb[:, :LANES] = x_ref[:, pl.ds(start, tile)].reshape(embeds, LANES)
        cot = x_ref[:, pl.ds(start + tile, tile)].reshape(embeds, LANES)
        sides[:, LANES:] = cot
        other[:, :LANES] = cot
        tail = x_ref[:, pl.ds(start + 2 * tile, half)]
        upper = jnp.concatenate([tail[:, :, rest:], tail[:, :, :rest]], axis=2)
        both = jnp.concatenate([tail, upper], axis=1).reshape(embeds, LANES)
        emb[:, LANES:] = both[:, :rest]
        feats = emb[...]
        gram = lax.dot_general(feats, feats, TURN, preferred_element_type=f32)
        masked = (mask[...] * gram).astype(bf16)
        both = jnp.dot(masked, sides[...], preferred_element_type=f32)
        grad[...] += both[:, LANES:]
        y_ref[:, pl.ds(start, tile)] = both[:, :LANES].astype(bf16).reshape(fields, tile, LANES)
        hmat = lax.dot_general(other[...], sides[...], TURN, preferred_element_type=f32)
        sym = (mask[...] * hmat).astype(bf16)
        dfeat = jnp.dot(sym, feats, preferred_element_type=f32).astype(bf16)
        y_ref[:, pl.ds(start + tile, tile)] = dfeat[:, :LANES].reshape(fields, tile, LANES)
        last = dfeat[:, LANES:].reshape(fields, tile, rest)
        y_ref[:, pl.ds(start + 2 * tile, half)] = jnp.concatenate(
            [last[:, :half], last[:, half:]], axis=2
        )
        return total

    lax.fori_loop(0, each, sample, 0)
    if chunk == CHUNKS - 1:
        y_ref[:, each * rows :] = grad[...].astype(bf16).reshape(fields, tile, LANES)


def unpack_kernel(chunk, y_ref, *refs):
    *before, mixed_ref, dfeat_ref, turned = refs
    tile, width, samples = dfeat_ref.shape
    fields = y_ref.shape[0]
    step = samples // CHUNKS
    each = step // fields
    half, rest = tile // 2, width - LANES
    rows = 2 * tile + half
    f32, bf16 = jnp.float32, jnp.bfloat16

    def peer(p, carry):
        for j in range(each):
            number = p * each + j
            base = j * rows
            mixed_ref[number] = y_ref[p, base : base + tile]
            turned[pl.ds(number, tile + half, stride=step), :] = y_ref[
                p, base + tile : base + rows
            ].astype(f32)
        return carry

    lax.fori_loop(0, fields, peer, 0)
    for r in range(tile + half):
        block = turned[r * step : (r + 1) * step].T.astype(bf16)
        pieces = (
            [(r, slice(0, LANES), block)]
            if r < tile
            else [
                (r - tile, slice(LANES, width), block[:rest]),
                (r - half, slice(LANES, width), block[rest:]),
            ]
        )
        for row, part, piece in pieces:
            if chunk > 0:
                piece = jnp.concatenate([before[1][row, part, : chunk * step], piece], axis=1)
            dfeat_ref[row, part, : (chunk + 1) * step] = piece


def dp_sum(x):
    size = lax.axis_size("dp")
    copies = lax.optimization_barrier(jnp.broadcast_to(x, (size,) + x.shape))
    return jnp.sum(lax.all_to_all(copies, "dp", 0, 0), axis=0)


def per_device(emb, comp, cot, pairs, counts):
    samp_rows, tile, width = emb.shape
    fields = lax.axis_size("field")
    embeds = tile * fields
    packed = tile + tile // 2
    rows = packed + tile
    step = samp_rows // CHUNKS
    each = step // fields
    f32, bf16 = jnp.float32, jnp.bfloat16
    params = pltpu.CompilerParams(vmem_limit_bytes=24 * MIB)
    vmem = pl.BlockSpec(memory_space=pltpu.VMEM)
    smem = pl.BlockSpec(memory_space=pltpu.SMEM)
    turned = pltpu.VMEM((packed * step, LANES), f32)
    emb = jnp.transpose(emb, (1, 2, 0))
    whole_emb = pl.BlockSpec(emb.shape, lambda i: (0, 0, 0))

    def part_of(chunk):
        return pl.BlockSpec((step, tile, LANES), lambda i: (chunk, 0, 0))

    def cost(flops, moved):
        return pl.CostEstimate(flops=flops, bytes_accessed=moved, transcendentals=0)

    sent = []
    for chunk in range(CHUNKS):
        first = chunk == 0
        message = (fields, each * rows + (tile + TABLE if first else 0), LANES)
        sent.append(
            pl.pallas_call(
                functools.partial(pack_kernel, chunk),
                grid=(1,),
                out_shape=jax.ShapeDtypeStruct(message, bf16),
                in_specs=[whole_emb, part_of(chunk)] + ([vmem, vmem, smem] if first else []),
                out_specs=pl.BlockSpec(message, lambda i: (0, 0, 0)),
                scratch_shapes=[turned],
                compiler_params=params,
                cost_estimate=cost(10**9, 8 * 10**6),
            )(emb, cot, *([comp, pairs.T, counts] if first else []))
        )
    kept = [
        jax.ShapeDtypeStruct((embeds, embeds), f32),
        jax.ShapeDtypeStruct((embeds, LANES), bf16),
        jax.ShapeDtypeStruct((embeds, LANES), f32),
    ]
    state, back = None, []
    for chunk in range(CHUNKS):
        first, last = chunk == 0, chunk == CHUNKS - 1
        x = lax.all_to_all(sent[chunk], "field", 0, 0)
        message = (fields, each * rows + (tile if last else 0), LANES)
        keep = kept if first and not last else []
        out = pl.pallas_call(
            functools.partial(block_kernel, chunk, width ** (-0.5), tile, width),
            out_shape=[jax.ShapeDtypeStruct(message, bf16)] + keep,
            in_specs=[vmem] + ([] if first else [vmem] * 3),
            out_specs=[vmem] * (1 + len(keep)),
            scratch_shapes=([pltpu.VMEM(k.shape, k.dtype) for k in kept] if first and last else [])
            + [
                pltpu.VMEM((embeds, width), bf16),
                pltpu.VMEM((embeds, 2 * LANES), bf16),
                pltpu.VMEM((embeds, 2 * LANES), bf16),
            ],
            compiler_params=params,
            cost_estimate=cost(4 * 10**9, 6 * 10**6),
        )(x, *([] if first else state))
        if first:
            state = out[1:]
        back.append(lax.all_to_all(out[0], "field", 0, 0))

    grad = dp_sum(jnp.sum(back[-1][:, each * rows :].astype(f32), axis=0))
    weight_grad = grad / (samp_rows * lax.axis_size("dp"))

    result = ()
    for chunk in range(CHUNKS):
        y = back[chunk]
        first = chunk == 0
        result = pl.pallas_call(
            functools.partial(unpack_kernel, chunk),
            grid=(1,),
            out_shape=(
                jax.ShapeDtypeStruct((samp_rows, tile, LANES), bf16),
                jax.ShapeDtypeStruct((tile, width, samp_rows), bf16),
            ),
            in_specs=[pl.BlockSpec(y.shape, lambda i: (0, 0, 0))]
            + ([] if first else [pl.BlockSpec(memory_space=pl.ANY), whole_emb]),
            out_specs=(part_of(chunk), whole_emb),
            input_output_aliases={} if first else {1: 0},
            scratch_shapes=[turned],
            compiler_params=params,
            cost_estimate=cost(10**9, 8 * 10**6),
        )(y, *result)
    mixed, emb_grad = result
    return mixed, jnp.transpose(emb_grad, (2, 0, 1)), weight_grad


def solution(mesh):
    in_specs = (
        P("dp", "field", None),
        P("field", None),
        P("dp", "field", None),
        P("field", None),
        P("field"),
    )
    out_specs = (P("dp", "field", None), P("dp", "field", None), P("field", None))
    return jax.shard_map(
        per_device, mesh=mesh, in_specs=in_specs, out_specs=out_specs, check_vma=False
    )
```

```python
import functools

import jax
import jax.numpy as jnp
from jax import lax
from jax.experimental import pallas as pl
from jax.experimental.pallas import tpu as pltpu
from jax.sharding import PartitionSpec as P

LANES = 128
GROUPS = 4
AT_ONCE = 4
HALVES = (1, 8, 2, 6)
BUTTERFLY = (1, 3, 4)
TABLE = 16
TURN = (((1,), (1,)), ((), ()))
MIB = 1024 * 1024


def row_groups(tile):
    size = tile // 2 // GROUPS
    return [(g * size, tile // 2 + g * size, size) for g in range(GROUPS)]


def pack_kernel(
    emb_hbm, cot_hbm, comp_hbm, pairs_hbm, counts_ref, out_hbm, emb, comp, pairs, turned, message, sems
):
    tile, width, samples = emb.shape
    fields = out_hbm.shape[0]
    each = samples // fields
    half = tile // 2
    packed = tile + half
    f32, bf16 = jnp.float32, jnp.bfloat16
    groups = row_groups(tile)
    loads = [
        pltpu.make_async_copy(
            emb_hbm.at[pl.ds(start, size)], emb.at[pl.ds(start, size)], sems.at[2 * g + h]
        )
        for g, (low, high, size) in enumerate(groups)
        for h, start in enumerate((low, high))
    ]
    small = [
        pltpu.make_async_copy(comp_hbm, comp, sems.at[2 * GROUPS]),
        pltpu.make_async_copy(pairs_hbm, pairs, sems.at[2 * GROUPS + 1]),
    ]
    direct = pltpu.make_async_copy(
        cot_hbm, message.at[:, pl.ds(each * packed, each * tile)], sems.at[2 * GROUPS + 2]
    )
    for copy in loads[:2] + small + loads[2:] + [direct]:
        copy.start()
    for copy in small:
        copy.wait()
    slots = pairs.shape[1]
    number = lax.broadcasted_iota(jnp.int32, (LANES, slots), 0)
    live = lax.broadcasted_iota(jnp.int32, (LANES, slots), 1) < counts_ref[0]
    first = jnp.where((pairs[0:1] == number) & live, 1.0, 0.0).astype(bf16)
    second = jnp.where(pairs[1:2] == number, 1.0, 0.0).astype(bf16)
    table = lax.dot_general(first, second, TURN, preferred_element_type=f32)
    base = each * (packed + tile)
    for p in range(fields):
        message[p, base : base + tile] = comp[...]
        message[p, base + tile : base + tile + TABLE] = table[:TABLE].astype(bf16)
    for g, (low, high, size) in enumerate(groups):
        loads[2 * g].wait()
        loads[2 * g + 1].wait()
        for r in range(size):
            blocks = [
                (low + r, emb[low + r, :LANES]),
                (high + r, emb[high + r, :LANES]),
                (
                    tile + low + r,
                    jnp.concatenate([emb[low + r, LANES:], emb[high + r, LANES:]], axis=0),
                ),
            ]
            for place, block in blocks:
                turned[place * samples : (place + 1) * samples] = block.astype(f32).T
    direct.wait()
    stores = []
    for g in range(GROUPS):
        some = fields // GROUPS

        def peer(p, carry):
            for j in range(each):
                both = turned[pl.ds(p * each + j, packed, stride=samples), :]
                message[p, j * packed : (j + 1) * packed] = both.astype(bf16)
            return carry

        lax.fori_loop(g * some, (g + 1) * some, peer, 0)
        here = pl.ds(g * some, some)
        stores.append(
            pltpu.make_async_copy(message.at[here], out_hbm.at[here], sems.at[2 * GROUPS + 3 + g])
        )
        stores[-1].start()
    for copy in stores:
        copy.wait()


def pair_mask(x_ref, base, scale, mask, tile):
    fields = x_ref.shape[0]
    f32 = jnp.float32
    table = jnp.zeros((TABLE, LANES), f32)
    for f in range(fields):
        table += x_ref[f, base : base + TABLE].astype(f32)
    square = jnp.concatenate([table, jnp.zeros((LANES - TABLE, LANES), f32)], axis=0)
    on_diag = lax.broadcasted_iota(jnp.int32, square.shape, 0) == lax.broadcasted_iota(
        jnp.int32, square.shape, 1
    )
    mult = (square + square.T - jnp.where(on_diag, square, 0.0)) * scale
    for a in range(fields):
        row = jnp.concatenate(
            [jnp.broadcast_to(mult[a : a + 1, b : b + 1], (1, tile)) for b in range(fields)], axis=1
        )
        mask[a * tile : (a + 1) * tile] = jnp.broadcast_to(row, (tile, row.shape[1]))


def block_kernel(scale, tile, width, me_ref, x_ref, y_ref, keep_ref, send_ref, mask, grad, *sets):
    fields = x_ref.shape[0]
    half, rest = tile // 2, width - LANES
    packed = tile + half
    rows = packed + tile
    embeds = fields * tile
    f32, bf16 = jnp.float32, jnp.bfloat16
    each = (x_ref.shape[1] - tile - TABLE) // rows
    base = each * rows
    sets = [sets[i : i + 3] for i in range(0, len(sets), 3)]
    pair_mask(x_ref, base + tile, scale, mask, tile)
    weights = x_ref[:, base : base + tile].reshape(embeds, LANES)
    for _, sides, other in sets:
        sides[:, :LANES] = weights
        other[:, LANES:] = weights
    grad[...] = jnp.zeros_like(grad)

    def sample(j, emb, sides, other):
        start = pl.multiple_of(j * packed, 16)
        second = pl.multiple_of(each * packed + j * tile, 16)
        emb[:, :LANES] = x_ref[:, pl.ds(start, tile)].reshape(embeds, LANES)
        cot = x_ref[:, pl.ds(second, tile)].reshape(embeds, LANES)
        sides[:, LANES:] = cot
        other[:, :LANES] = cot
        tail = x_ref[:, pl.ds(start + tile, half)]
        upper = jnp.concatenate([tail[:, :, rest:], tail[:, :, :rest]], axis=2)
        both = jnp.concatenate([tail, upper], axis=1).reshape(embeds, LANES)
        emb[:, LANES:] = both[:, :rest]
        feats = emb[...]
        gram = lax.dot_general(feats, feats, TURN, preferred_element_type=f32)
        hmat = lax.dot_general(other[...], sides[...], TURN, preferred_element_type=f32)
        masked = (mask[...] * gram).astype(bf16)
        sym = (mask[...] * hmat).astype(bf16)
        both = jnp.dot(masked, sides[...], preferred_element_type=f32)
        dfeat = jnp.dot(sym, feats, preferred_element_type=f32).astype(bf16)
        y_ref[:, pl.ds(second, tile)] = both[:, :LANES].astype(bf16).reshape(fields, tile, LANES)
        y_ref[:, pl.ds(start, tile)] = dfeat[:, :LANES].reshape(fields, tile, LANES)
        last = dfeat[:, LANES:].reshape(fields, tile, rest)
        y_ref[:, pl.ds(start + tile, half)] = jnp.concatenate(
            [last[:, :half], last[:, half:]], axis=2
        )
        return both[:, LANES:]

    def some(i, carry):
        terms = [sample(i * len(sets) + u, *refs) for u, refs in enumerate(sets)]
        grad[...] += sum(terms[1:], terms[0])
        return carry

    lax.fori_loop(0, each // len(sets), some, 0)
    for n in range(fields):
        owner = me_ref[0]
        for bit, flip in enumerate(HALVES):
            if n & (fields >> (bit + 1)):
                owner = jnp.bitwise_xor(owner, flip)
        term = grad[pl.ds(pl.multiple_of(owner * tile, tile), tile)]
        if n < fields // 2:
            keep_ref[n] = term
        else:
            send_ref[n - fields // 2] = term


def unpack_kernel(y_ref, mixed_hbm, dfeat_hbm, dfeat, turned, sems):
    tile, width, samples = dfeat.shape
    fields = y_ref.shape[0]
    each = samples // fields
    half, rest = tile // 2, width - LANES
    packed = tile + half
    f32, bf16 = jnp.float32, jnp.bfloat16
    copies = [
        pltpu.make_async_copy(
            y_ref.at[:, pl.ds(each * packed, each * tile)], mixed_hbm, sems.at[2 * GROUPS]
        )
    ]
    copies[0].start()

    def peer(p, carry):
        for j in range(each):
            turned[pl.ds(p * each + j, packed, stride=samples), :] = y_ref[
                p, j * packed : (j + 1) * packed
            ].astype(f32)
        return carry

    lax.fori_loop(0, fields, peer, 0)
    for g, (low, high, size) in enumerate(row_groups(tile)):
        for r in range(size):
            for row in (low + r, high + r):
                dfeat[row, :LANES] = turned[row * samples : (row + 1) * samples].T.astype(bf16)
            place = tile + low + r
            block = turned[place * samples : (place + 1) * samples].T.astype(bf16)
            dfeat[low + r, LANES:] = block[:rest]
            dfeat[high + r, LANES:] = block[rest:]
        for h, start in enumerate((low, high)):
            copy = pltpu.make_async_copy(
                dfeat.at[pl.ds(start, size)], dfeat_hbm.at[pl.ds(start, size)], sems.at[2 * g + h]
            )
            copy.start()
            copies.append(copy)
    for copy in copies:
        copy.wait()


def halve_sum(keep, send):
    size = lax.axis_size("field")
    for flip in HALVES:
        total = keep + lax.ppermute(send, "field", [(i, i ^ flip) for i in range(size)])
        left = total.shape[0] // 2
        keep, send = total[:left], total[left:]
    return total[0]


def dp_sum(total):
    size = lax.axis_size("dp")
    for flip in [f for f in BUTTERFLY if f < size]:
        total = total + lax.ppermute(total, "dp", [(i, i ^ flip) for i in range(size)])
    return total


def per_device(emb, comp, cot, pairs, counts):
    samp_rows, tile, width = emb.shape
    fields = lax.axis_size("field")
    embeds = tile * fields
    packed = tile + tile // 2
    rows = packed + tile
    each = samp_rows // fields
    f32, bf16 = jnp.float32, jnp.bfloat16
    params = pltpu.CompilerParams(vmem_limit_bytes=24 * MIB)
    vmem = pl.BlockSpec(memory_space=pltpu.VMEM)
    smem = pl.BlockSpec(memory_space=pltpu.SMEM)
    hbm = pl.BlockSpec(memory_space=pltpu.HBM)
    turned = pltpu.VMEM((packed * samp_rows, LANES), f32)
    by_row = pltpu.VMEM((tile, width, samp_rows), bf16)

    def cost(flops, moved):
        return pl.CostEstimate(flops=flops, bytes_accessed=moved, transcendentals=0)

    x = pl.pallas_call(
        pack_kernel,
        out_shape=jax.ShapeDtypeStruct((fields, each * rows + tile + TABLE, LANES), bf16),
        in_specs=[hbm, hbm, hbm, hbm, smem],
        out_specs=hbm,
        scratch_shapes=[
            by_row,
            pltpu.VMEM(comp.shape, bf16),
            pltpu.VMEM(pairs.shape[::-1], jnp.int32),
            turned,
            pltpu.VMEM((fields, each * rows + tile + TABLE, LANES), bf16),
            pltpu.SemaphoreType.DMA((3 * GROUPS + 3,)),
        ],
        compiler_params=pltpu.CompilerParams(vmem_limit_bytes=56 * MIB),
        cost_estimate=cost(10**9, 8 * 10**6),
    )(
        jnp.transpose(emb, (1, 2, 0)),
        cot.reshape(fields, each * tile, LANES),
        comp,
        pairs.T,
        counts,
    )
    x = lax.all_to_all(x, "field", 0, 0)
    terms = jax.ShapeDtypeStruct((fields // 2, tile, LANES), f32)
    y, keep, send = pl.pallas_call(
        functools.partial(block_kernel, width ** (-0.5), tile, width),
        out_shape=(jax.ShapeDtypeStruct((fields, each * rows, LANES), bf16), terms, terms),
        in_specs=[smem, vmem],
        out_specs=(vmem, vmem, vmem),
        scratch_shapes=[pltpu.VMEM((embeds, embeds), f32), pltpu.VMEM((embeds, LANES), f32)]
        + [
            pltpu.VMEM((embeds, width), bf16),
            pltpu.VMEM((embeds, 2 * LANES), bf16),
            pltpu.VMEM((embeds, 2 * LANES), bf16),
        ]
        * AT_ONCE,
        compiler_params=params,
        cost_estimate=cost(4 * 10**9, 6 * 10**6),
    )(lax.axis_index("field").astype(jnp.int32).reshape(1), x)
    y = lax.all_to_all(y, "field", 0, 0)
    weight_grad = dp_sum(halve_sum(keep, send)) / (samp_rows * lax.axis_size("dp"))

    mixed, emb_grad = pl.pallas_call(
        unpack_kernel,
        out_shape=(
            jax.ShapeDtypeStruct((fields, each * tile, LANES), bf16),
            jax.ShapeDtypeStruct((tile, width, samp_rows), bf16),
        ),
        in_specs=[vmem],
        out_specs=(hbm, hbm),
        scratch_shapes=[by_row, turned, pltpu.SemaphoreType.DMA((2 * GROUPS + 1,))],
        compiler_params=params,
        cost_estimate=cost(10**9, 8 * 10**6),
    )(y)
    return mixed.reshape(cot.shape), jnp.transpose(emb_grad, (2, 0, 1)), weight_grad


def solution(mesh):
    in_specs = (
        P("dp", "field", None),
        P("field", None),
        P("dp", "field", None),
        P("field", None),
        P("field"),
    )
    out_specs = (P("dp", "field", None), P("dp", "field", None), P("field", None))
    return jax.shard_map(
        per_device, mesh=mesh, in_specs=in_specs, out_specs=out_specs, check_vma=False
    )
```

```python
import functools

import jax
import jax.numpy as jnp
from jax import lax
from jax.experimental import pallas as pl
from jax.experimental.pallas import tpu as pltpu
from jax.sharding import PartitionSpec as P

LANES = 128
GROUPS = 4
AT_ONCE = 4
BUTTERFLY = (1, 3, 4)
TABLE = 16
TURN = (((1,), (1,)), ((), ()))
MIB = 1024 * 1024


def row_groups(tile):
    size = tile // 2 // GROUPS
    return [(g * size, tile // 2 + g * size, size) for g in range(GROUPS)]


def pack_kernel(
    emb_hbm, cot_hbm, comp_hbm, pairs_hbm, counts_ref, out_hbm, emb, comp, pairs, turned, message, sems
):
    tile, width, samples = emb.shape
    fields = out_hbm.shape[0]
    each = samples // fields
    half = tile // 2
    packed = tile + half
    f32, bf16 = jnp.float32, jnp.bfloat16
    groups = row_groups(tile)
    loads = [
        pltpu.make_async_copy(
            emb_hbm.at[pl.ds(start, size)], emb.at[pl.ds(start, size)], sems.at[2 * g + h]
        )
        for g, (low, high, size) in enumerate(groups)
        for h, start in enumerate((low, high))
    ]
    small = [
        pltpu.make_async_copy(comp_hbm, comp, sems.at[2 * GROUPS]),
        pltpu.make_async_copy(pairs_hbm, pairs, sems.at[2 * GROUPS + 1]),
    ]
    direct = pltpu.make_async_copy(
        cot_hbm, message.at[:, pl.ds(each * packed, each * tile)], sems.at[2 * GROUPS + 2]
    )
    for copy in loads[:2] + small + loads[2:] + [direct]:
        copy.start()
    for copy in small:
        copy.wait()
    slots = pairs.shape[1]
    number = lax.broadcasted_iota(jnp.int32, (LANES, slots), 0)
    live = lax.broadcasted_iota(jnp.int32, (LANES, slots), 1) < counts_ref[0]
    first = jnp.where((pairs[0:1] == number) & live, 1.0, 0.0).astype(bf16)
    second = jnp.where(pairs[1:2] == number, 1.0, 0.0).astype(bf16)
    table = lax.dot_general(first, second, TURN, preferred_element_type=f32)
    base = each * (packed + tile)
    for p in range(fields):
        message[p, base : base + tile] = comp[...]
        message[p, base + tile : base + tile + TABLE] = table[:TABLE].astype(bf16)
    for g, (low, high, size) in enumerate(groups):
        loads[2 * g].wait()
        loads[2 * g + 1].wait()
        for r in range(size):
            blocks = [
                (low + r, emb[low + r, :LANES]),
                (high + r, emb[high + r, :LANES]),
                (
                    tile + low + r,
                    jnp.concatenate([emb[low + r, LANES:], emb[high + r, LANES:]], axis=0),
                ),
            ]
            for place, block in blocks:
                turned[place * samples : (place + 1) * samples] = block.astype(f32).T
    direct.wait()
    stores = []
    for g in range(GROUPS):
        some = fields // GROUPS

        def peer(p, carry):
            for j in range(each):
                both = turned[pl.ds(p * each + j, packed, stride=samples), :]
                message[p, j * packed : (j + 1) * packed] = both.astype(bf16)
            return carry

        lax.fori_loop(g * some, (g + 1) * some, peer, 0)
        here = pl.ds(g * some, some)
        stores.append(
            pltpu.make_async_copy(message.at[here], out_hbm.at[here], sems.at[2 * GROUPS + 3 + g])
        )
        stores[-1].start()
    for copy in stores:
        copy.wait()


def pair_mask(x_ref, base, scale, mask, tile):
    fields = x_ref.shape[0]
    f32 = jnp.float32
    table = jnp.zeros((TABLE, LANES), f32)
    for f in range(fields):
        table += x_ref[f, base : base + TABLE].astype(f32)
    square = jnp.concatenate([table, jnp.zeros((LANES - TABLE, LANES), f32)], axis=0)
    on_diag = lax.broadcasted_iota(jnp.int32, square.shape, 0) == lax.broadcasted_iota(
        jnp.int32, square.shape, 1
    )
    mult = (square + square.T - jnp.where(on_diag, square, 0.0)) * scale
    for a in range(fields):
        row = jnp.concatenate(
            [jnp.broadcast_to(mult[a : a + 1, b : b + 1], (1, tile)) for b in range(fields)], axis=1
        )
        mask[a * tile : (a + 1) * tile] = jnp.broadcast_to(row, (tile, row.shape[1]))


def block_kernel(scale, tile, width, x_ref, y_ref, mask, grad, *sets):
    fields = x_ref.shape[0]
    half, rest = tile // 2, width - LANES
    packed = tile + half
    rows = packed + tile
    embeds = fields * tile
    f32, bf16 = jnp.float32, jnp.bfloat16
    each = (x_ref.shape[1] - tile - TABLE) // rows
    base = each * rows
    sets = [sets[i : i + 3] for i in range(0, len(sets), 3)]
    pair_mask(x_ref, base + tile, scale, mask, tile)
    weights = x_ref[:, base : base + tile].reshape(embeds, LANES)
    for _, sides, other in sets:
        sides[:, :LANES] = weights
        other[:, LANES:] = weights
    grad[...] = jnp.zeros_like(grad)

    def sample(j, emb, sides, other):
        start = pl.multiple_of(j * packed, 16)
        second = pl.multiple_of(each * packed + j * tile, 16)
        emb[:, :LANES] = x_ref[:, pl.ds(start, tile)].reshape(embeds, LANES)
        cot = x_ref[:, pl.ds(second, tile)].reshape(embeds, LANES)
        sides[:, LANES:] = cot
        other[:, :LANES] = cot
        tail = x_ref[:, pl.ds(start + tile, half)]
        upper = jnp.concatenate([tail[:, :, rest:], tail[:, :, :rest]], axis=2)
        both = jnp.concatenate([tail, upper], axis=1).reshape(embeds, LANES)
        emb[:, LANES:] = both[:, :rest]
        feats = emb[...]
        gram = lax.dot_general(feats, feats, TURN, preferred_element_type=f32)
        hmat = lax.dot_general(other[...], sides[...], TURN, preferred_element_type=f32)
        masked = (mask[...] * gram).astype(bf16)
        sym = (mask[...] * hmat).astype(bf16)
        both = jnp.dot(masked, sides[...], preferred_element_type=f32)
        dfeat = jnp.dot(sym, feats, preferred_element_type=f32).astype(bf16)
        y_ref[:, pl.ds(second, tile)] = both[:, :LANES].astype(bf16).reshape(fields, tile, LANES)
        y_ref[:, pl.ds(start, tile)] = dfeat[:, :LANES].reshape(fields, tile, LANES)
        last = dfeat[:, LANES:].reshape(fields, tile, rest)
        y_ref[:, pl.ds(start + tile, half)] = jnp.concatenate(
            [last[:, :half], last[:, half:]], axis=2
        )
        return both[:, LANES:]

    def some(i, carry):
        terms = [sample(i * len(sets) + u, *refs) for u, refs in enumerate(sets)]
        grad[...] += sum(terms[1:], terms[0])
        return carry

    lax.fori_loop(0, each // len(sets), some, 0)
    y_ref[:, base:] = grad[...].astype(bf16).reshape(fields, tile, LANES)


def regroup_kernel(samples, y_ref, mixed_hbm, turned, sem):
    fields, rows = y_ref.shape[0], turned.shape[0] // samples
    each = samples // fields
    copy = pltpu.make_async_copy(
        y_ref.at[:, pl.ds(each * rows, mixed_hbm.shape[1])], mixed_hbm, sem
    )
    copy.start()

    def peer(p, carry):
        for j in range(each):
            turned[pl.ds(p * each + j, rows, stride=samples), :] = y_ref[
                p, j * rows : (j + 1) * rows
            ].astype(jnp.float32)
        return carry

    lax.fori_loop(0, fields, peer, 0)
    copy.wait()


def turn_kernel(part, turned, *refs):
    dfeat_hbm, dfeat, sems = refs[-3:]
    tile, width, samples = dfeat.shape
    rest = width - LANES
    groups = row_groups(tile)
    share = len(groups) // 2
    copies = []
    for g, (low, high, size) in enumerate(groups[part * share : (part + 1) * share]):
        for r in range(size):
            for row in (low + r, high + r):
                block = turned[row * samples : (row + 1) * samples].T
                dfeat[row, :LANES] = block.astype(jnp.bfloat16)
            place = tile + low + r
            block = turned[place * samples : (place + 1) * samples].T.astype(jnp.bfloat16)
            dfeat[low + r, LANES:] = block[:rest]
            dfeat[high + r, LANES:] = block[rest:]
        for h, start in enumerate((low, high)):
            copy = pltpu.make_async_copy(
                dfeat.at[pl.ds(start, size)], dfeat_hbm.at[pl.ds(start, size)], sems.at[2 * g + h]
            )
            copy.start()
            copies.append(copy)
    for copy in copies:
        copy.wait()


def dp_sum(total):
    size = lax.axis_size("dp")
    for flip in [f for f in BUTTERFLY if f < size]:
        total = total + lax.ppermute(total, "dp", [(i, i ^ flip) for i in range(size)])
    return total


def per_device(emb, comp, cot, pairs, counts):
    samp_rows, tile, width = emb.shape
    fields = lax.axis_size("field")
    embeds = tile * fields
    packed = tile + tile // 2
    rows = packed + tile
    each = samp_rows // fields
    f32, bf16 = jnp.float32, jnp.bfloat16
    params = pltpu.CompilerParams(vmem_limit_bytes=24 * MIB)
    vmem = pl.BlockSpec(memory_space=pltpu.VMEM)
    smem = pl.BlockSpec(memory_space=pltpu.SMEM)
    hbm = pl.BlockSpec(memory_space=pltpu.HBM)
    turned = pltpu.VMEM((packed * samp_rows, LANES), f32)
    by_row = pltpu.VMEM((tile, width, samp_rows), bf16)

    def cost(flops, moved):
        return pl.CostEstimate(flops=flops, bytes_accessed=moved, transcendentals=0)

    x = pl.pallas_call(
        pack_kernel,
        out_shape=jax.ShapeDtypeStruct((fields, each * rows + tile + TABLE, LANES), bf16),
        in_specs=[hbm, hbm, hbm, hbm, smem],
        out_specs=hbm,
        scratch_shapes=[
            by_row,
            pltpu.VMEM(comp.shape, bf16),
            pltpu.VMEM(pairs.shape[::-1], jnp.int32),
            turned,
            pltpu.VMEM((fields, each * rows + tile + TABLE, LANES), bf16),
            pltpu.SemaphoreType.DMA((3 * GROUPS + 3,)),
        ],
        compiler_params=pltpu.CompilerParams(vmem_limit_bytes=56 * MIB),
        cost_estimate=cost(10**9, 8 * 10**6),
    )(
        jnp.transpose(emb, (1, 2, 0)),
        cot.reshape(fields, each * tile, LANES),
        comp,
        pairs.T,
        counts,
    )
    x = lax.all_to_all(x, "field", 0, 0)
    y = pl.pallas_call(
        functools.partial(block_kernel, width ** (-0.5), tile, width),
        out_shape=jax.ShapeDtypeStruct((fields, each * rows + tile, LANES), bf16),
        in_specs=[vmem],
        out_specs=vmem,
        scratch_shapes=[pltpu.VMEM((embeds, embeds), f32), pltpu.VMEM((embeds, LANES), f32)]
        + [
            pltpu.VMEM((embeds, width), bf16),
            pltpu.VMEM((embeds, 2 * LANES), bf16),
            pltpu.VMEM((embeds, 2 * LANES), bf16),
        ]
        * AT_ONCE,
        compiler_params=params,
        cost_estimate=cost(4 * 10**9, 6 * 10**6),
    )(x)
    y = lax.all_to_all(y, "field", 0, 0)
    grad = dp_sum(jnp.sum(y[:, each * rows :].astype(f32), axis=0))
    weight_grad = grad / (samp_rows * lax.axis_size("dp"))

    mixed, sorted_rows = pl.pallas_call(
        functools.partial(regroup_kernel, samp_rows),
        out_shape=(
            jax.ShapeDtypeStruct((fields, each * tile, LANES), bf16),
            jax.ShapeDtypeStruct((packed * samp_rows, LANES), f32),
        ),
        in_specs=[vmem],
        out_specs=(hbm, vmem),
        scratch_shapes=[pltpu.SemaphoreType.DMA],
        compiler_params=params,
        cost_estimate=cost(10**9, 8 * 10**6),
    )(y)
    emb_grad = ()
    for part in range(2):
        emb_grad = pl.pallas_call(
            functools.partial(turn_kernel, part),
            out_shape=(jax.ShapeDtypeStruct((tile, width, samp_rows), bf16),),
            in_specs=[vmem] + [hbm] * part,
            out_specs=(hbm,),
            input_output_aliases={1: 0} if part else {},
            scratch_shapes=[by_row, pltpu.SemaphoreType.DMA((GROUPS,))],
            compiler_params=params,
            cost_estimate=cost(10**9, 8 * 10**6),
        )(sorted_rows, *emb_grad)
    (emb_grad,) = emb_grad
    return mixed.reshape(cot.shape), jnp.transpose(emb_grad, (2, 0, 1)), weight_grad


def solution(mesh):
    in_specs = (
        P("dp", "field", None),
        P("field", None),
        P("dp", "field", None),
        P("field", None),
        P("field"),
    )
    out_specs = (P("dp", "field", None), P("dp", "field", None), P("field", None))
    return jax.shard_map(
        per_device, mesh=mesh, in_specs=in_specs, out_specs=out_specs, check_vma=False
    )
```

```python
import functools

import jax
import jax.numpy as jnp
from jax import lax
from jax.experimental import pallas as pl
from jax.experimental.pallas import tpu as pltpu
from jax.sharding import PartitionSpec as P

LANES = 128
GROUPS = 4
AT_ONCE = 8
ALONG_X = 4
TABLE = 16
TURN = (((1,), (1,)), ((), ()))
MIB = 1024 * 1024


def row_groups(tile):
    size = tile // 2 // GROUPS
    return [(g * size, tile // 2 + g * size, size) for g in range(GROUPS)]


def pack_kernel(
    emb_hbm, cot_hbm, comp_hbm, pairs_hbm, counts_ref, out_hbm, emb, comp, pairs, turned, message, sems
):
    tile, width, samples = emb.shape
    fields = out_hbm.shape[0]
    each = samples // fields
    half = tile // 2
    packed = tile + half
    f32, bf16 = jnp.float32, jnp.bfloat16
    groups = row_groups(tile)
    loads = [
        pltpu.make_async_copy(
            emb_hbm.at[pl.ds(start, size)], emb.at[pl.ds(start, size)], sems.at[2 * g + h]
        )
        for g, (low, high, size) in enumerate(groups)
        for h, start in enumerate((low, high))
    ]
    small = [
        pltpu.make_async_copy(comp_hbm, comp, sems.at[2 * GROUPS]),
        pltpu.make_async_copy(pairs_hbm, pairs, sems.at[2 * GROUPS + 1]),
    ]
    direct = pltpu.make_async_copy(
        cot_hbm, message.at[:, pl.ds(each * packed, each * tile)], sems.at[2 * GROUPS + 2]
    )
    for copy in loads[:2] + small + loads[2:] + [direct]:
        copy.start()
    for copy in small:
        copy.wait()
    slots = pairs.shape[1]
    number = lax.broadcasted_iota(jnp.int32, (LANES, slots), 0)
    live = lax.broadcasted_iota(jnp.int32, (LANES, slots), 1) < counts_ref[0]
    first = jnp.where((pairs[0:1] == number) & live, 1.0, 0.0).astype(bf16)
    second = jnp.where(pairs[1:2] == number, 1.0, 0.0).astype(bf16)
    table = lax.dot_general(first, second, TURN, preferred_element_type=f32)
    base = each * (packed + tile)
    for p in range(fields):
        message[p, base : base + tile] = comp[...]
        message[p, base + tile : base + tile + TABLE] = table[:TABLE].astype(bf16)
    for g, (low, high, size) in enumerate(groups):
        loads[2 * g].wait()
        loads[2 * g + 1].wait()
        for r in range(size):
            blocks = [
                (low + r, emb[low + r, :LANES]),
                (high + r, emb[high + r, :LANES]),
                (
                    tile + low + r,
                    jnp.concatenate([emb[low + r, LANES:], emb[high + r, LANES:]], axis=0),
                ),
            ]
            for place, block in blocks:
                turned[place * samples : (place + 1) * samples] = block.astype(f32).T
    direct.wait()
    stores = []
    for g in range(GROUPS):
        some = fields // GROUPS

        def peer(p, carry):
            for j in range(each):
                both = turned[pl.ds(p * each + j, packed, stride=samples), :]
                message[p, j * packed : (j + 1) * packed] = both.astype(bf16)
            return carry

        lax.fori_loop(g * some, (g + 1) * some, peer, 0)
        here = pl.ds(g * some, some)
        stores.append(
            pltpu.make_async_copy(message.at[here], out_hbm.at[here], sems.at[2 * GROUPS + 3 + g])
        )
        stores[-1].start()
    for copy in stores:
        copy.wait()


def pair_mask(x_ref, base, scale, mask, tile):
    fields = x_ref.shape[0]
    f32 = jnp.float32
    table = jnp.zeros((TABLE, LANES), f32)
    for f in range(fields):
        table += x_ref[f, base : base + TABLE].astype(f32)
    square = jnp.concatenate([table, jnp.zeros((LANES - TABLE, LANES), f32)], axis=0)
    on_diag = lax.broadcasted_iota(jnp.int32, square.shape, 0) == lax.broadcasted_iota(
        jnp.int32, square.shape, 1
    )
    mult = (square + square.T - jnp.where(on_diag, square, 0.0)) * scale
    for a in range(fields):
        row = jnp.concatenate(
            [jnp.broadcast_to(mult[a : a + 1, b : b + 1], (1, tile)) for b in range(fields)], axis=1
        )
        mask[a * tile : (a + 1) * tile] = jnp.broadcast_to(row, (tile, row.shape[1]))


def block_kernel(scale, tile, width, x_ref, y_ref, mask, grad, *sets):
    fields = x_ref.shape[0]
    half, rest = tile // 2, width - LANES
    packed = tile + half
    rows = packed + tile
    embeds = fields * tile
    f32, bf16 = jnp.float32, jnp.bfloat16
    each = (x_ref.shape[1] - tile - TABLE) // rows
    base = each * rows
    sets = [sets[i : i + 3] for i in range(0, len(sets), 3)]
    pair_mask(x_ref, base + tile, scale, mask, tile)
    weights = x_ref[:, base : base + tile].reshape(embeds, LANES)
    for _, sides, other in sets:
        sides[:, :LANES] = weights
        other[:, LANES:] = weights
    grad[...] = jnp.zeros_like(grad)

    def sample(j, emb, sides, other):
        start = pl.multiple_of(j * packed, 16)
        second = pl.multiple_of(each * packed + j * tile, 16)
        emb[:, :LANES] = x_ref[:, pl.ds(start, tile)].reshape(embeds, LANES)
        cot = x_ref[:, pl.ds(second, tile)].reshape(embeds, LANES)
        sides[:, LANES:] = cot
        other[:, :LANES] = cot
        tail = x_ref[:, pl.ds(start + tile, half)]
        upper = jnp.concatenate([tail[:, :, rest:], tail[:, :, :rest]], axis=2)
        both = jnp.concatenate([tail, upper], axis=1).reshape(embeds, LANES)
        emb[:, LANES:] = both[:, :rest]
        feats = emb[...]
        gram = lax.dot_general(feats, feats, TURN, preferred_element_type=f32)
        hmat = lax.dot_general(other[...], sides[...], TURN, preferred_element_type=f32)
        masked = (mask[...] * gram).astype(bf16)
        sym = (mask[...] * hmat).astype(bf16)
        both = jnp.dot(masked, sides[...], preferred_element_type=f32)
        dfeat = jnp.dot(sym, feats, preferred_element_type=f32).astype(bf16)
        y_ref[:, pl.ds(second, tile)] = both[:, :LANES].astype(bf16).reshape(fields, tile, LANES)
        y_ref[:, pl.ds(start, tile)] = dfeat[:, :LANES].reshape(fields, tile, LANES)
        last = dfeat[:, LANES:].reshape(fields, tile, rest)
        y_ref[:, pl.ds(start + tile, half)] = jnp.concatenate(
            [last[:, :half], last[:, half:]], axis=2
        )
        return both[:, LANES:]

    def some(i, carry):
        terms = [sample(i * len(sets) + u, *refs) for u, refs in enumerate(sets)]
        grad[...] += sum(terms[1:], terms[0])
        return carry

    lax.fori_loop(0, each // len(sets), some, 0)
    y_ref[:, base:] = grad[...].astype(bf16).reshape(fields, tile, LANES)


def turn(part, sorted_rows, dfeat_hbm, dfeat, sems):
    tile, width, samples = dfeat.shape
    rest = width - LANES
    packed = tile + tile // 2
    groups = row_groups(tile)
    share = len(groups) // 2

    def block(row):
        rows = sorted_rows[pl.ds(row, samples, stride=packed), :]
        return rows.T.astype(jnp.bfloat16)

    copies = []
    for g, (low, high, size) in enumerate(groups[part * share : (part + 1) * share]):
        for r in range(size):
            for row in (low + r, high + r):
                dfeat[row, :LANES] = block(row)
            both = block(tile + low + r)
            dfeat[low + r, LANES:] = both[:rest]
            dfeat[high + r, LANES:] = both[rest:]
        for h, start in enumerate((low, high)):
            copy = pltpu.make_async_copy(
                dfeat.at[pl.ds(start, size)], dfeat_hbm.at[pl.ds(start, size)], sems.at[2 * g + h]
            )
            copy.start()
            copies.append(copy)
    return copies


def unpack_kernel(y_ref, mixed_hbm, dfeat_hbm, sorted_rows, dfeat, sems):
    fields, length = mixed_hbm.shape[:2]
    share = sorted_rows.shape[0] // fields
    mixed = pltpu.make_async_copy(
        y_ref.at[:, pl.ds(share, length)], mixed_hbm, sems.at[GROUPS]
    )
    mixed.start()
    for p in range(fields):
        sorted_rows[p * share : (p + 1) * share] = y_ref[p, :share].astype(jnp.float32)
    for copy in turn(0, sorted_rows, dfeat_hbm, dfeat, sems) + [mixed]:
        copy.wait()


def finish_kernel(sorted_rows, _, dfeat_hbm, dfeat, sems):
    for copy in turn(1, sorted_rows, dfeat_hbm, dfeat, sems):
        copy.wait()


def dp_sum(own):
    size = lax.axis_size("dp")

    def partner(value, flip):
        return lax.ppermute(value, "dp", [(i, i ^ flip) for i in range(size)])

    if size != 2 * ALONG_X:
        return lax.psum(own, "dp")
    total = (own + partner(own, 1)) + (partner(own, 2) + partner(own, 3))
    return total + partner(total, ALONG_X)


def per_device(emb, comp, cot, pairs, counts):
    samp_rows, tile, width = emb.shape
    fields = lax.axis_size("field")
    embeds = tile * fields
    packed = tile + tile // 2
    rows = packed + tile
    each = samp_rows // fields
    f32, bf16 = jnp.float32, jnp.bfloat16
    params = pltpu.CompilerParams(vmem_limit_bytes=24 * MIB)
    vmem = pl.BlockSpec(memory_space=pltpu.VMEM)
    smem = pl.BlockSpec(memory_space=pltpu.SMEM)
    hbm = pl.BlockSpec(memory_space=pltpu.HBM)
    turned = pltpu.VMEM((packed * samp_rows, LANES), f32)
    by_row = pltpu.VMEM((tile, width, samp_rows), bf16)

    def cost(flops, moved):
        return pl.CostEstimate(flops=flops, bytes_accessed=moved, transcendentals=0)

    x = pl.pallas_call(
        pack_kernel,
        out_shape=jax.ShapeDtypeStruct((fields, each * rows + tile + TABLE, LANES), bf16),
        in_specs=[hbm, hbm, hbm, hbm, smem],
        out_specs=hbm,
        scratch_shapes=[
            by_row,
            pltpu.VMEM(comp.shape, bf16),
            pltpu.VMEM(pairs.shape[::-1], jnp.int32),
            turned,
            pltpu.VMEM((fields, each * rows + tile + TABLE, LANES), bf16),
            pltpu.SemaphoreType.DMA((3 * GROUPS + 3,)),
        ],
        compiler_params=pltpu.CompilerParams(vmem_limit_bytes=56 * MIB),
        cost_estimate=cost(10**9, 8 * 10**6),
    )(
        jnp.transpose(emb, (1, 2, 0)),
        cot.reshape(fields, each * tile, LANES),
        comp,
        pairs.T,
        counts,
    )
    x = lax.all_to_all(x, "field", 0, 0)
    y = pl.pallas_call(
        functools.partial(block_kernel, width ** (-0.5), tile, width),
        out_shape=jax.ShapeDtypeStruct((fields, each * rows + tile, LANES), bf16),
        in_specs=[vmem],
        out_specs=vmem,
        scratch_shapes=[pltpu.VMEM((embeds, embeds), f32), pltpu.VMEM((embeds, LANES), f32)]
        + [
            pltpu.VMEM((embeds, width), bf16),
            pltpu.VMEM((embeds, 2 * LANES), bf16),
            pltpu.VMEM((embeds, 2 * LANES), bf16),
        ]
        * AT_ONCE,
        compiler_params=params,
        cost_estimate=cost(4 * 10**9, 6 * 10**6),
    )(x)
    y = lax.all_to_all(y, "field", 0, 0)
    grad = dp_sum(jnp.sum(y[:, each * rows :].astype(f32), axis=0))
    weight_grad = grad / (samp_rows * lax.axis_size("dp"))

    by_row_out = jax.ShapeDtypeStruct((tile, width, samp_rows), bf16)
    mixed, emb_grad, sorted_rows = pl.pallas_call(
        unpack_kernel,
        out_shape=(
            jax.ShapeDtypeStruct((fields, each * tile, LANES), bf16),
            by_row_out,
            jax.ShapeDtypeStruct((packed * samp_rows, LANES), f32),
        ),
        in_specs=[vmem],
        out_specs=(hbm, hbm, vmem),
        scratch_shapes=[by_row, pltpu.SemaphoreType.DMA((GROUPS + 1,))],
        compiler_params=params,
        cost_estimate=cost(10**9, 8 * 10**6),
    )(y)
    (emb_grad,) = pl.pallas_call(
        finish_kernel,
        out_shape=(by_row_out,),
        in_specs=[vmem, hbm],
        out_specs=(hbm,),
        input_output_aliases={1: 0},
        scratch_shapes=[by_row, pltpu.SemaphoreType.DMA((GROUPS,))],
        compiler_params=params,
        cost_estimate=cost(10**9, 8 * 10**6),
    )(sorted_rows, emb_grad)
    return mixed.reshape(cot.shape), jnp.transpose(emb_grad, (2, 0, 1)), weight_grad


def solution(mesh):
    in_specs = (
        P("dp", "field", None),
        P("field", None),
        P("dp", "field", None),
        P("field", None),
        P("field"),
    )
    out_specs = (P("dp", "field", None), P("dp", "field", None), P("field", None))
    return jax.shard_map(
        per_device, mesh=mesh, in_specs=in_specs, out_specs=out_specs, check_vma=False
    )
```

```python
import functools

import jax
import jax.numpy as jnp
from jax import lax
from jax.experimental import pallas as pl
from jax.experimental.pallas import tpu as pltpu
from jax.sharding import PartitionSpec as P

LANES = 128
GROUPS = 4
AT_ONCE = 8
ALONG_X = 4
TABLE = 16
TURN = (((1,), (1,)), ((), ()))
MIB = 1024 * 1024


def row_groups(tile):
    size = tile // 2 // GROUPS
    return [(g * size, tile // 2 + g * size, size) for g in range(GROUPS)]


def pack_kernel(
    emb_hbm, cot_hbm, comp_hbm, pairs_hbm, counts_ref, out_hbm, emb, comp, pairs, turned, message, sems
):
    tile, width, samples = emb.shape
    fields = out_hbm.shape[0]
    each = samples // fields
    half = tile // 2
    packed = tile + half
    f32, bf16 = jnp.float32, jnp.bfloat16
    groups = row_groups(tile)
    loads = [
        pltpu.make_async_copy(
            emb_hbm.at[pl.ds(start, size)], emb.at[pl.ds(start, size)], sems.at[2 * g + h]
        )
        for g, (low, high, size) in enumerate(groups)
        for h, start in enumerate((low, high))
    ]
    small = [
        pltpu.make_async_copy(comp_hbm, comp, sems.at[2 * GROUPS]),
        pltpu.make_async_copy(pairs_hbm, pairs, sems.at[2 * GROUPS + 1]),
    ]
    direct = pltpu.make_async_copy(
        cot_hbm, message.at[:, pl.ds(each * packed, each * tile)], sems.at[2 * GROUPS + 2]
    )
    for copy in loads[:2] + small + loads[2:] + [direct]:
        copy.start()
    for copy in small:
        copy.wait()
    slots = pairs.shape[1]
    number = lax.broadcasted_iota(jnp.int32, (LANES, slots), 0)
    live = lax.broadcasted_iota(jnp.int32, (LANES, slots), 1) < counts_ref[0]
    first = jnp.where((pairs[0:1] == number) & live, 1.0, 0.0).astype(bf16)
    second = jnp.where(pairs[1:2] == number, 1.0, 0.0).astype(bf16)
    table = lax.dot_general(first, second, TURN, preferred_element_type=f32)
    base = each * (packed + tile)
    for p in range(fields):
        message[p, base : base + tile] = comp[...]
        message[p, base + tile : base + tile + TABLE] = table[:TABLE].astype(bf16)
    for g, (low, high, size) in enumerate(groups):
        loads[2 * g].wait()
        loads[2 * g + 1].wait()
        for r in range(size):
            blocks = [
                (low + r, emb[low + r, :LANES]),
                (high + r, emb[high + r, :LANES]),
                (
                    tile + low + r,
                    jnp.concatenate([emb[low + r, LANES:], emb[high + r, LANES:]], axis=0),
                ),
            ]
            for place, block in blocks:
                turned[place * samples : (place + 1) * samples] = block.T.astype(f32)
    direct.wait()
    stores = []
    for g in range(GROUPS):
        some = fields // GROUPS

        def peer(p, carry):
            for j in range(each):
                both = turned[pl.ds(p * each + j, packed, stride=samples), :]
                message[p, j * packed : (j + 1) * packed] = both.astype(bf16)
            return carry

        lax.fori_loop(g * some, (g + 1) * some, peer, 0)
        here = pl.ds(g * some, some)
        stores.append(
            pltpu.make_async_copy(message.at[here], out_hbm.at[here], sems.at[2 * GROUPS + 3 + g])
        )
        stores[-1].start()
    for copy in stores:
        copy.wait()


def pair_mask(x_ref, base, scale, mask, tile):
    fields = x_ref.shape[0]
    f32 = jnp.float32
    table = jnp.zeros((TABLE, LANES), f32)
    for f in range(fields):
        table += x_ref[f, base : base + TABLE].astype(f32)
    square = jnp.concatenate([table, jnp.zeros((LANES - TABLE, LANES), f32)], axis=0)
    on_diag = lax.broadcasted_iota(jnp.int32, square.shape, 0) == lax.broadcasted_iota(
        jnp.int32, square.shape, 1
    )
    mult = (square + square.T - jnp.where(on_diag, square, 0.0)) * scale
    for a in range(fields):
        row = jnp.concatenate(
            [jnp.broadcast_to(mult[a : a + 1, b : b + 1], (1, tile)) for b in range(fields)], axis=1
        )
        mask[a * tile : (a + 1) * tile] = jnp.broadcast_to(row, (tile, row.shape[1]))


def block_kernel(scale, tile, width, x_ref, y_ref, mask, grad, *sets):
    fields = x_ref.shape[0]
    half, rest = tile // 2, width - LANES
    packed = tile + half
    rows = packed + tile
    embeds = fields * tile
    f32, bf16 = jnp.float32, jnp.bfloat16
    each = (x_ref.shape[1] - tile - TABLE) // rows
    base = each * rows
    sets = [sets[i : i + 3] for i in range(0, len(sets), 3)]
    pair_mask(x_ref, base + tile, scale, mask, tile)
    weights = x_ref[:, base : base + tile].reshape(embeds, LANES)
    for _, sides, other in sets:
        sides[:, :LANES] = weights
        other[:, LANES:] = weights
    grad[...] = jnp.zeros_like(grad)

    def sample(j, emb, sides, other):
        start = pl.multiple_of(j * packed, 16)
        second = pl.multiple_of(each * packed + j * tile, 16)
        emb[:, :LANES] = x_ref[:, pl.ds(start, tile)].reshape(embeds, LANES)
        cot = x_ref[:, pl.ds(second, tile)].reshape(embeds, LANES)
        sides[:, LANES:] = cot
        other[:, :LANES] = cot
        tail = x_ref[:, pl.ds(start + tile, half)]
        upper = jnp.concatenate([tail[:, :, rest:], tail[:, :, :rest]], axis=2)
        both = jnp.concatenate([tail, upper], axis=1).reshape(embeds, LANES)
        emb[:, LANES:] = both[:, :rest]
        feats = emb[...]
        gram = lax.dot_general(feats, feats, TURN, preferred_element_type=f32)
        hmat = lax.dot_general(other[...], sides[...], TURN, preferred_element_type=f32)
        masked = (mask[...] * gram).astype(bf16)
        sym = (mask[...] * hmat).astype(bf16)
        both = jnp.dot(masked, sides[...], preferred_element_type=f32)
        dfeat = jnp.dot(sym, feats, preferred_element_type=f32).astype(bf16)
        y_ref[:, pl.ds(second, tile)] = both[:, :LANES].astype(bf16).reshape(fields, tile, LANES)
        y_ref[:, pl.ds(start, tile)] = dfeat[:, :LANES].reshape(fields, tile, LANES)
        last = dfeat[:, LANES:].reshape(fields, tile, rest)
        y_ref[:, pl.ds(start + tile, half)] = jnp.concatenate(
            [last[:, :half], last[:, half:]], axis=2
        )
        return both[:, LANES:]

    def some(i, carry):
        terms = [sample(i * len(sets) + u, *refs) for u, refs in enumerate(sets)]
        grad[...] += sum(terms[1:], terms[0])
        return carry

    lax.fori_loop(0, each // len(sets), some, 0)
    y_ref[:, base:] = grad[...].astype(bf16).reshape(fields, tile, LANES)


def turn(part, sorted_rows, dfeat_hbm, dfeat, sems):
    tile, width, samples = dfeat.shape
    rest = width - LANES
    packed = tile + tile // 2
    groups = row_groups(tile)
    share = len(groups) // 2

    def block(row):
        rows = sorted_rows[pl.ds(row, samples, stride=packed), :]
        return rows.astype(jnp.bfloat16).T

    copies = []
    for g, (low, high, size) in enumerate(groups[part * share : (part + 1) * share]):
        for r in range(size):
            for row in (low + r, high + r):
                dfeat[row, :LANES] = block(row)
            both = block(tile + low + r)
            dfeat[low + r, LANES:] = both[:rest]
            dfeat[high + r, LANES:] = both[rest:]
        for h, start in enumerate((low, high)):
            copy = pltpu.make_async_copy(
                dfeat.at[pl.ds(start, size)], dfeat_hbm.at[pl.ds(start, size)], sems.at[2 * g + h]
            )
            copy.start()
            copies.append(copy)
    return copies


def unpack_kernel(y_ref, mixed_hbm, dfeat_hbm, sorted_rows, dfeat, sems):
    fields, length = mixed_hbm.shape[:2]
    share = sorted_rows.shape[0] // fields
    mixed = pltpu.make_async_copy(
        y_ref.at[:, pl.ds(share, length)], mixed_hbm, sems.at[GROUPS]
    )
    mixed.start()
    for p in range(fields):
        sorted_rows[p * share : (p + 1) * share] = y_ref[p, :share].astype(jnp.float32)
    for copy in turn(0, sorted_rows, dfeat_hbm, dfeat, sems) + [mixed]:
        copy.wait()


def finish_kernel(sorted_rows, _, dfeat_hbm, dfeat, sems):
    for copy in turn(1, sorted_rows, dfeat_hbm, dfeat, sems):
        copy.wait()


def dp_sum(own):
    size = lax.axis_size("dp")

    def partner(value, flip):
        return lax.ppermute(value, "dp", [(i, i ^ flip) for i in range(size)])

    if size != 2 * ALONG_X:
        return lax.psum(own, "dp")
    total = own + partner(own, ALONG_X)
    return (total + partner(total, 1)) + (partner(total, 2) + partner(total, 3))


def per_device(emb, comp, cot, pairs, counts):
    samp_rows, tile, width = emb.shape
    fields = lax.axis_size("field")
    embeds = tile * fields
    packed = tile + tile // 2
    rows = packed + tile
    each = samp_rows // fields
    f32, bf16 = jnp.float32, jnp.bfloat16
    params = pltpu.CompilerParams(vmem_limit_bytes=24 * MIB)
    vmem = pl.BlockSpec(memory_space=pltpu.VMEM)
    smem = pl.BlockSpec(memory_space=pltpu.SMEM)
    hbm = pl.BlockSpec(memory_space=pltpu.HBM)
    turned = pltpu.VMEM((packed * samp_rows, LANES), f32)
    by_row = pltpu.VMEM((tile, width, samp_rows), bf16)

    def cost(flops, moved):
        return pl.CostEstimate(flops=flops, bytes_accessed=moved, transcendentals=0)

    x = pl.pallas_call(
        pack_kernel,
        out_shape=jax.ShapeDtypeStruct((fields, each * rows + tile + TABLE, LANES), bf16),
        in_specs=[hbm, hbm, hbm, hbm, smem],
        out_specs=hbm,
        scratch_shapes=[
            by_row,
            pltpu.VMEM(comp.shape, bf16),
            pltpu.VMEM(pairs.shape[::-1], jnp.int32),
            turned,
            pltpu.VMEM((fields, each * rows + tile + TABLE, LANES), bf16),
            pltpu.SemaphoreType.DMA((3 * GROUPS + 3,)),
        ],
        compiler_params=pltpu.CompilerParams(vmem_limit_bytes=56 * MIB),
        cost_estimate=cost(10**9, 8 * 10**6),
    )(
        jnp.transpose(emb, (1, 2, 0)),
        cot.reshape(fields, each * tile, LANES),
        comp,
        pairs.T,
        counts,
    )
    x = lax.all_to_all(x, "field", 0, 0)
    y = pl.pallas_call(
        functools.partial(block_kernel, width ** (-0.5), tile, width),
        out_shape=jax.ShapeDtypeStruct((fields, each * rows + tile, LANES), bf16),
        in_specs=[vmem],
        out_specs=vmem,
        scratch_shapes=[pltpu.VMEM((embeds, embeds), f32), pltpu.VMEM((embeds, LANES), f32)]
        + [
            pltpu.VMEM((embeds, width), bf16),
            pltpu.VMEM((embeds, 2 * LANES), bf16),
            pltpu.VMEM((embeds, 2 * LANES), bf16),
        ]
        * AT_ONCE,
        compiler_params=params,
        cost_estimate=cost(4 * 10**9, 6 * 10**6),
    )(x)
    y = lax.all_to_all(y, "field", 0, 0)
    grad = dp_sum(jnp.sum(y[:, each * rows :].astype(f32), axis=0))
    weight_grad = grad / (samp_rows * lax.axis_size("dp"))

    by_row_out = jax.ShapeDtypeStruct((tile, width, samp_rows), bf16)
    mixed, emb_grad, sorted_rows = pl.pallas_call(
        unpack_kernel,
        out_shape=(
            jax.ShapeDtypeStruct((fields, each * tile, LANES), bf16),
            by_row_out,
            jax.ShapeDtypeStruct((packed * samp_rows, LANES), f32),
        ),
        in_specs=[vmem],
        out_specs=(hbm, hbm, vmem),
        scratch_shapes=[by_row, pltpu.SemaphoreType.DMA((GROUPS + 1,))],
        compiler_params=params,
        cost_estimate=cost(10**9, 8 * 10**6),
    )(y)
    (emb_grad,) = pl.pallas_call(
        finish_kernel,
        out_shape=(by_row_out,),
        in_specs=[vmem, hbm],
        out_specs=(hbm,),
        input_output_aliases={1: 0},
        scratch_shapes=[by_row, pltpu.SemaphoreType.DMA((GROUPS,))],
        compiler_params=params,
        cost_estimate=cost(10**9, 8 * 10**6),
    )(sorted_rows, emb_grad)
    return mixed.reshape(cot.shape), jnp.transpose(emb_grad, (2, 0, 1)), weight_grad


def solution(mesh):
    in_specs = (
        P("dp", "field", None),
        P("field", None),
        P("dp", "field", None),
        P("field", None),
        P("field"),
    )
    out_specs = (P("dp", "field", None), P("dp", "field", None), P("field", None))
    return jax.shard_map(
        per_device, mesh=mesh, in_specs=in_specs, out_specs=out_specs, check_vma=False
    )
```

```python
import functools

import jax
import jax.numpy as jnp
from jax import lax
from jax.experimental import pallas as pl
from jax.experimental.pallas import tpu as pltpu
from jax.sharding import PartitionSpec as P

LANES = 128
GROUPS = 8
AT_ONCE = 8
TABLE = 16
TURN = (((1,), (1,)), ((), ()))
MIB = 1024 * 1024


def row_groups(tile):
    size = tile // 2 // GROUPS
    return [(g * size, tile // 2 + g * size, size) for g in range(GROUPS)]


def pack_kernel(
    emb_hbm, cot_hbm, comp_hbm, pairs_hbm, counts_ref, out_hbm, emb, comp, pairs, turned, message, sems
):
    tile, width, samples = emb.shape
    fields = out_hbm.shape[0]
    each = samples // fields
    half = tile // 2
    packed = tile + half
    f32, bf16 = jnp.float32, jnp.bfloat16
    groups = row_groups(tile)
    loads = [
        pltpu.make_async_copy(
            emb_hbm.at[pl.ds(start, size)], emb.at[pl.ds(start, size)], sems.at[2 * g + h]
        )
        for g, (low, high, size) in enumerate(groups)
        for h, start in enumerate((low, high))
    ]
    small = [
        pltpu.make_async_copy(comp_hbm, comp, sems.at[2 * GROUPS]),
        pltpu.make_async_copy(pairs_hbm, pairs, sems.at[2 * GROUPS + 1]),
    ]
    direct = pltpu.make_async_copy(
        cot_hbm, message.at[:, pl.ds(each * packed, each * tile)], sems.at[2 * GROUPS + 2]
    )
    for copy in loads[:2] + small + loads[2:] + [direct]:
        copy.start()
    for copy in small:
        copy.wait()
    slots = pairs.shape[1]
    number = lax.broadcasted_iota(jnp.int32, (LANES, slots), 0)
    live = lax.broadcasted_iota(jnp.int32, (LANES, slots), 1) < counts_ref[0]
    first = jnp.where((pairs[0:1] == number) & live, 1.0, 0.0).astype(bf16)
    second = jnp.where(pairs[1:2] == number, 1.0, 0.0).astype(bf16)
    table = lax.dot_general(first, second, TURN, preferred_element_type=f32)
    base = each * (packed + tile)
    for p in range(fields):
        message[p, base : base + tile] = comp[...]
        message[p, base + tile : base + tile + TABLE] = table[:TABLE].astype(bf16)
    for g, (low, high, size) in enumerate(groups):
        loads[2 * g].wait()
        loads[2 * g + 1].wait()
        for r in range(size):
            blocks = [
                (low + r, emb[low + r, :LANES]),
                (high + r, emb[high + r, :LANES]),
                (
                    tile + low + r,
                    jnp.concatenate([emb[low + r, LANES:], emb[high + r, LANES:]], axis=0),
                ),
            ]
            for place, block in blocks:
                turned[place * samples : (place + 1) * samples] = block.T.astype(f32)
    direct.wait()
    stores = []
    for g in range(GROUPS):
        some = fields // GROUPS

        def peer(p, carry):
            for j in range(each):
                both = turned[pl.ds(p * each + j, packed, stride=samples), :]
                message[p, j * packed : (j + 1) * packed] = both.astype(bf16)
            return carry

        lax.fori_loop(g * some, (g + 1) * some, peer, 0)
        here = pl.ds(g * some, some)
        stores.append(
            pltpu.make_async_copy(message.at[here], out_hbm.at[here], sems.at[2 * GROUPS + 3 + g])
        )
        stores[-1].start()
    for copy in stores:
        copy.wait()


def pair_mask(x_ref, base, scale, mask, tile):
    fields = x_ref.shape[0]
    f32 = jnp.float32
    table = jnp.zeros((TABLE, LANES), f32)
    for f in range(fields):
        table += x_ref[f, base : base + TABLE].astype(f32)
    square = jnp.concatenate([table, jnp.zeros((LANES - TABLE, LANES), f32)], axis=0)
    on_diag = lax.broadcasted_iota(jnp.int32, square.shape, 0) == lax.broadcasted_iota(
        jnp.int32, square.shape, 1
    )
    mult = (square + square.T - jnp.where(on_diag, square, 0.0)) * scale
    for a in range(fields):
        row = jnp.concatenate(
            [jnp.broadcast_to(mult[a : a + 1, b : b + 1], (1, tile)) for b in range(fields)], axis=1
        )
        mask[a * tile : (a + 1) * tile] = jnp.broadcast_to(row, (tile, row.shape[1]))


def block_kernel(scale, tile, width, x_ref, y_ref, mask, grad, *sets):
    fields = x_ref.shape[0]
    half, rest = tile // 2, width - LANES
    packed = tile + half
    rows = packed + tile
    embeds = fields * tile
    f32, bf16 = jnp.float32, jnp.bfloat16
    each = (x_ref.shape[1] - tile - TABLE) // rows
    base = each * rows
    sets = [sets[i : i + 3] for i in range(0, len(sets), 3)]
    pair_mask(x_ref, base + tile, scale, mask, tile)
    weights = x_ref[:, base : base + tile].reshape(embeds, LANES)
    for _, sides, other in sets:
        sides[:, :LANES] = weights
        other[:, LANES:] = weights
    grad[...] = jnp.zeros_like(grad)

    def sample(j, emb, sides, other):
        start = pl.multiple_of(j * packed, 16)
        second = pl.multiple_of(each * packed + j * tile, 16)
        emb[:, :LANES] = x_ref[:, pl.ds(start, tile)].reshape(embeds, LANES)
        cot = x_ref[:, pl.ds(second, tile)].reshape(embeds, LANES)
        sides[:, LANES:] = cot
        other[:, :LANES] = cot
        tail = x_ref[:, pl.ds(start + tile, half)]
        upper = jnp.concatenate([tail[:, :, rest:], tail[:, :, :rest]], axis=2)
        both = jnp.concatenate([tail, upper], axis=1).reshape(embeds, LANES)
        emb[:, LANES:] = both[:, :rest]
        feats = emb[...]
        gram = lax.dot_general(feats, feats, TURN, preferred_element_type=f32)
        hmat = lax.dot_general(other[...], sides[...], TURN, preferred_element_type=f32)
        masked = (mask[...] * gram).astype(bf16)
        sym = (mask[...] * hmat).astype(bf16)
        both = jnp.dot(masked, sides[...], preferred_element_type=f32)
        dfeat = jnp.dot(sym, feats, preferred_element_type=f32).astype(bf16)
        y_ref[:, pl.ds(second, tile)] = both[:, :LANES].astype(bf16).reshape(fields, tile, LANES)
        y_ref[:, pl.ds(start, tile)] = dfeat[:, :LANES].reshape(fields, tile, LANES)
        last = dfeat[:, LANES:].reshape(fields, tile, rest)
        y_ref[:, pl.ds(start + tile, half)] = jnp.concatenate(
            [last[:, :half], last[:, half:]], axis=2
        )
        return both[:, LANES:]

    def some(i, carry):
        terms = [sample(i * len(sets) + u, *refs) for u, refs in enumerate(sets)]
        grad[...] += sum(terms[1:], terms[0])
        return carry

    lax.fori_loop(0, each // len(sets), some, 0)
    y_ref[:, base:] = grad[...].astype(bf16).reshape(fields, tile, LANES)


def turn(part, sorted_rows, dfeat_hbm, dfeat, sems):
    tile, width, samples = dfeat.shape
    rest = width - LANES
    packed = tile + tile // 2
    groups = row_groups(tile)
    share = len(groups) // 2

    def block(row):
        rows = sorted_rows[pl.ds(row, samples, stride=packed), :]
        return rows.astype(jnp.bfloat16).T

    copies = []
    for g, (low, high, size) in enumerate(groups[part * share : (part + 1) * share]):
        for r in range(size):
            for row in (low + r, high + r):
                dfeat[row, :LANES] = block(row)
            both = block(tile + low + r)
            dfeat[low + r, LANES:] = both[:rest]
            dfeat[high + r, LANES:] = both[rest:]
        for h, start in enumerate((low, high)):
            copy = pltpu.make_async_copy(
                dfeat.at[pl.ds(start, size)], dfeat_hbm.at[pl.ds(start, size)], sems.at[2 * g + h]
            )
            copy.start()
            copies.append(copy)
    return copies


def unpack_kernel(y_ref, mixed_hbm, dfeat_hbm, sorted_rows, dfeat, sems):
    fields, length = mixed_hbm.shape[:2]
    share = sorted_rows.shape[0] // fields
    mixed = pltpu.make_async_copy(
        y_ref.at[:, pl.ds(share, length)], mixed_hbm, sems.at[GROUPS]
    )
    mixed.start()
    for p in range(fields):
        sorted_rows[p * share : (p + 1) * share] = y_ref[p, :share].astype(jnp.float32)
    for copy in turn(0, sorted_rows, dfeat_hbm, dfeat, sems) + [mixed]:
        copy.wait()


def finish_kernel(sorted_rows, _, dfeat_hbm, dfeat, sems):
    for copy in turn(1, sorted_rows, dfeat_hbm, dfeat, sems):
        copy.wait()


def dp_sum(own):
    size = lax.axis_size("dp")
    copies = lax.optimization_barrier(jnp.broadcast_to(own, (size,) + own.shape))
    return jnp.sum(lax.all_to_all(copies, "dp", 0, 0), axis=0)


def per_device(emb, comp, cot, pairs, counts):
    samp_rows, tile, width = emb.shape
    fields = lax.axis_size("field")
    embeds = tile * fields
    packed = tile + tile // 2
    rows = packed + tile
    each = samp_rows // fields
    f32, bf16 = jnp.float32, jnp.bfloat16
    params = pltpu.CompilerParams(vmem_limit_bytes=24 * MIB)
    vmem = pl.BlockSpec(memory_space=pltpu.VMEM)
    smem = pl.BlockSpec(memory_space=pltpu.SMEM)
    hbm = pl.BlockSpec(memory_space=pltpu.HBM)
    turned = pltpu.VMEM((packed * samp_rows, LANES), f32)
    by_row = pltpu.VMEM((tile, width, samp_rows), bf16)

    def cost(flops, moved):
        return pl.CostEstimate(flops=flops, bytes_accessed=moved, transcendentals=0)

    x = pl.pallas_call(
        pack_kernel,
        out_shape=jax.ShapeDtypeStruct((fields, each * rows + tile + TABLE, LANES), bf16),
        in_specs=[hbm, hbm, hbm, hbm, smem],
        out_specs=hbm,
        scratch_shapes=[
            by_row,
            pltpu.VMEM(comp.shape, bf16),
            pltpu.VMEM(pairs.shape[::-1], jnp.int32),
            turned,
            pltpu.VMEM((fields, each * rows + tile + TABLE, LANES), bf16),
            pltpu.SemaphoreType.DMA((3 * GROUPS + 3,)),
        ],
        compiler_params=pltpu.CompilerParams(vmem_limit_bytes=56 * MIB),
        cost_estimate=cost(10**9, 8 * 10**6),
    )(
        jnp.transpose(emb, (1, 2, 0)),
        cot.reshape(fields, each * tile, LANES),
        comp,
        pairs.T,
        counts,
    )
    x = lax.all_to_all(x, "field", 0, 0)
    y = pl.pallas_call(
        functools.partial(block_kernel, width ** (-0.5), tile, width),
        out_shape=jax.ShapeDtypeStruct((fields, each * rows + tile, LANES), bf16),
        in_specs=[vmem],
        out_specs=vmem,
        scratch_shapes=[pltpu.VMEM((embeds, embeds), f32), pltpu.VMEM((embeds, LANES), f32)]
        + [
            pltpu.VMEM((embeds, width), bf16),
            pltpu.VMEM((embeds, 2 * LANES), bf16),
            pltpu.VMEM((embeds, 2 * LANES), bf16),
        ]
        * AT_ONCE,
        compiler_params=params,
        cost_estimate=cost(4 * 10**9, 6 * 10**6),
    )(x)
    y = lax.all_to_all(y, "field", 0, 0)
    grad = dp_sum(jnp.sum(y[:, each * rows :].astype(f32), axis=0))
    weight_grad = grad / (samp_rows * lax.axis_size("dp"))
    y, weight_grad = lax.optimization_barrier((y, weight_grad))

    by_row_out = jax.ShapeDtypeStruct((tile, width, samp_rows), bf16)
    mixed, emb_grad, sorted_rows = pl.pallas_call(
        unpack_kernel,
        out_shape=(
            jax.ShapeDtypeStruct((fields, each * tile, LANES), bf16),
            by_row_out,
            jax.ShapeDtypeStruct((packed * samp_rows, LANES), f32),
        ),
        in_specs=[vmem],
        out_specs=(hbm, hbm, vmem),
        scratch_shapes=[by_row, pltpu.SemaphoreType.DMA((GROUPS + 1,))],
        compiler_params=params,
        cost_estimate=cost(10**9, 8 * 10**6),
    )(y)
    (emb_grad,) = pl.pallas_call(
        finish_kernel,
        out_shape=(by_row_out,),
        in_specs=[vmem, hbm],
        out_specs=(hbm,),
        input_output_aliases={1: 0},
        scratch_shapes=[by_row, pltpu.SemaphoreType.DMA((GROUPS,))],
        compiler_params=params,
        cost_estimate=cost(10**9, 8 * 10**6),
    )(sorted_rows, emb_grad)
    return mixed.reshape(cot.shape), jnp.transpose(emb_grad, (2, 0, 1)), weight_grad


def solution(mesh):
    in_specs = (
        P("dp", "field", None),
        P("field", None),
        P("dp", "field", None),
        P("field", None),
        P("field"),
    )
    out_specs = (P("dp", "field", None), P("dp", "field", None), P("field", None))
    return jax.shard_map(
        per_device, mesh=mesh, in_specs=in_specs, out_specs=out_specs, check_vma=False
    )
```

```python
import functools

import jax
import jax.numpy as jnp
from jax import lax
from jax.experimental import pallas as pl
from jax.experimental.pallas import tpu as pltpu
from jax.sharding import PartitionSpec as P

LANES = 128
GROUPS = 4
AT_ONCE = 8
ALONG_X = 4
TABLE = 16
TURN = (((1,), (1,)), ((), ()))
MIB = 1024 * 1024


def row_groups(tile):
    size = tile // 2 // GROUPS
    return [(g * size, tile // 2 + g * size, size) for g in range(GROUPS)]


def pack_kernel(
    emb_hbm, cot_hbm, comp_hbm, pairs_hbm, counts_ref, out_hbm, emb, comp, pairs, turned, message, sems
):
    tile, width, samples = emb.shape
    fields = out_hbm.shape[0]
    each = samples // fields
    half = tile // 2
    packed = tile + half
    f32, bf16 = jnp.float32, jnp.bfloat16
    groups = row_groups(tile)
    loads = [
        pltpu.make_async_copy(
            emb_hbm.at[pl.ds(start, size)], emb.at[pl.ds(start, size)], sems.at[2 * g + h]
        )
        for g, (low, high, size) in enumerate(groups)
        for h, start in enumerate((low, high))
    ]
    small = [
        pltpu.make_async_copy(comp_hbm, comp, sems.at[2 * GROUPS]),
        pltpu.make_async_copy(pairs_hbm, pairs, sems.at[2 * GROUPS + 1]),
    ]
    direct = pltpu.make_async_copy(
        cot_hbm, message.at[:, pl.ds(each * packed, each * tile)], sems.at[2 * GROUPS + 2]
    )
    for copy in small + loads[:2] + [direct] + loads[2:]:
        copy.start()
    for copy in small:
        copy.wait()
    slots = pairs.shape[1]
    number = lax.broadcasted_iota(jnp.int32, (LANES, slots), 0)
    live = lax.broadcasted_iota(jnp.int32, (LANES, slots), 1) < counts_ref[0]
    first = jnp.where((pairs[0:1] == number) & live, 1.0, 0.0).astype(bf16)
    second = jnp.where(pairs[1:2] == number, 1.0, 0.0).astype(bf16)
    table = lax.dot_general(first, second, TURN, preferred_element_type=f32)
    base = each * (packed + tile)
    for p in range(fields):
        message[p, base : base + tile] = comp[...]
        message[p, base + tile : base + tile + TABLE] = table[:TABLE].astype(bf16)
    stores = []
    for g, (low, high, size) in enumerate(groups):
        if g == 1:
            direct.wait()
            later = pl.ds(each * packed, each * tile + tile + TABLE)
            stores.append(
                pltpu.make_async_copy(
                    message.at[:, later], out_hbm.at[:, later], sems.at[3 * GROUPS + 3]
                )
            )
            stores[-1].start()
        loads[2 * g].wait()
        loads[2 * g + 1].wait()
        for r in range(size):
            blocks = [
                (low + r, emb[low + r, :LANES]),
                (high + r, emb[high + r, :LANES]),
                (
                    tile + low + r,
                    jnp.concatenate([emb[low + r, LANES:], emb[high + r, LANES:]], axis=0),
                ),
            ]
            for place, block in blocks:
                turned[place * samples : (place + 1) * samples] = block.T.astype(f32)
    for g in range(GROUPS):
        some = fields // GROUPS

        def peer(p, carry):
            for j in range(each):
                both = turned[pl.ds(p * each + j, packed, stride=samples), :]
                message[p, j * packed : (j + 1) * packed] = both.astype(bf16)
            return carry

        lax.fori_loop(g * some, (g + 1) * some, peer, 0)
        here = (pl.ds(g * some, some), pl.ds(0, each * packed))
        stores.append(
            pltpu.make_async_copy(message.at[here], out_hbm.at[here], sems.at[2 * GROUPS + 3 + g])
        )
        stores[-1].start()
    for copy in stores:
        copy.wait()


def pair_mask(x_ref, base, scale, mask, tile):
    fields = x_ref.shape[0]
    f32 = jnp.float32
    table = jnp.zeros((TABLE, LANES), f32)
    for f in range(fields):
        table += x_ref[f, base : base + TABLE].astype(f32)
    square = jnp.concatenate([table, jnp.zeros((LANES - TABLE, LANES), f32)], axis=0)
    on_diag = lax.broadcasted_iota(jnp.int32, square.shape, 0) == lax.broadcasted_iota(
        jnp.int32, square.shape, 1
    )
    mult = (square + square.T - jnp.where(on_diag, square, 0.0)) * scale
    for a in range(fields):
        row = jnp.concatenate(
            [jnp.broadcast_to(mult[a : a + 1, b : b + 1], (1, tile)) for b in range(fields)], axis=1
        )
        mask[a * tile : (a + 1) * tile] = jnp.broadcast_to(row, (tile, row.shape[1]))


def block_kernel(scale, tile, width, x_ref, y_ref, mask, grad, *sets):
    fields = x_ref.shape[0]
    half, rest = tile // 2, width - LANES
    packed = tile + half
    rows = packed + tile
    embeds = fields * tile
    f32, bf16 = jnp.float32, jnp.bfloat16
    each = (x_ref.shape[1] - tile - TABLE) // rows
    base = each * rows
    sets = [sets[i : i + 3] for i in range(0, len(sets), 3)]
    pair_mask(x_ref, base + tile, scale, mask, tile)
    weights = x_ref[:, base : base + tile].reshape(embeds, LANES)
    for _, sides, other in sets:
        sides[:, :LANES] = weights
        other[:, LANES:] = weights
    grad[...] = jnp.zeros_like(grad)

    def sample(j, emb, sides, other):
        start = pl.multiple_of(j * packed, 16)
        second = pl.multiple_of(each * packed + j * tile, 16)
        emb[:, :LANES] = x_ref[:, pl.ds(start, tile)].reshape(embeds, LANES)
        cot = x_ref[:, pl.ds(second, tile)].reshape(embeds, LANES)
        sides[:, LANES:] = cot
        other[:, :LANES] = cot
        tail = x_ref[:, pl.ds(start + tile, half)]
        upper = jnp.concatenate([tail[:, :, rest:], tail[:, :, :rest]], axis=2)
        both = jnp.concatenate([tail, upper], axis=1).reshape(embeds, LANES)
        emb[:, LANES:] = both[:, :rest]
        feats = emb[...]
        gram = lax.dot_general(feats, feats, TURN, preferred_element_type=f32)
        hmat = lax.dot_general(other[...], sides[...], TURN, preferred_element_type=f32)
        masked = (mask[...] * gram).astype(bf16)
        sym = (mask[...] * hmat).astype(bf16)
        both = jnp.dot(masked, sides[...], preferred_element_type=f32)
        dfeat = jnp.dot(sym, feats, preferred_element_type=f32).astype(bf16)
        y_ref[:, pl.ds(second, tile)] = both[:, :LANES].astype(bf16).reshape(fields, tile, LANES)
        y_ref[:, pl.ds(start, tile)] = dfeat[:, :LANES].reshape(fields, tile, LANES)
        last = dfeat[:, LANES:].reshape(fields, tile, rest)
        y_ref[:, pl.ds(start + tile, half)] = jnp.concatenate(
            [last[:, :half], last[:, half:]], axis=2
        )
        return both[:, LANES:]

    def some(i, carry):
        terms = [sample(i * len(sets) + u, *refs) for u, refs in enumerate(sets)]
        grad[...] += sum(terms[1:], terms[0])
        return carry

    lax.fori_loop(0, each // len(sets), some, 0)
    y_ref[:, base:] = grad[...].astype(bf16).reshape(fields, tile, LANES)


def turn(part, sorted_rows, dfeat_hbm, dfeat, sems):
    tile, width, samples = dfeat.shape
    rest = width - LANES
    packed = tile + tile // 2
    groups = row_groups(tile)
    share = len(groups) // 2

    def block(row):
        rows = sorted_rows[pl.ds(row, samples, stride=packed), :]
        return rows.astype(jnp.bfloat16).T

    copies = []
    for g, (low, high, size) in enumerate(groups[part * share : (part + 1) * share]):
        for r in range(size):
            for row in (low + r, high + r):
                dfeat[row, :LANES] = block(row)
            both = block(tile + low + r)
            dfeat[low + r, LANES:] = both[:rest]
            dfeat[high + r, LANES:] = both[rest:]
        for h, start in enumerate((low, high)):
            copy = pltpu.make_async_copy(
                dfeat.at[pl.ds(start, size)], dfeat_hbm.at[pl.ds(start, size)], sems.at[2 * g + h]
            )
            copy.start()
            copies.append(copy)
    return copies


def unpack_kernel(y_ref, mixed_hbm, dfeat_hbm, sorted_rows, dfeat, sems):
    fields, length = mixed_hbm.shape[:2]
    share = sorted_rows.shape[0] // fields
    mixed = pltpu.make_async_copy(
        y_ref.at[:, pl.ds(share, length)], mixed_hbm, sems.at[GROUPS]
    )
    mixed.start()
    for p in range(fields):
        sorted_rows[p * share : (p + 1) * share] = y_ref[p, :share].astype(jnp.float32)
    for copy in turn(0, sorted_rows, dfeat_hbm, dfeat, sems) + [mixed]:
        copy.wait()


def finish_kernel(sorted_rows, _, dfeat_hbm, dfeat, sems):
    for copy in turn(1, sorted_rows, dfeat_hbm, dfeat, sems):
        copy.wait()


def dp_sum(own):
    size = lax.axis_size("dp")

    def partner(value, flip):
        return lax.ppermute(value, "dp", [(i, i ^ flip) for i in range(size)])

    if size != 2 * ALONG_X:
        return lax.psum(own, "dp")
    total = own + partner(own, ALONG_X)
    first, third = partner(total, 1), partner(total, 3)
    second = partner(total, 2)
    return (first + third) + (total + second)


def per_device(emb, comp, cot, pairs, counts):
    samp_rows, tile, width = emb.shape
    fields = lax.axis_size("field")
    embeds = tile * fields
    packed = tile + tile // 2
    rows = packed + tile
    each = samp_rows // fields
    f32, bf16 = jnp.float32, jnp.bfloat16
    params = pltpu.CompilerParams(vmem_limit_bytes=24 * MIB)
    vmem = pl.BlockSpec(memory_space=pltpu.VMEM)
    smem = pl.BlockSpec(memory_space=pltpu.SMEM)
    hbm = pl.BlockSpec(memory_space=pltpu.HBM)
    turned = pltpu.VMEM((packed * samp_rows, LANES), f32)
    by_row = pltpu.VMEM((tile, width, samp_rows), bf16)

    def cost(flops, moved):
        return pl.CostEstimate(flops=flops, bytes_accessed=moved, transcendentals=0)

    x = pl.pallas_call(
        pack_kernel,
        out_shape=jax.ShapeDtypeStruct((fields, each * rows + tile + TABLE, LANES), bf16),
        in_specs=[hbm, hbm, hbm, hbm, smem],
        out_specs=hbm,
        scratch_shapes=[
            by_row,
            pltpu.VMEM(comp.shape, bf16),
            pltpu.VMEM(pairs.shape[::-1], jnp.int32),
            turned,
            pltpu.VMEM((fields, each * rows + tile + TABLE, LANES), bf16),
            pltpu.SemaphoreType.DMA((3 * GROUPS + 4,)),
        ],
        compiler_params=pltpu.CompilerParams(vmem_limit_bytes=56 * MIB),
        cost_estimate=cost(10**9, 8 * 10**6),
    )(
        jnp.transpose(emb, (1, 2, 0)),
        cot.reshape(fields, each * tile, LANES),
        comp,
        pairs.T,
        counts,
    )
    x = lax.all_to_all(x, "field", 0, 0)
    y = pl.pallas_call(
        functools.partial(block_kernel, width ** (-0.5), tile, width),
        out_shape=jax.ShapeDtypeStruct((fields, each * rows + tile, LANES), bf16),
        in_specs=[vmem],
        out_specs=vmem,
        scratch_shapes=[pltpu.VMEM((embeds, embeds), f32), pltpu.VMEM((embeds, LANES), f32)]
        + [
            pltpu.VMEM((embeds, width), bf16),
            pltpu.VMEM((embeds, 2 * LANES), bf16),
            pltpu.VMEM((embeds, 2 * LANES), bf16),
        ]
        * AT_ONCE,
        compiler_params=params,
        cost_estimate=cost(4 * 10**9, 6 * 10**6),
    )(x)
    y = lax.all_to_all(y, "field", 0, 0)
    grad = dp_sum(jnp.sum(y[:, each * rows :].astype(f32), axis=0))
    weight_grad = grad / (samp_rows * lax.axis_size("dp"))

    by_row_out = jax.ShapeDtypeStruct((tile, width, samp_rows), bf16)
    mixed, emb_grad, sorted_rows = pl.pallas_call(
        unpack_kernel,
        out_shape=(
            jax.ShapeDtypeStruct((fields, each * tile, LANES), bf16),
            by_row_out,
            jax.ShapeDtypeStruct((packed * samp_rows, LANES), f32),
        ),
        in_specs=[vmem],
        out_specs=(hbm, hbm, vmem),
        scratch_shapes=[by_row, pltpu.SemaphoreType.DMA((GROUPS + 1,))],
        compiler_params=params,
        cost_estimate=cost(10**9, 8 * 10**6),
    )(y)
    (emb_grad,) = pl.pallas_call(
        finish_kernel,
        out_shape=(by_row_out,),
        in_specs=[vmem, hbm],
        out_specs=(hbm,),
        input_output_aliases={1: 0},
        scratch_shapes=[by_row, pltpu.SemaphoreType.DMA((GROUPS,))],
        compiler_params=params,
        cost_estimate=cost(10**9, 8 * 10**6),
    )(sorted_rows, emb_grad)
    return mixed.reshape(cot.shape), jnp.transpose(emb_grad, (2, 0, 1)), weight_grad


def solution(mesh):
    in_specs = (
        P("dp", "field", None),
        P("field", None),
        P("dp", "field", None),
        P("field", None),
        P("field"),
    )
    out_specs = (P("dp", "field", None), P("dp", "field", None), P("field", None))
    return jax.shard_map(
        per_device, mesh=mesh, in_specs=in_specs, out_specs=out_specs, check_vma=False
    )
```

```python
import functools

import jax
import jax.numpy as jnp
from jax import lax
from jax.experimental import pallas as pl
from jax.experimental.pallas import tpu as pltpu
from jax.sharding import PartitionSpec as P

LANES = 128
GROUPS = 4
AT_ONCE = 8
ALONG_X = 4
TABLE = 16
TURN = (((1,), (1,)), ((), ()))
MIB = 1024 * 1024


def row_groups(tile):
    size = tile // 2 // GROUPS
    return [(g * size, tile // 2 + g * size, size) for g in range(GROUPS)]


def pack_kernel(emb_hbm, cot_hbm, comp_hbm, pairs_hbm, counts_ref, out_ref, emb, comp, pairs, turned, sems):
    tile, width, samples = emb.shape
    fields = out_ref.shape[0]
    each = samples // fields
    packed = tile + tile // 2
    f32, bf16 = jnp.float32, jnp.bfloat16
    groups = row_groups(tile)
    loads = [
        pltpu.make_async_copy(
            emb_hbm.at[pl.ds(start, size)], emb.at[pl.ds(start, size)], sems.at[2 * g + h]
        )
        for g, (low, high, size) in enumerate(groups)
        for h, start in enumerate((low, high))
    ]
    others = [
        pltpu.make_async_copy(comp_hbm, comp, sems.at[2 * GROUPS]),
        pltpu.make_async_copy(pairs_hbm, pairs, sems.at[2 * GROUPS + 1]),
        pltpu.make_async_copy(
            cot_hbm, out_ref.at[:, pl.ds(each * packed, each * tile)], sems.at[2 * GROUPS + 2]
        ),
    ]
    for copy in loads + others:
        copy.start()
    for g, (low, high, size) in enumerate(groups):
        loads[2 * g].wait()
        loads[2 * g + 1].wait()
        for r in range(size):
            blocks = [
                (low + r, emb[low + r, :LANES]),
                (high + r, emb[high + r, :LANES]),
                (
                    tile + low + r,
                    jnp.concatenate([emb[low + r, LANES:], emb[high + r, LANES:]], axis=0),
                ),
            ]
            for place, block in blocks:
                turned[place * samples : (place + 1) * samples] = block.T.astype(f32)

    def peer(p, carry):
        for j in range(each):
            both = turned[pl.ds(p * each + j, packed, stride=samples), :]
            out_ref[p, j * packed : (j + 1) * packed] = both.astype(bf16)
        return carry

    lax.fori_loop(0, fields, peer, 0)
    for copy in others:
        copy.wait()
    slots = pairs.shape[1]
    number = lax.broadcasted_iota(jnp.int32, (LANES, slots), 0)
    live = lax.broadcasted_iota(jnp.int32, (LANES, slots), 1) < counts_ref[0]
    first = jnp.where((pairs[0:1] == number) & live, 1.0, 0.0).astype(bf16)
    second = jnp.where(pairs[1:2] == number, 1.0, 0.0).astype(bf16)
    table = lax.dot_general(first, second, TURN, preferred_element_type=f32)
    base = each * (packed + tile)
    for p in range(fields):
        out_ref[p, base : base + tile] = comp[...]
        out_ref[p, base + tile : base + tile + TABLE] = table[:TABLE].astype(bf16)


def pair_mask(x_ref, base, scale, mask, tile):
    fields = x_ref.shape[0]
    f32 = jnp.float32
    table = jnp.zeros((TABLE, LANES), f32)
    for f in range(fields):
        table += x_ref[f, base : base + TABLE].astype(f32)
    square = jnp.concatenate([table, jnp.zeros((LANES - TABLE, LANES), f32)], axis=0)
    on_diag = lax.broadcasted_iota(jnp.int32, square.shape, 0) == lax.broadcasted_iota(
        jnp.int32, square.shape, 1
    )
    mult = (square + square.T - jnp.where(on_diag, square, 0.0)) * scale
    for a in range(fields):
        row = jnp.concatenate(
            [jnp.broadcast_to(mult[a : a + 1, b : b + 1], (1, tile)) for b in range(fields)], axis=1
        )
        mask[a * tile : (a + 1) * tile] = jnp.broadcast_to(row, (tile, row.shape[1]))


def block_kernel(scale, tile, width, x_ref, y_ref, mask, grad, *sets):
    fields = x_ref.shape[0]
    half, rest = tile // 2, width - LANES
    packed = tile + half
    rows = packed + tile
    embeds = fields * tile
    f32, bf16 = jnp.float32, jnp.bfloat16
    each = (x_ref.shape[1] - tile - TABLE) // rows
    base = each * rows
    sets = [sets[i : i + 3] for i in range(0, len(sets), 3)]
    pair_mask(x_ref, base + tile, scale, mask, tile)
    weights = x_ref[:, base : base + tile].reshape(embeds, LANES)
    for _, sides, other in sets:
        sides[:, :LANES] = weights
        other[:, LANES:] = weights
    grad[...] = jnp.zeros_like(grad)

    def sample(j, emb, sides, other):
        start = pl.multiple_of(j * packed, 16)
        second = pl.multiple_of(each * packed + j * tile, 16)
        emb[:, :LANES] = x_ref[:, pl.ds(start, tile)].reshape(embeds, LANES)
        cot = x_ref[:, pl.ds(second, tile)].reshape(embeds, LANES)
        sides[:, LANES:] = cot
        other[:, :LANES] = cot
        tail = x_ref[:, pl.ds(start + tile, half)]
        upper = jnp.concatenate([tail[:, :, rest:], tail[:, :, :rest]], axis=2)
        both = jnp.concatenate([tail, upper], axis=1).reshape(embeds, LANES)
        emb[:, LANES:] = both[:, :rest]
        feats = emb[...]
        gram = lax.dot_general(feats, feats, TURN, preferred_element_type=f32)
        hmat = lax.dot_general(other[...], sides[...], TURN, preferred_element_type=f32)
        masked = (mask[...] * gram).astype(bf16)
        sym = (mask[...] * hmat).astype(bf16)
        both = jnp.dot(masked, sides[...], preferred_element_type=f32)
        dfeat = jnp.dot(sym, feats, preferred_element_type=f32).astype(bf16)
        y_ref[:, pl.ds(second, tile)] = both[:, :LANES].astype(bf16).reshape(fields, tile, LANES)
        y_ref[:, pl.ds(start, tile)] = dfeat[:, :LANES].reshape(fields, tile, LANES)
        last = dfeat[:, LANES:].reshape(fields, tile, rest)
        y_ref[:, pl.ds(start + tile, half)] = jnp.concatenate(
            [last[:, :half], last[:, half:]], axis=2
        )
        return both[:, LANES:]

    def some(i, carry):
        terms = [sample(i * len(sets) + u, *refs) for u, refs in enumerate(sets)]
        grad[...] += sum(terms[1:], terms[0])
        return carry

    lax.fori_loop(0, each // len(sets), some, 0)
    y_ref[:, base:] = grad[...].astype(bf16).reshape(fields, tile, LANES)


def turn(part, sorted_rows, dfeat_hbm, dfeat, sems):
    tile, width, samples = dfeat.shape
    rest = width - LANES
    packed = tile + tile // 2
    groups = row_groups(tile)
    share = len(groups) // 2

    def block(row):
        rows = sorted_rows[pl.ds(row, samples, stride=packed), :]
        return rows.astype(jnp.bfloat16).T

    copies = []
    for g, (low, high, size) in enumerate(groups[part * share : (part + 1) * share]):
        for r in range(size):
            for row in (low + r, high + r):
                dfeat[row, :LANES] = block(row)
            both = block(tile + low + r)
            dfeat[low + r, LANES:] = both[:rest]
            dfeat[high + r, LANES:] = both[rest:]
        for h, start in enumerate((low, high)):
            copy = pltpu.make_async_copy(
                dfeat.at[pl.ds(start, size)], dfeat_hbm.at[pl.ds(start, size)], sems.at[2 * g + h]
            )
            copy.start()
            copies.append(copy)
    return copies


def unpack_kernel(y_ref, mixed_hbm, dfeat_hbm, sorted_rows, dfeat, sems):
    fields, length = mixed_hbm.shape[:2]
    share = sorted_rows.shape[0] // fields
    mixed = pltpu.make_async_copy(
        y_ref.at[:, pl.ds(share, length)], mixed_hbm, sems.at[GROUPS]
    )
    mixed.start()
    for p in range(fields):
        sorted_rows[p * share : (p + 1) * share] = y_ref[p, :share].astype(jnp.float32)
    for copy in turn(0, sorted_rows, dfeat_hbm, dfeat, sems) + [mixed]:
        copy.wait()


def finish_kernel(sorted_rows, _, dfeat_hbm, dfeat, sems):
    for copy in turn(1, sorted_rows, dfeat_hbm, dfeat, sems):
        copy.wait()


def dp_sum(own):
    size = lax.axis_size("dp")

    def partner(value, flip):
        return lax.ppermute(value, "dp", [(i, i ^ flip) for i in range(size)])

    if size != 2 * ALONG_X:
        return lax.psum(own, "dp")
    total = own + partner(own, ALONG_X)
    return (total + partner(total, 1)) + (partner(total, 2) + partner(total, 3))


def per_device(emb, comp, cot, pairs, counts):
    samp_rows, tile, width = emb.shape
    fields = lax.axis_size("field")
    embeds = tile * fields
    packed = tile + tile // 2
    rows = packed + tile
    each = samp_rows // fields
    f32, bf16 = jnp.float32, jnp.bfloat16
    params = pltpu.CompilerParams(vmem_limit_bytes=24 * MIB)
    vmem = pl.BlockSpec(memory_space=pltpu.VMEM)
    smem = pl.BlockSpec(memory_space=pltpu.SMEM)
    hbm = pl.BlockSpec(memory_space=pltpu.HBM)
    turned = pltpu.VMEM((packed * samp_rows, LANES), f32)
    by_row = pltpu.VMEM((tile, width, samp_rows), bf16)

    def stay(array):
        return pltpu.with_memory_space_constraint(array, pltpu.HBM)

    def cost(flops, moved):
        return pl.CostEstimate(flops=flops, bytes_accessed=moved, transcendentals=0)

    x = pl.pallas_call(
        pack_kernel,
        out_shape=jax.ShapeDtypeStruct((fields, each * rows + tile + TABLE, LANES), bf16),
        in_specs=[hbm, hbm, hbm, hbm, smem],
        out_specs=vmem,
        scratch_shapes=[
            by_row,
            pltpu.VMEM(comp.shape, bf16),
            pltpu.VMEM(pairs.shape[::-1], jnp.int32),
            turned,
            pltpu.SemaphoreType.DMA((2 * GROUPS + 3,)),
        ],
        compiler_params=pltpu.CompilerParams(vmem_limit_bytes=24 * MIB),
        cost_estimate=cost(10**9, 8 * 10**6),
    )(
        stay(jnp.transpose(emb, (1, 2, 0))),
        stay(cot.reshape(fields, each * tile, LANES)),
        stay(comp),
        stay(pairs.T),
        counts,
    )
    x = lax.all_to_all(x, "field", 0, 0)
    y = pl.pallas_call(
        functools.partial(block_kernel, width ** (-0.5), tile, width),
        out_shape=jax.ShapeDtypeStruct((fields, each * rows + tile, LANES), bf16),
        in_specs=[vmem],
        out_specs=vmem,
        scratch_shapes=[pltpu.VMEM((embeds, embeds), f32), pltpu.VMEM((embeds, LANES), f32)]
        + [
            pltpu.VMEM((embeds, width), bf16),
            pltpu.VMEM((embeds, 2 * LANES), bf16),
            pltpu.VMEM((embeds, 2 * LANES), bf16),
        ]
        * AT_ONCE,
        compiler_params=params,
        cost_estimate=cost(4 * 10**9, 6 * 10**6),
    )(x)
    y = lax.all_to_all(y, "field", 0, 0)
    grad = dp_sum(jnp.sum(y[:, each * rows :].astype(f32), axis=0))
    weight_grad = grad / (samp_rows * lax.axis_size("dp"))

    by_row_out = jax.ShapeDtypeStruct((tile, width, samp_rows), bf16)
    mixed, emb_grad, sorted_rows = pl.pallas_call(
        unpack_kernel,
        out_shape=(
            jax.ShapeDtypeStruct((fields, each * tile, LANES), bf16),
            by_row_out,
            jax.ShapeDtypeStruct((packed * samp_rows, LANES), f32),
        ),
        in_specs=[vmem],
        out_specs=(hbm, hbm, vmem),
        scratch_shapes=[by_row, pltpu.SemaphoreType.DMA((GROUPS + 1,))],
        compiler_params=params,
        cost_estimate=cost(10**9, 8 * 10**6),
    )(y)
    (emb_grad,) = pl.pallas_call(
        finish_kernel,
        out_shape=(by_row_out,),
        in_specs=[vmem, hbm],
        out_specs=(hbm,),
        input_output_aliases={1: 0},
        scratch_shapes=[by_row, pltpu.SemaphoreType.DMA((GROUPS,))],
        compiler_params=params,
        cost_estimate=cost(10**9, 8 * 10**6),
    )(sorted_rows, emb_grad)
    return mixed.reshape(cot.shape), jnp.transpose(emb_grad, (2, 0, 1)), weight_grad


def solution(mesh):
    in_specs = (
        P("dp", "field", None),
        P("field", None),
        P("dp", "field", None),
        P("field", None),
        P("field"),
    )
    out_specs = (P("dp", "field", None), P("dp", "field", None), P("field", None))
    return jax.shard_map(
        per_device, mesh=mesh, in_specs=in_specs, out_specs=out_specs, check_vma=False
    )
```

```python
import functools

import jax
import jax.numpy as jnp
from jax import lax
from jax.experimental import pallas as pl
from jax.experimental.pallas import tpu as pltpu
from jax.sharding import PartitionSpec as P

LANES = 128
GROUPS = 8
AT_ONCE = 8
ALONG_X = 4
TABLE = 16
TURN = (((1,), (1,)), ((), ()))
MIB = 1024 * 1024


def row_groups(tile):
    size = tile // 2 // GROUPS
    return [(g * size, tile // 2 + g * size, size) for g in range(GROUPS)]


def pack_kernel(emb_hbm, cot_hbm, comp_hbm, pairs_hbm, counts_ref, out_ref, emb, comp, pairs, turned, sems):
    tile, width, samples = emb.shape
    fields = out_ref.shape[0]
    each = samples // fields
    packed = tile + tile // 2
    f32, bf16 = jnp.float32, jnp.bfloat16
    groups = row_groups(tile)
    loads = [
        pltpu.make_async_copy(
            emb_hbm.at[pl.ds(start, size)], emb.at[pl.ds(start, size)], sems.at[2 * g + h]
        )
        for g, (low, high, size) in enumerate(groups)
        for h, start in enumerate((low, high))
    ]
    others = [
        pltpu.make_async_copy(comp_hbm, comp, sems.at[2 * GROUPS]),
        pltpu.make_async_copy(pairs_hbm, pairs, sems.at[2 * GROUPS + 1]),
        pltpu.make_async_copy(
            cot_hbm, out_ref.at[:, pl.ds(each * packed, each * tile)], sems.at[2 * GROUPS + 2]
        ),
    ]
    for copy in loads + others:
        copy.start()
    for g, (low, high, size) in enumerate(groups):
        loads[2 * g].wait()
        loads[2 * g + 1].wait()
        for r in range(size):
            blocks = [
                (low + r, emb[low + r, :LANES]),
                (high + r, emb[high + r, :LANES]),
                (
                    tile + low + r,
                    jnp.concatenate([emb[low + r, LANES:], emb[high + r, LANES:]], axis=0),
                ),
            ]
            for place, block in blocks:
                turned[place * samples : (place + 1) * samples] = block.T.astype(f32)

    def peer(p, carry):
        for j in range(each):
            both = turned[pl.ds(p * each + j, packed, stride=samples), :]
            out_ref[p, j * packed : (j + 1) * packed] = both.astype(bf16)
        return carry

    lax.fori_loop(0, fields, peer, 0)
    for copy in others:
        copy.wait()
    slots = pairs.shape[1]
    number = lax.broadcasted_iota(jnp.int32, (LANES, slots), 0)
    live = lax.broadcasted_iota(jnp.int32, (LANES, slots), 1) < counts_ref[0]
    first = jnp.where((pairs[0:1] == number) & live, 1.0, 0.0).astype(bf16)
    second = jnp.where(pairs[1:2] == number, 1.0, 0.0).astype(bf16)
    table = lax.dot_general(first, second, TURN, preferred_element_type=f32)
    base = each * (packed + tile)
    for p in range(fields):
        out_ref[p, base : base + tile] = comp[...]
        out_ref[p, base + tile : base + tile + TABLE] = table[:TABLE].astype(bf16)


def pair_mask(x_ref, base, scale, mask, tile):
    fields = x_ref.shape[0]
    f32 = jnp.float32
    table = jnp.zeros((TABLE, LANES), f32)
    for f in range(fields):
        table += x_ref[f, base : base + TABLE].astype(f32)
    square = jnp.concatenate([table, jnp.zeros((LANES - TABLE, LANES), f32)], axis=0)
    on_diag = lax.broadcasted_iota(jnp.int32, square.shape, 0) == lax.broadcasted_iota(
        jnp.int32, square.shape, 1
    )
    mult = (square + square.T - jnp.where(on_diag, square, 0.0)) * scale
    for a in range(fields):
        row = jnp.concatenate(
            [jnp.broadcast_to(mult[a : a + 1, b : b + 1], (1, tile)) for b in range(fields)], axis=1
        )
        mask[a * tile : (a + 1) * tile] = jnp.broadcast_to(row, (tile, row.shape[1]))


def block_kernel(scale, tile, width, x_ref, y_ref, mask, grad, *sets):
    fields = x_ref.shape[0]
    half, rest = tile // 2, width - LANES
    packed = tile + half
    rows = packed + tile
    embeds = fields * tile
    f32, bf16 = jnp.float32, jnp.bfloat16
    each = (x_ref.shape[1] - tile - TABLE) // rows
    base = each * rows
    sets = [sets[i : i + 3] for i in range(0, len(sets), 3)]
    pair_mask(x_ref, base + tile, scale, mask, tile)
    weights = x_ref[:, base : base + tile].reshape(embeds, LANES)
    for _, sides, other in sets:
        sides[:, :LANES] = weights
        other[:, LANES:] = weights
    grad[...] = jnp.zeros_like(grad)

    def sample(j, emb, sides, other):
        start = pl.multiple_of(j * packed, 16)
        second = pl.multiple_of(each * packed + j * tile, 16)
        emb[:, :LANES] = x_ref[:, pl.ds(start, tile)].reshape(embeds, LANES)
        cot = x_ref[:, pl.ds(second, tile)].reshape(embeds, LANES)
        sides[:, LANES:] = cot
        other[:, :LANES] = cot
        tail = x_ref[:, pl.ds(start + tile, half)]
        upper = jnp.concatenate([tail[:, :, rest:], tail[:, :, :rest]], axis=2)
        both = jnp.concatenate([tail, upper], axis=1).reshape(embeds, LANES)
        emb[:, LANES:] = both[:, :rest]
        feats = emb[...]
        gram = lax.dot_general(feats, feats, TURN, preferred_element_type=f32)
        hmat = lax.dot_general(other[...], sides[...], TURN, preferred_element_type=f32)
        masked = (mask[...] * gram).astype(bf16)
        sym = (mask[...] * hmat).astype(bf16)
        both = jnp.dot(masked, sides[...], preferred_element_type=f32)
        dfeat = jnp.dot(sym, feats, preferred_element_type=f32).astype(bf16)
        y_ref[:, pl.ds(second, tile)] = both[:, :LANES].astype(bf16).reshape(fields, tile, LANES)
        y_ref[:, pl.ds(start, tile)] = dfeat[:, :LANES].reshape(fields, tile, LANES)
        last = dfeat[:, LANES:].reshape(fields, tile, rest)
        y_ref[:, pl.ds(start + tile, half)] = jnp.concatenate(
            [last[:, :half], last[:, half:]], axis=2
        )
        return both[:, LANES:]

    def some(i, carry):
        terms = [sample(i * len(sets) + u, *refs) for u, refs in enumerate(sets)]
        grad[...] += sum(terms[1:], terms[0])
        return carry

    lax.fori_loop(0, each // len(sets), some, 0)
    y_ref[:, base:] = grad[...].astype(bf16).reshape(fields, tile, LANES)


def turn(part, sorted_rows, dfeat_hbm, dfeat, sems):
    tile, width, samples = dfeat.shape
    rest = width - LANES
    packed = tile + tile // 2
    groups = row_groups(tile)
    share = len(groups) // 2

    def block(row):
        rows = sorted_rows[pl.ds(row, samples, stride=packed), :]
        return rows.astype(jnp.bfloat16).T

    copies = []
    for g, (low, high, size) in enumerate(groups[part * share : (part + 1) * share]):
        for r in range(size):
            for row in (low + r, high + r):
                dfeat[row, :LANES] = block(row)
            both = block(tile + low + r)
            dfeat[low + r, LANES:] = both[:rest]
            dfeat[high + r, LANES:] = both[rest:]
        for h, start in enumerate((low, high)):
            copy = pltpu.make_async_copy(
                dfeat.at[pl.ds(start, size)], dfeat_hbm.at[pl.ds(start, size)], sems.at[2 * g + h]
            )
            copy.start()
            copies.append(copy)
    return copies


def unpack_kernel(y_ref, mixed_hbm, dfeat_hbm, sorted_rows, dfeat, sems):
    fields, length = mixed_hbm.shape[:2]
    share = sorted_rows.shape[0] // fields
    mixed = pltpu.make_async_copy(
        y_ref.at[:, pl.ds(share, length)], mixed_hbm, sems.at[GROUPS]
    )
    mixed.start()
    for p in range(fields):
        sorted_rows[p * share : (p + 1) * share] = y_ref[p, :share].astype(jnp.float32)
    for copy in turn(0, sorted_rows, dfeat_hbm, dfeat, sems) + [mixed]:
        copy.wait()


def finish_kernel(sorted_rows, _, dfeat_hbm, dfeat, sems):
    for copy in turn(1, sorted_rows, dfeat_hbm, dfeat, sems):
        copy.wait()


def dp_sum(own):
    size = lax.axis_size("dp")

    def partner(value, flip):
        return lax.ppermute(value, "dp", [(i, i ^ flip) for i in range(size)])

    if size != 2 * ALONG_X:
        return lax.psum(own, "dp")
    total = own + partner(own, ALONG_X)
    first, third = partner(total, 1), partner(total, 3)
    second = partner(total, 2)
    return (total + second) + (third + first)


def per_device(emb, comp, cot, pairs, counts):
    samp_rows, tile, width = emb.shape
    fields = lax.axis_size("field")
    embeds = tile * fields
    packed = tile + tile // 2
    rows = packed + tile
    each = samp_rows // fields
    f32, bf16 = jnp.float32, jnp.bfloat16
    params = pltpu.CompilerParams(vmem_limit_bytes=24 * MIB)
    vmem = pl.BlockSpec(memory_space=pltpu.VMEM)
    smem = pl.BlockSpec(memory_space=pltpu.SMEM)
    hbm = pl.BlockSpec(memory_space=pltpu.HBM)
    turned = pltpu.VMEM((packed * samp_rows, LANES), f32)
    by_row = pltpu.VMEM((tile, width, samp_rows), bf16)

    def stay(array):
        return pltpu.with_memory_space_constraint(array, pltpu.HBM)

    def cost(flops, moved):
        return pl.CostEstimate(flops=flops, bytes_accessed=moved, transcendentals=0)

    x = pl.pallas_call(
        pack_kernel,
        out_shape=jax.ShapeDtypeStruct((fields, each * rows + tile + TABLE, LANES), bf16),
        in_specs=[hbm, hbm, hbm, hbm, smem],
        out_specs=vmem,
        scratch_shapes=[
            by_row,
            pltpu.VMEM(comp.shape, bf16),
            pltpu.VMEM(pairs.shape[::-1], jnp.int32),
            turned,
            pltpu.SemaphoreType.DMA((2 * GROUPS + 3,)),
        ],
        compiler_params=pltpu.CompilerParams(vmem_limit_bytes=24 * MIB),
        cost_estimate=cost(10**9, 8 * 10**6),
    )(
        stay(jnp.transpose(emb, (1, 2, 0))),
        stay(cot.reshape(fields, each * tile, LANES)),
        stay(comp),
        stay(pairs.T),
        counts,
    )
    x = lax.all_to_all(x, "field", 0, 0)
    y = pl.pallas_call(
        functools.partial(block_kernel, width ** (-0.5), tile, width),
        out_shape=jax.ShapeDtypeStruct((fields, each * rows + tile, LANES), bf16),
        in_specs=[vmem],
        out_specs=vmem,
        scratch_shapes=[pltpu.VMEM((embeds, embeds), f32), pltpu.VMEM((embeds, LANES), f32)]
        + [
            pltpu.VMEM((embeds, width), bf16),
            pltpu.VMEM((embeds, 2 * LANES), bf16),
            pltpu.VMEM((embeds, 2 * LANES), bf16),
        ]
        * AT_ONCE,
        compiler_params=params,
        cost_estimate=cost(4 * 10**9, 6 * 10**6),
    )(x)
    y = lax.all_to_all(y, "field", 0, 0)
    grad = dp_sum(jnp.sum(y[:, each * rows :].astype(f32), axis=0))
    weight_grad = grad / (samp_rows * lax.axis_size("dp"))

    by_row_out = jax.ShapeDtypeStruct((tile, width, samp_rows), bf16)
    mixed, emb_grad, sorted_rows = pl.pallas_call(
        unpack_kernel,
        out_shape=(
            jax.ShapeDtypeStruct((fields, each * tile, LANES), bf16),
            by_row_out,
            jax.ShapeDtypeStruct((packed * samp_rows, LANES), f32),
        ),
        in_specs=[vmem],
        out_specs=(hbm, hbm, vmem),
        scratch_shapes=[by_row, pltpu.SemaphoreType.DMA((GROUPS + 1,))],
        compiler_params=params,
        cost_estimate=cost(10**9, 8 * 10**6),
    )(y)
    (emb_grad,) = pl.pallas_call(
        finish_kernel,
        out_shape=(by_row_out,),
        in_specs=[vmem, hbm],
        out_specs=(hbm,),
        input_output_aliases={1: 0},
        scratch_shapes=[by_row, pltpu.SemaphoreType.DMA((GROUPS,))],
        compiler_params=params,
        cost_estimate=cost(10**9, 8 * 10**6),
    )(sorted_rows, emb_grad)
    return mixed.reshape(cot.shape), jnp.transpose(emb_grad, (2, 0, 1)), weight_grad


def solution(mesh):
    in_specs = (
        P("dp", "field", None),
        P("field", None),
        P("dp", "field", None),
        P("field", None),
        P("field"),
    )
    out_specs = (P("dp", "field", None), P("dp", "field", None), P("field", None))
    return jax.shard_map(
        per_device, mesh=mesh, in_specs=in_specs, out_specs=out_specs, check_vma=False
    )
```

```python
import functools

import jax
import jax.numpy as jnp
from jax import lax
from jax.experimental import pallas as pl
from jax.experimental.pallas import tpu as pltpu
from jax.sharding import PartitionSpec as P

LANES = 128
GROUPS = 4
AT_ONCE = 8
SETS = 4
ALONG_X = 4
TABLE = 16
TURN = (((1,), (1,)), ((), ()))
MIB = 1024 * 1024


def row_groups(tile):
    size = tile // 2 // GROUPS
    return [(g * size, tile // 2 + g * size, size) for g in range(GROUPS)]


def pack_kernel(emb_hbm, cot_hbm, comp_hbm, pairs_hbm, counts_ref, out_ref, emb, comp, pairs, turned, sems):
    tile, width, samples = emb.shape
    fields = out_ref.shape[0]
    each = samples // fields
    packed = tile + tile // 2
    f32, bf16 = jnp.float32, jnp.bfloat16
    groups = row_groups(tile)
    loads = [
        pltpu.make_async_copy(
            emb_hbm.at[pl.ds(start, size)], emb.at[pl.ds(start, size)], sems.at[2 * g + h]
        )
        for g, (low, high, size) in enumerate(groups)
        for h, start in enumerate((low, high))
    ]
    others = [
        pltpu.make_async_copy(comp_hbm, comp, sems.at[2 * GROUPS]),
        pltpu.make_async_copy(pairs_hbm, pairs, sems.at[2 * GROUPS + 1]),
        pltpu.make_async_copy(
            cot_hbm, out_ref.at[:, pl.ds(each * packed, each * tile)], sems.at[2 * GROUPS + 2]
        ),
    ]
    for copy in others[:2] + loads + others[2:]:
        copy.start()
    for copy in others[:2]:
        copy.wait()
    slots = pairs.shape[1]
    number = lax.broadcasted_iota(jnp.int32, (LANES, slots), 0)
    live = lax.broadcasted_iota(jnp.int32, (LANES, slots), 1) < counts_ref[0]
    first = jnp.where((pairs[0:1] == number) & live, 1.0, 0.0).astype(bf16)
    second = jnp.where(pairs[1:2] == number, 1.0, 0.0).astype(bf16)
    table = lax.dot_general(first, second, TURN, preferred_element_type=f32)
    base = each * (packed + tile)
    for p in range(fields):
        out_ref[p, base : base + tile] = comp[...]
        out_ref[p, base + tile : base + tile + TABLE] = table[:TABLE].astype(bf16)
    for g, (low, high, size) in enumerate(groups):
        loads[2 * g].wait()
        loads[2 * g + 1].wait()
        for r in range(size):
            blocks = [
                (low + r, emb[low + r, :LANES]),
                (high + r, emb[high + r, :LANES]),
                (
                    tile + low + r,
                    jnp.concatenate([emb[low + r, LANES:], emb[high + r, LANES:]], axis=0),
                ),
            ]
            for place, block in blocks:
                turned[place * samples : (place + 1) * samples] = block.T.astype(f32)

    def peer(p, carry):
        for j in range(each):
            both = turned[pl.ds(p * each + j, packed, stride=samples), :]
            out_ref[p, j * packed : (j + 1) * packed] = both.astype(bf16)
        return carry

    lax.fori_loop(0, fields, peer, 0)
    others[2].wait()


def pair_mask(x_ref, base, scale, mask, tile):
    fields = x_ref.shape[0]
    f32 = jnp.float32
    table = jnp.zeros((TABLE, LANES), f32)
    for f in range(fields):
        table += x_ref[f, base : base + TABLE].astype(f32)
    square = jnp.concatenate([table, jnp.zeros((LANES - TABLE, LANES), f32)], axis=0)
    on_diag = lax.broadcasted_iota(jnp.int32, square.shape, 0) == lax.broadcasted_iota(
        jnp.int32, square.shape, 1
    )
    mult = (square + square.T - jnp.where(on_diag, square, 0.0)) * scale
    for a in range(fields):
        row = jnp.concatenate(
            [jnp.broadcast_to(mult[a : a + 1, b : b + 1], (1, tile)) for b in range(fields)], axis=1
        )
        mask[a * tile : (a + 1) * tile] = jnp.broadcast_to(row, (tile, row.shape[1]))


def block_kernel(scale, tile, width, x_ref, y_ref, mask, grad, *sets):
    fields = x_ref.shape[0]
    half, rest = tile // 2, width - LANES
    packed = tile + half
    rows = packed + tile
    embeds = fields * tile
    f32, bf16 = jnp.float32, jnp.bfloat16
    each = (x_ref.shape[1] - tile - TABLE) // rows
    base = each * rows
    sets = [sets[i : i + 3] for i in range(0, len(sets), 3)]
    pair_mask(x_ref, base + tile, scale, mask, tile)
    weights = x_ref[:, base : base + tile].reshape(embeds, LANES)
    for _, sides, other in sets:
        sides[:, :LANES] = weights
        other[:, LANES:] = weights
    grad[...] = jnp.zeros_like(grad)

    def sample(j, emb, sides, other):
        start = pl.multiple_of(j * packed, 16)
        second = pl.multiple_of(each * packed + j * tile, 16)
        emb[:, :LANES] = x_ref[:, pl.ds(start, tile)].reshape(embeds, LANES)
        cot = x_ref[:, pl.ds(second, tile)].reshape(embeds, LANES)
        sides[:, LANES:] = cot
        other[:, :LANES] = cot
        tail = x_ref[:, pl.ds(start + tile, half)]
        upper = jnp.concatenate([tail[:, :, rest:], tail[:, :, :rest]], axis=2)
        both = jnp.concatenate([tail, upper], axis=1).reshape(embeds, LANES)
        emb[:, LANES:] = both[:, :rest]
        feats = emb[...]
        gram = lax.dot_general(feats, feats, TURN, preferred_element_type=f32)
        hmat = lax.dot_general(other[...], sides[...], TURN, preferred_element_type=f32)
        masked = (mask[...] * gram).astype(bf16)
        sym = (mask[...] * hmat).astype(bf16)
        both = jnp.dot(masked, sides[...], preferred_element_type=f32)
        dfeat = jnp.dot(sym, feats, preferred_element_type=f32).astype(bf16)
        y_ref[:, pl.ds(second, tile)] = both[:, :LANES].astype(bf16).reshape(fields, tile, LANES)
        y_ref[:, pl.ds(start, tile)] = dfeat[:, :LANES].reshape(fields, tile, LANES)
        last = dfeat[:, LANES:].reshape(fields, tile, rest)
        y_ref[:, pl.ds(start + tile, half)] = jnp.concatenate(
            [last[:, :half], last[:, half:]], axis=2
        )
        return both[:, LANES:]

    def some(i, carry):
        terms = [sample(i * AT_ONCE + u, *sets[u % SETS]) for u in range(AT_ONCE)]
        grad[...] += sum(terms[1:], terms[0])
        return carry

    lax.fori_loop(0, each // AT_ONCE, some, 0)
    y_ref[:, base:] = grad[...].astype(bf16).reshape(fields, tile, LANES)


def turn(part, sorted_rows, dfeat_hbm, dfeat, sems):
    tile, width, samples = dfeat.shape
    rest = width - LANES
    packed = tile + tile // 2
    groups = row_groups(tile)
    share = len(groups) // 2

    def block(row):
        rows = sorted_rows[pl.ds(row, samples, stride=packed), :]
        return rows.astype(jnp.bfloat16).T

    copies = []
    for g, (low, high, size) in enumerate(groups[part * share : (part + 1) * share]):
        for r in range(size):
            for row in (low + r, high + r):
                dfeat[row, :LANES] = block(row)
            both = block(tile + low + r)
            dfeat[low + r, LANES:] = both[:rest]
            dfeat[high + r, LANES:] = both[rest:]
        for h, start in enumerate((low, high)):
            copy = pltpu.make_async_copy(
                dfeat.at[pl.ds(start, size)], dfeat_hbm.at[pl.ds(start, size)], sems.at[2 * g + h]
            )
            copy.start()
            copies.append(copy)
    return copies


def unpack_kernel(y_ref, mixed_hbm, dfeat_hbm, sorted_rows, dfeat, sems):
    fields, length = mixed_hbm.shape[:2]
    share = sorted_rows.shape[0] // fields
    mixed = pltpu.make_async_copy(
        y_ref.at[:, pl.ds(share, length)], mixed_hbm, sems.at[GROUPS]
    )
    mixed.start()
    for p in range(fields):
        sorted_rows[p * share : (p + 1) * share] = y_ref[p, :share].astype(jnp.float32)
    for copy in turn(0, sorted_rows, dfeat_hbm, dfeat, sems) + [mixed]:
        copy.wait()


def finish_kernel(sorted_rows, _, dfeat_hbm, dfeat, sems):
    for copy in turn(1, sorted_rows, dfeat_hbm, dfeat, sems):
        copy.wait()


def dp_sum(own):
    size = lax.axis_size("dp")

    def partner(value, flip):
        return lax.ppermute(value, "dp", [(i, i ^ flip) for i in range(size)])

    if size != 2 * ALONG_X:
        return lax.psum(own, "dp")
    total = own + partner(own, ALONG_X)
    return (total + partner(total, 1)) + (partner(total, 2) + partner(total, 3))


def per_device(emb, comp, cot, pairs, counts):
    samp_rows, tile, width = emb.shape
    fields = lax.axis_size("field")
    embeds = tile * fields
    packed = tile + tile // 2
    rows = packed + tile
    each = samp_rows // fields
    f32, bf16 = jnp.float32, jnp.bfloat16
    params = pltpu.CompilerParams(vmem_limit_bytes=24 * MIB)
    vmem = pl.BlockSpec(memory_space=pltpu.VMEM)
    smem = pl.BlockSpec(memory_space=pltpu.SMEM)
    hbm = pl.BlockSpec(memory_space=pltpu.HBM)
    turned = pltpu.VMEM((packed * samp_rows, LANES), f32)
    by_row = pltpu.VMEM((tile, width, samp_rows), bf16)

    def stay(array):
        return pltpu.with_memory_space_constraint(array, pltpu.HBM)

    def cost(flops, moved):
        return pl.CostEstimate(flops=flops, bytes_accessed=moved, transcendentals=0)

    x = pl.pallas_call(
        pack_kernel,
        out_shape=jax.ShapeDtypeStruct((fields, each * rows + tile + TABLE, LANES), bf16),
        in_specs=[hbm, hbm, hbm, hbm, smem],
        out_specs=vmem,
        scratch_shapes=[
            by_row,
            pltpu.VMEM(comp.shape, bf16),
            pltpu.VMEM(pairs.shape[::-1], jnp.int32),
            turned,
            pltpu.SemaphoreType.DMA((2 * GROUPS + 3,)),
        ],
        compiler_params=pltpu.CompilerParams(vmem_limit_bytes=24 * MIB),
        cost_estimate=cost(10**9, 8 * 10**6),
    )(
        stay(jnp.transpose(emb, (1, 2, 0))),
        stay(cot.reshape(fields, each * tile, LANES)),
        stay(comp),
        stay(pairs.T),
        counts,
    )
    x = lax.all_to_all(x, "field", 0, 0)
    y = pl.pallas_call(
        functools.partial(block_kernel, width ** (-0.5), tile, width),
        out_shape=jax.ShapeDtypeStruct((fields, each * rows + tile, LANES), bf16),
        in_specs=[vmem],
        out_specs=vmem,
        scratch_shapes=[pltpu.VMEM((embeds, embeds), f32), pltpu.VMEM((embeds, LANES), f32)]
        + [
            pltpu.VMEM((embeds, width), bf16),
            pltpu.VMEM((embeds, 2 * LANES), bf16),
            pltpu.VMEM((embeds, 2 * LANES), bf16),
        ]
        * SETS,
        compiler_params=params,
        cost_estimate=cost(4 * 10**9, 6 * 10**6),
    )(x)
    y = lax.all_to_all(y, "field", 0, 0)
    grad = dp_sum(jnp.sum(y[:, each * rows :].astype(f32), axis=0))
    weight_grad = grad / (samp_rows * lax.axis_size("dp"))

    by_row_out = jax.ShapeDtypeStruct((tile, width, samp_rows), bf16)
    mixed, emb_grad, sorted_rows = pl.pallas_call(
        unpack_kernel,
        out_shape=(
            jax.ShapeDtypeStruct((fields, each * tile, LANES), bf16),
            by_row_out,
            jax.ShapeDtypeStruct((packed * samp_rows, LANES), f32),
        ),
        in_specs=[vmem],
        out_specs=(hbm, hbm, vmem),
        scratch_shapes=[by_row, pltpu.SemaphoreType.DMA((GROUPS + 1,))],
        compiler_params=params,
        cost_estimate=cost(10**9, 8 * 10**6),
    )(y)
    (emb_grad,) = pl.pallas_call(
        finish_kernel,
        out_shape=(by_row_out,),
        in_specs=[vmem, hbm],
        out_specs=(hbm,),
        input_output_aliases={1: 0},
        scratch_shapes=[by_row, pltpu.SemaphoreType.DMA((GROUPS,))],
        compiler_params=params,
        cost_estimate=cost(10**9, 8 * 10**6),
    )(sorted_rows, emb_grad)
    return mixed.reshape(cot.shape), jnp.transpose(emb_grad, (2, 0, 1)), weight_grad


def solution(mesh):
    in_specs = (
        P("dp", "field", None),
        P("field", None),
        P("dp", "field", None),
        P("field", None),
        P("field"),
    )
    out_specs = (P("dp", "field", None), P("dp", "field", None), P("field", None))
    return jax.shard_map(
        per_device, mesh=mesh, in_specs=in_specs, out_specs=out_specs, check_vma=False
    )
```

```python
import functools

import jax
import jax.numpy as jnp
from jax import lax
from jax.experimental import pallas as pl
from jax.experimental.pallas import tpu as pltpu
from jax.sharding import PartitionSpec as P

LANES = 128
GROUPS = 4
HALVES = 2
SETS = 4
ALONG_X = 4
TABLE = 16
TURN = (((1,), (1,)), ((), ()))
MIB = 1024 * 1024


def row_groups(tile):
    size = tile // 2 // GROUPS
    return [(g * size, tile // 2 + g * size, size) for g in range(GROUPS)]


def pack_kernel(emb_hbm, cot_hbm, comp_hbm, pairs_hbm, counts_ref, out_ref, emb, comp, pairs, turned, sems):
    tile, width, samples = emb.shape
    fields = out_ref.shape[0]
    each = samples // fields
    packed = tile + tile // 2
    f32, bf16 = jnp.float32, jnp.bfloat16
    groups = row_groups(tile)
    loads = [
        pltpu.make_async_copy(
            emb_hbm.at[pl.ds(start, size)], emb.at[pl.ds(start, size)], sems.at[2 * g + h]
        )
        for g, (low, high, size) in enumerate(groups)
        for h, start in enumerate((low, high))
    ]
    length = each // HALVES * tile
    others = [
        pltpu.make_async_copy(comp_hbm, comp, sems.at[2 * GROUPS]),
        pltpu.make_async_copy(pairs_hbm, pairs, sems.at[2 * GROUPS + 1]),
    ] + [
        pltpu.make_async_copy(
            cot_hbm.at[h],
            out_ref.at[:, pl.ds(each * packed + h * length, length)],
            sems.at[2 * GROUPS + 2 + h],
        )
        for h in range(HALVES)
    ]
    for copy in others[:2] + loads + others[2:]:
        copy.start()
    for copy in others[:2]:
        copy.wait()
    slots = pairs.shape[1]
    number = lax.broadcasted_iota(jnp.int32, (LANES, slots), 0)
    live = lax.broadcasted_iota(jnp.int32, (LANES, slots), 1) < counts_ref[0]
    first = jnp.where((pairs[0:1] == number) & live, 1.0, 0.0).astype(bf16)
    second = jnp.where(pairs[1:2] == number, 1.0, 0.0).astype(bf16)
    table = lax.dot_general(first, second, TURN, preferred_element_type=f32)
    base = each * (packed + tile)
    for p in range(fields):
        out_ref[p, base : base + tile] = comp[...]
        out_ref[p, base + tile : base + tile + TABLE] = table[:TABLE].astype(bf16)
    for g, (low, high, size) in enumerate(groups):
        loads[2 * g].wait()
        loads[2 * g + 1].wait()
        for r in range(size):
            blocks = [
                (low + r, emb[low + r, :LANES]),
                (high + r, emb[high + r, :LANES]),
                (
                    tile + low + r,
                    jnp.concatenate([emb[low + r, LANES:], emb[high + r, LANES:]], axis=0),
                ),
            ]
            for place, block in blocks:
                turned[place * samples : (place + 1) * samples] = block.T.astype(f32)

    def peer(p, carry):
        for j in range(each):
            half, rank = divmod(j, each // HALVES)
            number = half * (samples // HALVES) + p * (each // HALVES) + rank
            both = turned[pl.ds(number, packed, stride=samples), :]
            out_ref[p, j * packed : (j + 1) * packed] = both.astype(bf16)
        return carry

    lax.fori_loop(0, fields, peer, 0)
    for copy in others[2:]:
        copy.wait()


def pair_mask(x_ref, base, scale, mask, tile):
    fields = x_ref.shape[0]
    f32 = jnp.float32
    table = jnp.zeros((TABLE, LANES), f32)
    for f in range(fields):
        table += x_ref[f, base : base + TABLE].astype(f32)
    square = jnp.concatenate([table, jnp.zeros((LANES - TABLE, LANES), f32)], axis=0)
    on_diag = lax.broadcasted_iota(jnp.int32, square.shape, 0) == lax.broadcasted_iota(
        jnp.int32, square.shape, 1
    )
    mult = (square + square.T - jnp.where(on_diag, square, 0.0)) * scale
    for a in range(fields):
        row = jnp.concatenate(
            [jnp.broadcast_to(mult[a : a + 1, b : b + 1], (1, tile)) for b in range(fields)], axis=1
        )
        mask[a * tile : (a + 1) * tile] = jnp.broadcast_to(row, (tile, row.shape[1]))


def block_kernel(scale, tile, width, x_ref, *refs):
    fields = x_ref.shape[0]
    half, rest = tile // 2, width - LANES
    packed = tile + half
    rows = packed + tile
    embeds = fields * tile
    f32, bf16 = jnp.float32, jnp.bfloat16
    each = (x_ref.shape[1] - tile - TABLE) // rows
    base = each * rows
    y_refs, (mask, grad), sets = refs[:HALVES], refs[HALVES : HALVES + 2], refs[HALVES + 2 :]
    sets = [sets[i : i + 3] for i in range(0, len(sets), 3)]
    pair_mask(x_ref, base + tile, scale, mask, tile)
    weights = x_ref[:, base : base + tile].reshape(embeds, LANES)
    for _, sides, other in sets:
        sides[:, :LANES] = weights
        other[:, LANES:] = weights
    grad[...] = jnp.zeros_like(grad)

    def sample(j, emb, sides, other):
        start, second = j * packed, each * packed + j * tile
        emb[:, :LANES] = x_ref[:, pl.ds(start, tile)].reshape(embeds, LANES)
        cot = x_ref[:, pl.ds(second, tile)].reshape(embeds, LANES)
        sides[:, LANES:] = cot
        other[:, :LANES] = cot
        tail = x_ref[:, pl.ds(start + tile, half)]
        upper = jnp.concatenate([tail[:, :, rest:], tail[:, :, :rest]], axis=2)
        both = jnp.concatenate([tail, upper], axis=1).reshape(embeds, LANES)
        emb[:, LANES:] = both[:, :rest]
        feats = emb[...]
        gram = lax.dot_general(feats, feats, TURN, preferred_element_type=f32)
        hmat = lax.dot_general(other[...], sides[...], TURN, preferred_element_type=f32)
        masked = (mask[...] * gram).astype(bf16)
        sym = (mask[...] * hmat).astype(bf16)
        both = jnp.dot(masked, sides[...], preferred_element_type=f32)
        dfeat = jnp.dot(sym, feats, preferred_element_type=f32).astype(bf16)
        share = each // HALVES
        y_ref = y_refs[j // share]
        start, second = j % share * packed, share * packed + j % share * tile
        y_ref[:, pl.ds(second, tile)] = both[:, :LANES].astype(bf16).reshape(fields, tile, LANES)
        y_ref[:, pl.ds(start, tile)] = dfeat[:, :LANES].reshape(fields, tile, LANES)
        last = dfeat[:, LANES:].reshape(fields, tile, rest)
        y_ref[:, pl.ds(start + tile, half)] = jnp.concatenate([last[:, :half], last[:, half:]], axis=2)
        return both[:, LANES:]

    for j in range(each):
        grad[...] += sample(j, *sets[j % SETS])
    y_refs[0][:, base // HALVES :] = grad[...].astype(bf16).reshape(fields, tile, LANES)


def cast_rows(y_ref, rows_ref):
    fields = y_ref.shape[0]
    share = rows_ref.shape[0] // fields
    for p in range(fields):
        rows_ref[p * share : (p + 1) * share] = y_ref[p, :share].astype(jnp.float32)


def early_kernel(y_ref, mixed_hbm, rows_ref, sem):
    fields, length = mixed_hbm.shape[1:3]
    share = rows_ref.shape[0] // fields
    copy = pltpu.make_async_copy(y_ref.at[:, pl.ds(share, length)], mixed_hbm.at[0], sem)
    copy.start()
    cast_rows(y_ref, rows_ref)
    copy.wait()


def late_kernel(y_ref, rows_ref, _, mixed_hbm, dfeat_hbm, more, dfeat, sems):
    tile, width, samples = dfeat.shape
    rest = width - LANES
    packed = tile + tile // 2
    fields, length = mixed_hbm.shape[1:3]
    share = rows_ref.shape[0] // fields
    copies = [
        pltpu.make_async_copy(
            y_ref.at[:, pl.ds(share, length)], mixed_hbm.at[1], sems.at[2 * GROUPS]
        )
    ]
    copies[0].start()
    cast_rows(y_ref, more)

    def block(row):
        halves = [
            ref[pl.ds(row, samples // HALVES, stride=packed), :] for ref in (rows_ref, more)
        ]
        return jnp.concatenate(halves, axis=0).astype(jnp.bfloat16).T

    for g, (low, high, size) in enumerate(row_groups(tile)):
        for r in range(size):
            for row in (low + r, high + r):
                dfeat[row, :LANES] = block(row)
            both = block(tile + low + r)
            dfeat[low + r, LANES:] = both[:rest]
            dfeat[high + r, LANES:] = both[rest:]
        for h, start in enumerate((low, high)):
            copy = pltpu.make_async_copy(
                dfeat.at[pl.ds(start, size)], dfeat_hbm.at[pl.ds(start, size)], sems.at[2 * g + h]
            )
            copy.start()
            copies.append(copy)
    for copy in copies:
        copy.wait()


def dp_sum(own):
    size = lax.axis_size("dp")

    def partner(value, flip):
        return lax.ppermute(value, "dp", [(i, i ^ flip) for i in range(size)])

    if size != 2 * ALONG_X:
        return lax.psum(own, "dp")
    total = (own + partner(own, 1)) + (partner(own, 2) + partner(own, 3))
    return total + partner(total, ALONG_X)


def per_device(emb, comp, cot, pairs, counts):
    samp_rows, tile, width = emb.shape
    fields = lax.axis_size("field")
    embeds = tile * fields
    packed = tile + tile // 2
    rows = packed + tile
    each = samp_rows // fields
    f32, bf16 = jnp.float32, jnp.bfloat16
    params = pltpu.CompilerParams(vmem_limit_bytes=24 * MIB)
    vmem = pl.BlockSpec(memory_space=pltpu.VMEM)
    smem = pl.BlockSpec(memory_space=pltpu.SMEM)
    hbm = pl.BlockSpec(memory_space=pltpu.HBM)
    turned = pltpu.VMEM((packed * samp_rows, LANES), f32)
    by_row = pltpu.VMEM((tile, width, samp_rows), bf16)

    def stay(array):
        return pltpu.with_memory_space_constraint(array, pltpu.HBM)

    def cost(flops, moved):
        return pl.CostEstimate(flops=flops, bytes_accessed=moved, transcendentals=0)

    x = pl.pallas_call(
        pack_kernel,
        out_shape=jax.ShapeDtypeStruct((fields, each * rows + tile + TABLE, LANES), bf16),
        in_specs=[hbm, hbm, hbm, hbm, smem],
        out_specs=vmem,
        scratch_shapes=[
            by_row,
            pltpu.VMEM(comp.shape, bf16),
            pltpu.VMEM(pairs.shape[::-1], jnp.int32),
            turned,
            pltpu.SemaphoreType.DMA((2 * GROUPS + 2 + HALVES,)),
        ],
        compiler_params=pltpu.CompilerParams(vmem_limit_bytes=24 * MIB),
        cost_estimate=cost(10**9, 8 * 10**6),
    )(
        stay(jnp.transpose(emb, (1, 2, 0))),
        stay(cot.reshape(HALVES, fields, each // HALVES * tile, LANES)),
        stay(comp),
        stay(pairs.T),
        counts,
    )
    x = lax.all_to_all(x, "field", 0, 0)
    y, z = pl.pallas_call(
        functools.partial(block_kernel, width ** (-0.5), tile, width),
        out_shape=(
            jax.ShapeDtypeStruct((fields, each // HALVES * rows + tile, LANES), bf16),
            jax.ShapeDtypeStruct((fields, each // HALVES * rows, LANES), bf16),
        ),
        in_specs=[vmem],
        out_specs=(vmem, vmem),
        scratch_shapes=[pltpu.VMEM((embeds, embeds), f32), pltpu.VMEM((embeds, LANES), f32)]
        + [
            pltpu.VMEM((embeds, width), bf16),
            pltpu.VMEM((embeds, 2 * LANES), bf16),
            pltpu.VMEM((embeds, 2 * LANES), bf16),
        ]
        * SETS,
        compiler_params=params,
        cost_estimate=cost(4 * 10**9, 6 * 10**6),
    )(x)
    y = lax.all_to_all(y, "field", 0, 0)
    y, z = lax.optimization_barrier((y, z))
    z = lax.all_to_all(z, "field", 0, 0)
    grad = dp_sum(jnp.sum(y[:, each // HALVES * rows :].astype(f32), axis=0))
    weight_grad = grad / (samp_rows * lax.axis_size("dp"))

    mixed_out = jax.ShapeDtypeStruct((HALVES, fields, each // HALVES * tile, LANES), bf16)
    half_rows = (packed * samp_rows // HALVES, LANES)
    mixed, sorted_rows = pl.pallas_call(
        early_kernel,
        out_shape=(mixed_out, jax.ShapeDtypeStruct(half_rows, f32)),
        in_specs=[vmem],
        out_specs=(hbm, vmem),
        scratch_shapes=[pltpu.SemaphoreType.DMA],
        compiler_params=params,
        cost_estimate=cost(10**8, 4 * 10**6),
    )(y)
    mixed, emb_grad = pl.pallas_call(
        late_kernel,
        out_shape=(mixed_out, jax.ShapeDtypeStruct((tile, width, samp_rows), bf16)),
        in_specs=[vmem, vmem, hbm],
        out_specs=(hbm, hbm),
        input_output_aliases={2: 0},
        scratch_shapes=[
            pltpu.VMEM(half_rows, f32),
            by_row,
            pltpu.SemaphoreType.DMA((2 * GROUPS + 1,)),
        ],
        compiler_params=params,
        cost_estimate=cost(10**9, 8 * 10**6),
    )(z, sorted_rows, mixed)
    return mixed.reshape(cot.shape), jnp.transpose(emb_grad, (2, 0, 1)), weight_grad


def solution(mesh):
    in_specs = (
        P("dp", "field", None),
        P("field", None),
        P("dp", "field", None),
        P("field", None),
        P("field"),
    )
    out_specs = (P("dp", "field", None), P("dp", "field", None), P("field", None))
    return jax.shard_map(
        per_device, mesh=mesh, in_specs=in_specs, out_specs=out_specs, check_vma=False
    )
```

```python
import functools

import jax
import jax.numpy as jnp
from jax import lax
from jax.experimental import pallas as pl
from jax.experimental.pallas import tpu as pltpu
from jax.sharding import PartitionSpec as P

LANES = 128
GROUPS = 4
HALVES = 2
SETS = 4
ALONG_X = 4
TABLE = 16
TURN = (((1,), (1,)), ((), ()))
MIB = 1024 * 1024


def row_groups(tile):
    size = tile // 2 // GROUPS
    return [(g * size, tile // 2 + g * size, size) for g in range(GROUPS)]


def pack_kernel(emb_hbm, cot_hbm, comp_hbm, pairs_hbm, counts_ref, out_ref, emb, comp, pairs, turned, sems):
    tile, width, samples = emb.shape
    fields = out_ref.shape[0]
    each = samples // fields
    packed = tile + tile // 2
    f32, bf16 = jnp.float32, jnp.bfloat16
    groups = row_groups(tile)
    loads = [
        pltpu.make_async_copy(
            emb_hbm.at[pl.ds(start, size)], emb.at[pl.ds(start, size)], sems.at[2 * g + h]
        )
        for g, (low, high, size) in enumerate(groups)
        for h, start in enumerate((low, high))
    ]
    length = each // HALVES * tile
    others = [
        pltpu.make_async_copy(comp_hbm, comp, sems.at[2 * GROUPS]),
        pltpu.make_async_copy(pairs_hbm, pairs, sems.at[2 * GROUPS + 1]),
    ] + [
        pltpu.make_async_copy(
            cot_hbm.at[h],
            out_ref.at[:, pl.ds(each * packed + h * length, length)],
            sems.at[2 * GROUPS + 2 + h],
        )
        for h in range(HALVES)
    ]
    for copy in others[:2] + loads + others[2:]:
        copy.start()
    for copy in others[:2]:
        copy.wait()
    slots = pairs.shape[1]
    number = lax.broadcasted_iota(jnp.int32, (LANES, slots), 0)
    live = lax.broadcasted_iota(jnp.int32, (LANES, slots), 1) < counts_ref[0]
    first = jnp.where((pairs[0:1] == number) & live, 1.0, 0.0).astype(bf16)
    second = jnp.where(pairs[1:2] == number, 1.0, 0.0).astype(bf16)
    table = lax.dot_general(first, second, TURN, preferred_element_type=f32)
    base = each * (packed + tile)
    for p in range(fields):
        out_ref[p, base : base + tile] = comp[...]
        out_ref[p, base + tile : base + tile + TABLE] = table[:TABLE].astype(bf16)
    for g, (low, high, size) in enumerate(groups):
        loads[2 * g].wait()
        loads[2 * g + 1].wait()
        for r in range(size):
            blocks = [
                (low + r, emb[low + r, :LANES]),
                (high + r, emb[high + r, :LANES]),
                (
                    tile + low + r,
                    jnp.concatenate([emb[low + r, LANES:], emb[high + r, LANES:]], axis=0),
                ),
            ]
            for place, block in blocks:
                turned[place * samples : (place + 1) * samples] = block.T.astype(f32)

    def peer(p, carry):
        for j in range(each):
            half, rank = divmod(j, each // HALVES)
            number = half * (samples // HALVES) + p * (each // HALVES) + rank
            both = turned[pl.ds(number, packed, stride=samples), :]
            out_ref[p, j * packed : (j + 1) * packed] = both.astype(bf16)
        return carry

    lax.fori_loop(0, fields, peer, 0)
    for copy in others[2:]:
        copy.wait()


def pair_mask(x_ref, base, scale, mask, tile):
    fields = x_ref.shape[0]
    f32 = jnp.float32
    table = jnp.zeros((TABLE, LANES), f32)
    for f in range(fields):
        table += x_ref[f, base : base + TABLE].astype(f32)
    square = jnp.concatenate([table, jnp.zeros((LANES - TABLE, LANES), f32)], axis=0)
    on_diag = lax.broadcasted_iota(jnp.int32, square.shape, 0) == lax.broadcasted_iota(
        jnp.int32, square.shape, 1
    )
    mult = (square + square.T - jnp.where(on_diag, square, 0.0)) * scale
    for a in range(fields):
        row = jnp.concatenate(
            [jnp.broadcast_to(mult[a : a + 1, b : b + 1], (1, tile)) for b in range(fields)], axis=1
        )
        mask[a * tile : (a + 1) * tile] = jnp.broadcast_to(row, (tile, row.shape[1]))


def block_kernel(scale, tile, width, x_ref, *refs):
    fields = x_ref.shape[0]
    half, rest = tile // 2, width - LANES
    packed = tile + half
    rows = packed + tile
    embeds = fields * tile
    f32, bf16 = jnp.float32, jnp.bfloat16
    each = (x_ref.shape[1] - tile - TABLE) // rows
    base = each * rows
    y_refs, (mask, grad), sets = refs[:HALVES], refs[HALVES : HALVES + 2], refs[HALVES + 2 :]
    sets = [sets[i : i + 3] for i in range(0, len(sets), 3)]
    pair_mask(x_ref, base + tile, scale, mask, tile)
    weights = x_ref[:, base : base + tile].reshape(embeds, LANES)
    for _, sides, other in sets:
        sides[:, :LANES] = weights
        other[:, LANES:] = weights
    grad[...] = jnp.zeros_like(grad)

    def sample(j, emb, sides, other):
        start, second = j * packed, each * packed + j * tile
        emb[:, :LANES] = x_ref[:, pl.ds(start, tile)].reshape(embeds, LANES)
        cot = x_ref[:, pl.ds(second, tile)].reshape(embeds, LANES)
        sides[:, LANES:] = cot
        other[:, :LANES] = cot
        tail = x_ref[:, pl.ds(start + tile, half)]
        upper = jnp.concatenate([tail[:, :, rest:], tail[:, :, :rest]], axis=2)
        both = jnp.concatenate([tail, upper], axis=1).reshape(embeds, LANES)
        emb[:, LANES:] = both[:, :rest]
        feats = emb[...]
        gram = lax.dot_general(feats, feats, TURN, preferred_element_type=f32)
        hmat = lax.dot_general(other[...], sides[...], TURN, preferred_element_type=f32)
        masked = (mask[...] * gram).astype(bf16)
        sym = (mask[...] * hmat).astype(bf16)
        both = jnp.dot(masked, sides[...], preferred_element_type=f32)
        dfeat = jnp.dot(sym, feats, preferred_element_type=f32).astype(bf16)
        share = each // HALVES
        y_ref = y_refs[j // share]
        start, second = j % share * packed, share * packed + j % share * tile
        y_ref[:, pl.ds(second, tile)] = both[:, :LANES].astype(bf16).reshape(fields, tile, LANES)
        y_ref[:, pl.ds(start, tile)] = dfeat[:, :LANES].reshape(fields, tile, LANES)
        last = dfeat[:, LANES:].reshape(fields, tile, rest)
        y_ref[:, pl.ds(start + tile, half)] = jnp.concatenate([last[:, :half], last[:, half:]], axis=2)
        return both[:, LANES:]

    for j in range(each):
        grad[...] += sample(j, *sets[j % SETS])
    y_refs[0][:, base // HALVES :] = grad[...].astype(bf16).reshape(fields, tile, LANES)


def cast_rows(y_ref, rows_ref, peers):
    share = rows_ref.shape[0] // y_ref.shape[0]
    for p in peers:
        rows_ref[p * share : (p + 1) * share] = y_ref[p, :share].astype(jnp.float32)


def early_kernel(y_ref, mixed_hbm, rows_ref, sem):
    fields, length = mixed_hbm.shape[1:3]
    share = rows_ref.shape[0] // fields
    copy = pltpu.make_async_copy(y_ref.at[:, pl.ds(share, length)], mixed_hbm.at[0], sem)
    copy.start()
    cast_rows(y_ref, rows_ref, range(fields))
    copy.wait()


def late_kernel(y_hbm, rows_ref, _, mixed_hbm, dfeat_hbm, y, more, dfeat, sems):
    tile, width, samples = dfeat.shape
    rest = width - LANES
    packed = tile + tile // 2
    fields, length = mixed_hbm.shape[1:3]
    share = rows_ref.shape[0] // fields
    some = fields // GROUPS
    loads = []
    for g in range(GROUPS):
        here = pl.ds(g * some, some)
        loads.append(pltpu.make_async_copy(y_hbm.at[here], y.at[here], sems.at[2 * GROUPS + g]))
        loads[-1].start()
    copies = []
    for g in range(GROUPS):
        here = pl.ds(g * some, some)
        loads[g].wait()
        copy = pltpu.make_async_copy(
            y.at[here, pl.ds(share, length)], mixed_hbm.at[1, here], sems.at[3 * GROUPS + g]
        )
        copy.start()
        copies.append(copy)
        cast_rows(y, more, range(g * some, (g + 1) * some))

    def block(row):
        halves = [
            ref[pl.ds(row, samples // HALVES, stride=packed), :] for ref in (rows_ref, more)
        ]
        return jnp.concatenate(halves, axis=0).astype(jnp.bfloat16).T

    for g, (low, high, size) in enumerate(row_groups(tile)):
        for r in range(size):
            for row in (low + r, high + r):
                dfeat[row, :LANES] = block(row)
            both = block(tile + low + r)
            dfeat[low + r, LANES:] = both[:rest]
            dfeat[high + r, LANES:] = both[rest:]
        for h, start in enumerate((low, high)):
            copy = pltpu.make_async_copy(
                dfeat.at[pl.ds(start, size)], dfeat_hbm.at[pl.ds(start, size)], sems.at[2 * g + h]
            )
            copy.start()
            copies.append(copy)
    for copy in copies:
        copy.wait()


def dp_sum(own):
    size = lax.axis_size("dp")

    def partner(value, flip):
        return lax.ppermute(value, "dp", [(i, i ^ flip) for i in range(size)])

    if size != 2 * ALONG_X:
        return lax.psum(own, "dp")
    total = (own + partner(own, 1)) + (partner(own, 2) + partner(own, 3))
    return total + partner(total, ALONG_X)


def per_device(emb, comp, cot, pairs, counts):
    samp_rows, tile, width = emb.shape
    fields = lax.axis_size("field")
    embeds = tile * fields
    packed = tile + tile // 2
    rows = packed + tile
    each = samp_rows // fields
    f32, bf16 = jnp.float32, jnp.bfloat16
    params = pltpu.CompilerParams(vmem_limit_bytes=24 * MIB)
    vmem = pl.BlockSpec(memory_space=pltpu.VMEM)
    smem = pl.BlockSpec(memory_space=pltpu.SMEM)
    hbm = pl.BlockSpec(memory_space=pltpu.HBM)
    turned = pltpu.VMEM((packed * samp_rows, LANES), f32)
    by_row = pltpu.VMEM((tile, width, samp_rows), bf16)

    def stay(array):
        return pltpu.with_memory_space_constraint(array, pltpu.HBM)

    def cost(flops, moved):
        return pl.CostEstimate(flops=flops, bytes_accessed=moved, transcendentals=0)

    x = pl.pallas_call(
        pack_kernel,
        out_shape=jax.ShapeDtypeStruct((fields, each * rows + tile + TABLE, LANES), bf16),
        in_specs=[hbm, hbm, hbm, hbm, smem],
        out_specs=vmem,
        scratch_shapes=[
            by_row,
            pltpu.VMEM(comp.shape, bf16),
            pltpu.VMEM(pairs.shape[::-1], jnp.int32),
            turned,
            pltpu.SemaphoreType.DMA((2 * GROUPS + 2 + HALVES,)),
        ],
        compiler_params=pltpu.CompilerParams(vmem_limit_bytes=24 * MIB),
        cost_estimate=cost(10**9, 8 * 10**6),
    )(
        stay(jnp.transpose(emb, (1, 2, 0))),
        stay(cot.reshape(HALVES, fields, each // HALVES * tile, LANES)),
        stay(comp),
        stay(pairs.T),
        counts,
    )
    x = lax.all_to_all(x, "field", 0, 0)
    y, z = pl.pallas_call(
        functools.partial(block_kernel, width ** (-0.5), tile, width),
        out_shape=(
            jax.ShapeDtypeStruct((fields, each // HALVES * rows + tile, LANES), bf16),
            jax.ShapeDtypeStruct((fields, each // HALVES * rows, LANES), bf16),
        ),
        in_specs=[vmem],
        out_specs=(vmem, vmem),
        scratch_shapes=[pltpu.VMEM((embeds, embeds), f32), pltpu.VMEM((embeds, LANES), f32)]
        + [
            pltpu.VMEM((embeds, width), bf16),
            pltpu.VMEM((embeds, 2 * LANES), bf16),
            pltpu.VMEM((embeds, 2 * LANES), bf16),
        ]
        * SETS,
        compiler_params=params,
        cost_estimate=cost(4 * 10**9, 6 * 10**6),
    )(x)
    y = lax.all_to_all(y, "field", 0, 0)
    y, z = lax.optimization_barrier((y, z))
    z = lax.all_to_all(z, "field", 0, 0)
    grad = dp_sum(jnp.sum(y[:, each // HALVES * rows :].astype(f32), axis=0))
    weight_grad = grad / (samp_rows * lax.axis_size("dp"))

    mixed_out = jax.ShapeDtypeStruct((HALVES, fields, each // HALVES * tile, LANES), bf16)
    half_rows = (packed * samp_rows // HALVES, LANES)
    mixed, sorted_rows = pl.pallas_call(
        early_kernel,
        out_shape=(mixed_out, jax.ShapeDtypeStruct(half_rows, f32)),
        in_specs=[vmem],
        out_specs=(hbm, vmem),
        scratch_shapes=[pltpu.SemaphoreType.DMA],
        compiler_params=params,
        cost_estimate=cost(10**8, 4 * 10**6),
    )(y)
    mixed, emb_grad = pl.pallas_call(
        late_kernel,
        out_shape=(mixed_out, jax.ShapeDtypeStruct((tile, width, samp_rows), bf16)),
        in_specs=[hbm, vmem, hbm],
        out_specs=(hbm, hbm),
        input_output_aliases={2: 0},
        scratch_shapes=[
            pltpu.VMEM(z.shape, bf16),
            pltpu.VMEM(half_rows, f32),
            by_row,
            pltpu.SemaphoreType.DMA((4 * GROUPS,)),
        ],
        compiler_params=params,
        cost_estimate=cost(10**9, 8 * 10**6),
    )(stay(z), sorted_rows, mixed)
    return mixed.reshape(cot.shape), jnp.transpose(emb_grad, (2, 0, 1)), weight_grad


def solution(mesh):
    in_specs = (
        P("dp", "field", None),
        P("field", None),
        P("dp", "field", None),
        P("field", None),
        P("field"),
    )
    out_specs = (P("dp", "field", None), P("dp", "field", None), P("field", None))
    return jax.shard_map(
        per_device, mesh=mesh, in_specs=in_specs, out_specs=out_specs, check_vma=False
    )
```

```python
import functools

import jax
import jax.numpy as jnp
from jax import lax
from jax.experimental import pallas as pl
from jax.experimental.pallas import tpu as pltpu
from jax.sharding import PartitionSpec as P

LANES = 128
GROUPS = 4
HALVES = 2
SETS = 4
ALONG_X = 4
TABLE = 16
TURN = (((1,), (1,)), ((), ()))
MIB = 1024 * 1024


def row_groups(tile):
    size = tile // 2 // GROUPS
    return [(g * size, tile // 2 + g * size, size) for g in range(GROUPS)]


def pack_kernel(emb_hbm, cot_hbm, comp_hbm, pairs_hbm, counts_ref, out_ref, emb, comp, pairs, turned, sems):
    tile, width, samples = emb.shape
    fields = out_ref.shape[0]
    each = samples // fields
    packed = tile + tile // 2
    f32, bf16 = jnp.float32, jnp.bfloat16
    groups = row_groups(tile)
    loads = [
        pltpu.make_async_copy(
            emb_hbm.at[pl.ds(start, size)], emb.at[pl.ds(start, size)], sems.at[2 * g + h]
        )
        for g, (low, high, size) in enumerate(groups)
        for h, start in enumerate((low, high))
    ]
    length = each // HALVES * tile
    others = [
        pltpu.make_async_copy(comp_hbm, comp, sems.at[2 * GROUPS]),
        pltpu.make_async_copy(pairs_hbm, pairs, sems.at[2 * GROUPS + 1]),
    ] + [
        pltpu.make_async_copy(
            cot_hbm.at[h],
            out_ref.at[:, pl.ds(each * packed + h * length, length)],
            sems.at[2 * GROUPS + 2 + h],
        )
        for h in range(HALVES)
    ]
    for copy in others[:2] + loads + others[2:]:
        copy.start()
    for copy in others[:2]:
        copy.wait()
    slots = pairs.shape[1]
    number = lax.broadcasted_iota(jnp.int32, (LANES, slots), 0)
    live = lax.broadcasted_iota(jnp.int32, (LANES, slots), 1) < counts_ref[0]
    first = jnp.where((pairs[0:1] == number) & live, 1.0, 0.0).astype(bf16)
    second = jnp.where(pairs[1:2] == number, 1.0, 0.0).astype(bf16)
    table = lax.dot_general(first, second, TURN, preferred_element_type=f32)
    base = each * (packed + tile)
    for p in range(fields):
        out_ref[p, base : base + tile] = comp[...]
        out_ref[p, base + tile : base + tile + TABLE] = table[:TABLE].astype(bf16)
    for g, (low, high, size) in enumerate(groups):
        loads[2 * g].wait()
        loads[2 * g + 1].wait()
        for r in range(size):
            blocks = [
                (low + r, emb[low + r, :LANES]),
                (high + r, emb[high + r, :LANES]),
                (
                    tile + low + r,
                    jnp.concatenate([emb[low + r, LANES:], emb[high + r, LANES:]], axis=0),
                ),
            ]
            for place, block in blocks:
                turned[place * samples : (place + 1) * samples] = block.T.astype(f32)

    def peer(p, carry):
        for j in range(each):
            half, rank = divmod(j, each // HALVES)
            number = half * (samples // HALVES) + p * (each // HALVES) + rank
            both = turned[pl.ds(number, packed, stride=samples), :]
            out_ref[p, j * packed : (j + 1) * packed] = both.astype(bf16)
        return carry

    lax.fori_loop(0, fields, peer, 0)
    for copy in others[2:]:
        copy.wait()


def pair_mask(x_ref, base, scale, mask, tile):
    fields = x_ref.shape[0]
    f32 = jnp.float32
    table = jnp.zeros((TABLE, LANES), f32)
    for f in range(fields):
        table += x_ref[f, base : base + TABLE].astype(f32)
    square = jnp.concatenate([table, jnp.zeros((LANES - TABLE, LANES), f32)], axis=0)
    on_diag = lax.broadcasted_iota(jnp.int32, square.shape, 0) == lax.broadcasted_iota(
        jnp.int32, square.shape, 1
    )
    mult = (square + square.T - jnp.where(on_diag, square, 0.0)) * scale
    for a in range(fields):
        row = jnp.concatenate(
            [jnp.broadcast_to(mult[a : a + 1, b : b + 1], (1, tile)) for b in range(fields)], axis=1
        )
        mask[a * tile : (a + 1) * tile] = jnp.broadcast_to(row, (tile, row.shape[1]))


def block_kernel(scale, tile, width, x_ref, *refs):
    fields = x_ref.shape[0]
    half, rest = tile // 2, width - LANES
    packed = tile + half
    rows = packed + tile
    embeds = fields * tile
    f32, bf16 = jnp.float32, jnp.bfloat16
    each = (x_ref.shape[1] - tile - TABLE) // rows
    base = each * rows
    y_refs, (mask, grad), sets = refs[:HALVES], refs[HALVES : HALVES + 2], refs[HALVES + 2 :]
    sets = [sets[i : i + 3] for i in range(0, len(sets), 3)]
    pair_mask(x_ref, base + tile, scale, mask, tile)
    weights = x_ref[:, base : base + tile].reshape(embeds, LANES)
    for _, sides, other in sets:
        sides[:, :LANES] = weights
        other[:, LANES:] = weights
    grad[...] = jnp.zeros_like(grad)

    def sample(j, emb, sides, other):
        start, second = j * packed, each * packed + j * tile
        emb[:, :LANES] = x_ref[:, pl.ds(start, tile)].reshape(embeds, LANES)
        cot = x_ref[:, pl.ds(second, tile)].reshape(embeds, LANES)
        sides[:, LANES:] = cot
        other[:, :LANES] = cot
        tail = x_ref[:, pl.ds(start + tile, half)]
        upper = jnp.concatenate([tail[:, :, rest:], tail[:, :, :rest]], axis=2)
        both = jnp.concatenate([tail, upper], axis=1).reshape(embeds, LANES)
        emb[:, LANES:] = both[:, :rest]
        feats = emb[...]
        gram = lax.dot_general(feats, feats, TURN, preferred_element_type=f32)
        hmat = lax.dot_general(other[...], sides[...], TURN, preferred_element_type=f32)
        masked = (mask[...] * gram).astype(bf16)
        sym = (mask[...] * hmat).astype(bf16)
        both = jnp.dot(masked, sides[...], preferred_element_type=f32)
        dfeat = jnp.dot(sym, feats, preferred_element_type=f32).astype(bf16)
        share = each // HALVES
        y_ref = y_refs[j // share]
        start, second = j % share * packed, share * packed + j % share * tile
        y_ref[:, pl.ds(second, tile)] = both[:, :LANES].astype(bf16).reshape(fields, tile, LANES)
        y_ref[:, pl.ds(start, tile)] = dfeat[:, :LANES].reshape(fields, tile, LANES)
        last = dfeat[:, LANES:].reshape(fields, tile, rest)
        y_ref[:, pl.ds(start + tile, half)] = jnp.concatenate([last[:, :half], last[:, half:]], axis=2)
        return both[:, LANES:]

    for j in range(each):
        grad[...] += sample(j, *sets[j % SETS])
    y_refs[0][:, base // HALVES :] = grad[...].astype(bf16).reshape(fields, tile, LANES)


def cast_rows(y_ref, rows_ref):
    fields = y_ref.shape[0]
    share = rows_ref.shape[0] // fields
    for p in range(fields):
        rows_ref[p * share : (p + 1) * share] = y_ref[p, :share].astype(jnp.float32)


def early_kernel(y_ref, mixed_hbm, rows_hbm, rows, sems):
    fields, length = mixed_hbm.shape[1:3]
    share = rows.shape[0] // fields
    copy = pltpu.make_async_copy(
        y_ref.at[:, pl.ds(share, length)], mixed_hbm.at[0], sems.at[0]
    )
    copy.start()
    cast_rows(y_ref, rows)
    store = pltpu.make_async_copy(rows, rows_hbm, sems.at[1])
    store.start()
    copy.wait()
    store.wait()


def late_kernel(y_ref, rows_hbm, _, mixed_hbm, dfeat_hbm, rows_ref, more, dfeat, sems):
    tile, width, samples = dfeat.shape
    rest = width - LANES
    packed = tile + tile // 2
    fields, length = mixed_hbm.shape[1:3]
    share = rows_ref.shape[0] // fields
    load = pltpu.make_async_copy(rows_hbm, rows_ref, sems.at[2 * GROUPS + 1])
    load.start()
    copies = [
        pltpu.make_async_copy(
            y_ref.at[:, pl.ds(share, length)], mixed_hbm.at[1], sems.at[2 * GROUPS]
        )
    ]
    copies[0].start()
    cast_rows(y_ref, more)
    load.wait()

    def block(row):
        halves = [
            ref[pl.ds(row, samples // HALVES, stride=packed), :] for ref in (rows_ref, more)
        ]
        return jnp.concatenate(halves, axis=0).astype(jnp.bfloat16).T

    for g, (low, high, size) in enumerate(row_groups(tile)):
        for r in range(size):
            for row in (low + r, high + r):
                dfeat[row, :LANES] = block(row)
            both = block(tile + low + r)
            dfeat[low + r, LANES:] = both[:rest]
            dfeat[high + r, LANES:] = both[rest:]
        for h, start in enumerate((low, high)):
            copy = pltpu.make_async_copy(
                dfeat.at[pl.ds(start, size)], dfeat_hbm.at[pl.ds(start, size)], sems.at[2 * g + h]
            )
            copy.start()
            copies.append(copy)
    for copy in copies:
        copy.wait()


def dp_sum(own):
    size = lax.axis_size("dp")

    def partner(value, flip):
        return lax.ppermute(value, "dp", [(i, i ^ flip) for i in range(size)])

    if size != 2 * ALONG_X:
        return lax.psum(own, "dp")
    total = (own + partner(own, 1)) + (partner(own, 2) + partner(own, 3))
    return total + partner(total, ALONG_X)


def per_device(emb, comp, cot, pairs, counts):
    samp_rows, tile, width = emb.shape
    fields = lax.axis_size("field")
    embeds = tile * fields
    packed = tile + tile // 2
    rows = packed + tile
    each = samp_rows // fields
    f32, bf16 = jnp.float32, jnp.bfloat16
    params = pltpu.CompilerParams(vmem_limit_bytes=24 * MIB)
    vmem = pl.BlockSpec(memory_space=pltpu.VMEM)
    smem = pl.BlockSpec(memory_space=pltpu.SMEM)
    hbm = pl.BlockSpec(memory_space=pltpu.HBM)
    turned = pltpu.VMEM((packed * samp_rows, LANES), f32)
    by_row = pltpu.VMEM((tile, width, samp_rows), bf16)

    def stay(array):
        return pltpu.with_memory_space_constraint(array, pltpu.HBM)

    def cost(flops, moved):
        return pl.CostEstimate(flops=flops, bytes_accessed=moved, transcendentals=0)

    x = pl.pallas_call(
        pack_kernel,
        out_shape=jax.ShapeDtypeStruct((fields, each * rows + tile + TABLE, LANES), bf16),
        in_specs=[hbm, hbm, hbm, hbm, smem],
        out_specs=vmem,
        scratch_shapes=[
            by_row,
            pltpu.VMEM(comp.shape, bf16),
            pltpu.VMEM(pairs.shape[::-1], jnp.int32),
            turned,
            pltpu.SemaphoreType.DMA((2 * GROUPS + 2 + HALVES,)),
        ],
        compiler_params=pltpu.CompilerParams(vmem_limit_bytes=24 * MIB),
        cost_estimate=cost(10**9, 8 * 10**6),
    )(
        stay(jnp.transpose(emb, (1, 2, 0))),
        stay(cot.reshape(HALVES, fields, each // HALVES * tile, LANES)),
        stay(comp),
        stay(pairs.T),
        counts,
    )
    x = lax.all_to_all(x, "field", 0, 0)
    y, z = pl.pallas_call(
        functools.partial(block_kernel, width ** (-0.5), tile, width),
        out_shape=(
            jax.ShapeDtypeStruct((fields, each // HALVES * rows + tile, LANES), bf16),
            jax.ShapeDtypeStruct((fields, each // HALVES * rows, LANES), bf16),
        ),
        in_specs=[vmem],
        out_specs=(vmem, vmem),
        scratch_shapes=[pltpu.VMEM((embeds, embeds), f32), pltpu.VMEM((embeds, LANES), f32)]
        + [
            pltpu.VMEM((embeds, width), bf16),
            pltpu.VMEM((embeds, 2 * LANES), bf16),
            pltpu.VMEM((embeds, 2 * LANES), bf16),
        ]
        * SETS,
        compiler_params=params,
        cost_estimate=cost(4 * 10**9, 6 * 10**6),
    )(x)
    y = lax.all_to_all(y, "field", 0, 0)
    y, z = lax.optimization_barrier((y, z))
    z = lax.all_to_all(z, "field", 0, 0)
    grad = dp_sum(jnp.sum(y[:, each // HALVES * rows :].astype(f32), axis=0))
    weight_grad = grad / (samp_rows * lax.axis_size("dp"))

    mixed_out = jax.ShapeDtypeStruct((HALVES, fields, each // HALVES * tile, LANES), bf16)
    half_rows = (packed * samp_rows // HALVES, LANES)
    mixed, sorted_rows = pl.pallas_call(
        early_kernel,
        out_shape=(mixed_out, jax.ShapeDtypeStruct(half_rows, f32)),
        in_specs=[vmem],
        out_specs=(hbm, hbm),
        scratch_shapes=[pltpu.VMEM(half_rows, f32), pltpu.SemaphoreType.DMA((2,))],
        compiler_params=params,
        cost_estimate=cost(10**8, 4 * 10**6),
    )(y)
    mixed, emb_grad = pl.pallas_call(
        late_kernel,
        out_shape=(mixed_out, jax.ShapeDtypeStruct((tile, width, samp_rows), bf16)),
        in_specs=[vmem, hbm, hbm],
        out_specs=(hbm, hbm),
        input_output_aliases={2: 0},
        scratch_shapes=[
            pltpu.VMEM(half_rows, f32),
            pltpu.VMEM(half_rows, f32),
            by_row,
            pltpu.SemaphoreType.DMA((2 * GROUPS + 2,)),
        ],
        compiler_params=params,
        cost_estimate=cost(10**9, 8 * 10**6),
    )(z, stay(sorted_rows), mixed)
    return mixed.reshape(cot.shape), jnp.transpose(emb_grad, (2, 0, 1)), weight_grad


def solution(mesh):
    in_specs = (
        P("dp", "field", None),
        P("field", None),
        P("dp", "field", None),
        P("field", None),
        P("field"),
    )
    out_specs = (P("dp", "field", None), P("dp", "field", None), P("field", None))
    return jax.shard_map(
        per_device, mesh=mesh, in_specs=in_specs, out_specs=out_specs, check_vma=False
    )
```

```python
import functools

import jax
import jax.numpy as jnp
from jax import lax
from jax.experimental import pallas as pl
from jax.experimental.pallas import tpu as pltpu
from jax.sharding import PartitionSpec as P

LANES = 128
GROUPS = 4
HALVES = 2
SETS = 4
ALONG_X = 4
TABLE = 16
TURN = (((1,), (1,)), ((), ()))
MIB = 1024 * 1024


def row_groups(tile):
    size = tile // 2 // GROUPS
    return [(g * size, tile // 2 + g * size, size) for g in range(GROUPS)]


def pack_kernel(emb_hbm, cot_hbm, comp_hbm, pairs_hbm, counts_ref, out_ref, emb, comp, pairs, turned, sems):
    tile, width, samples = emb.shape
    fields = out_ref.shape[0]
    each = samples // fields
    packed = tile + tile // 2
    f32, bf16 = jnp.float32, jnp.bfloat16
    groups = row_groups(tile)
    loads = [
        pltpu.make_async_copy(
            emb_hbm.at[pl.ds(start, size)], emb.at[pl.ds(start, size)], sems.at[2 * g + h]
        )
        for g, (low, high, size) in enumerate(groups)
        for h, start in enumerate((low, high))
    ]
    length = each // HALVES * tile
    others = [
        pltpu.make_async_copy(comp_hbm, comp, sems.at[2 * GROUPS]),
        pltpu.make_async_copy(pairs_hbm, pairs, sems.at[2 * GROUPS + 1]),
    ] + [
        pltpu.make_async_copy(
            cot_hbm.at[h],
            out_ref.at[:, pl.ds(each * packed + h * length, length)],
            sems.at[2 * GROUPS + 2 + h],
        )
        for h in range(HALVES)
    ]
    for copy in others[:2] + loads + others[2:]:
        copy.start()
    for copy in others[:2]:
        copy.wait()
    slots = pairs.shape[1]
    number = lax.broadcasted_iota(jnp.int32, (LANES, slots), 0)
    live = lax.broadcasted_iota(jnp.int32, (LANES, slots), 1) < counts_ref[0]
    first = jnp.where((pairs[0:1] == number) & live, 1.0, 0.0).astype(bf16)
    second = jnp.where(pairs[1:2] == number, 1.0, 0.0).astype(bf16)
    table = lax.dot_general(first, second, TURN, preferred_element_type=f32)
    base = each * (packed + tile)
    for p in range(fields):
        out_ref[p, base : base + tile] = comp[...]
        out_ref[p, base + tile : base + tile + TABLE] = table[:TABLE].astype(bf16)
    for g, (low, high, size) in enumerate(groups):
        loads[2 * g].wait()
        loads[2 * g + 1].wait()
        for r in range(size):
            blocks = [
                (low + r, emb[low + r, :LANES]),
                (high + r, emb[high + r, :LANES]),
                (
                    tile + low + r,
                    jnp.concatenate([emb[low + r, LANES:], emb[high + r, LANES:]], axis=0),
                ),
            ]
            for place, block in blocks:
                turned[place * samples : (place + 1) * samples] = block.T.astype(f32)

    def peer(p, carry):
        for j in range(each):
            half, rank = divmod(j, each // HALVES)
            number = half * (samples // HALVES) + p * (each // HALVES) + rank
            both = turned[pl.ds(number, packed, stride=samples), :]
            out_ref[p, j * packed : (j + 1) * packed] = both.astype(bf16)
        return carry

    lax.fori_loop(0, fields, peer, 0)
    for copy in others[2:]:
        copy.wait()


def pair_mask(x_ref, base, scale, mask, tile):
    fields = x_ref.shape[0]
    f32 = jnp.float32
    table = jnp.zeros((TABLE, LANES), f32)
    for f in range(fields):
        table += x_ref[f, base : base + TABLE].astype(f32)
    square = jnp.concatenate([table, jnp.zeros((LANES - TABLE, LANES), f32)], axis=0)
    on_diag = lax.broadcasted_iota(jnp.int32, square.shape, 0) == lax.broadcasted_iota(
        jnp.int32, square.shape, 1
    )
    mult = (square + square.T - jnp.where(on_diag, square, 0.0)) * scale
    for a in range(fields):
        row = jnp.concatenate(
            [jnp.broadcast_to(mult[a : a + 1, b : b + 1], (1, tile)) for b in range(fields)], axis=1
        )
        mask[a * tile : (a + 1) * tile] = jnp.broadcast_to(row, (tile, row.shape[1]))


def block_kernel(scale, tile, width, x_ref, *refs):
    fields = x_ref.shape[0]
    half, rest = tile // 2, width - LANES
    packed = tile + half
    rows = packed + tile
    embeds = fields * tile
    f32, bf16 = jnp.float32, jnp.bfloat16
    each = (x_ref.shape[1] - tile - TABLE) // rows
    base = each * rows
    y_refs, (mask, grad), sets = refs[:HALVES], refs[HALVES : HALVES + 2], refs[HALVES + 2 :]
    sets = [sets[i : i + 3] for i in range(0, len(sets), 3)]
    pair_mask(x_ref, base + tile, scale, mask, tile)
    weights = x_ref[:, base : base + tile].reshape(embeds, LANES)
    for _, sides, other in sets:
        sides[:, :LANES] = weights
        other[:, LANES:] = weights
    grad[...] = jnp.zeros_like(grad)

    def sample(j, emb, sides, other):
        start, second = j * packed, each * packed + j * tile
        emb[:, :LANES] = x_ref[:, pl.ds(start, tile)].reshape(embeds, LANES)
        cot = x_ref[:, pl.ds(second, tile)].reshape(embeds, LANES)
        sides[:, LANES:] = cot
        other[:, :LANES] = cot
        tail = x_ref[:, pl.ds(start + tile, half)]
        upper = jnp.concatenate([tail[:, :, rest:], tail[:, :, :rest]], axis=2)
        both = jnp.concatenate([tail, upper], axis=1).reshape(embeds, LANES)
        emb[:, LANES:] = both[:, :rest]
        feats = emb[...]
        gram = lax.dot_general(feats, feats, TURN, preferred_element_type=f32)
        hmat = lax.dot_general(other[...], sides[...], TURN, preferred_element_type=f32)
        masked = (mask[...] * gram).astype(bf16)
        sym = (mask[...] * hmat).astype(bf16)
        both = jnp.dot(masked, sides[...], preferred_element_type=f32)
        dfeat = jnp.dot(sym, feats, preferred_element_type=f32).astype(bf16)
        share = each // HALVES
        y_ref = y_refs[j // share]
        start, second = j % share * packed, share * packed + j % share * tile
        y_ref[:, pl.ds(second, tile)] = both[:, :LANES].astype(bf16).reshape(fields, tile, LANES)
        y_ref[:, pl.ds(start, tile)] = dfeat[:, :LANES].reshape(fields, tile, LANES)
        last = dfeat[:, LANES:].reshape(fields, tile, rest)
        y_ref[:, pl.ds(start + tile, half)] = jnp.concatenate([last[:, :half], last[:, half:]], axis=2)
        return both[:, LANES:]

    for j in range(each):
        grad[...] += sample(j, *sets[j % SETS])
    y_refs[0][:, base // HALVES :] = grad[...].astype(bf16).reshape(fields, tile, LANES)


def cast_rows(y_ref, rows_ref):
    fields = y_ref.shape[0]
    share = rows_ref.shape[0] // fields
    for p in range(fields):
        rows_ref[p * share : (p + 1) * share] = y_ref[p, :share].astype(rows_ref.dtype)


def early_kernel(y_ref, mixed_hbm, rows_ref, sem):
    fields, length = mixed_hbm.shape[1:3]
    share = rows_ref.shape[0] // fields
    copy = pltpu.make_async_copy(y_ref.at[:, pl.ds(share, length)], mixed_hbm.at[0], sem)
    copy.start()
    cast_rows(y_ref, rows_ref)
    copy.wait()


def late_kernel(y_ref, early_ref, _, mixed_hbm, dfeat_hbm, rows_ref, more, dfeat, sems):
    tile, width, samples = dfeat.shape
    rest = width - LANES
    packed = tile + tile // 2
    fields, length = mixed_hbm.shape[1:3]
    share = rows_ref.shape[0] // fields
    copies = [
        pltpu.make_async_copy(
            y_ref.at[:, pl.ds(share, length)], mixed_hbm.at[1], sems.at[2 * GROUPS]
        )
    ]
    copies[0].start()
    rows_ref[...] = early_ref[...].astype(jnp.float32)
    cast_rows(y_ref, more)

    def block(row):
        halves = [
            ref[pl.ds(row, samples // HALVES, stride=packed), :] for ref in (rows_ref, more)
        ]
        return jnp.concatenate(halves, axis=0).astype(jnp.bfloat16).T

    for g, (low, high, size) in enumerate(row_groups(tile)):
        for r in range(size):
            for row in (low + r, high + r):
                dfeat[row, :LANES] = block(row)
            both = block(tile + low + r)
            dfeat[low + r, LANES:] = both[:rest]
            dfeat[high + r, LANES:] = both[rest:]
        for h, start in enumerate((low, high)):
            copy = pltpu.make_async_copy(
                dfeat.at[pl.ds(start, size)], dfeat_hbm.at[pl.ds(start, size)], sems.at[2 * g + h]
            )
            copy.start()
            copies.append(copy)
    for copy in copies:
        copy.wait()


def dp_sum(own):
    size = lax.axis_size("dp")

    def partner(value, flip):
        return lax.ppermute(value, "dp", [(i, i ^ flip) for i in range(size)])

    if size != 2 * ALONG_X:
        return lax.psum(own, "dp")
    total = (own + partner(own, 1)) + (partner(own, 2) + partner(own, 3))
    return total + partner(total, ALONG_X)


def per_device(emb, comp, cot, pairs, counts):
    samp_rows, tile, width = emb.shape
    fields = lax.axis_size("field")
    embeds = tile * fields
    packed = tile + tile // 2
    rows = packed + tile
    each = samp_rows // fields
    f32, bf16 = jnp.float32, jnp.bfloat16
    params = pltpu.CompilerParams(vmem_limit_bytes=24 * MIB)
    vmem = pl.BlockSpec(memory_space=pltpu.VMEM)
    smem = pl.BlockSpec(memory_space=pltpu.SMEM)
    hbm = pl.BlockSpec(memory_space=pltpu.HBM)
    turned = pltpu.VMEM((packed * samp_rows, LANES), f32)
    by_row = pltpu.VMEM((tile, width, samp_rows), bf16)

    def stay(array):
        return pltpu.with_memory_space_constraint(array, pltpu.HBM)

    def cost(flops, moved):
        return pl.CostEstimate(flops=flops, bytes_accessed=moved, transcendentals=0)

    x = pl.pallas_call(
        pack_kernel,
        out_shape=jax.ShapeDtypeStruct((fields, each * rows + tile + TABLE, LANES), bf16),
        in_specs=[hbm, hbm, hbm, hbm, smem],
        out_specs=vmem,
        scratch_shapes=[
            by_row,
            pltpu.VMEM(comp.shape, bf16),
            pltpu.VMEM(pairs.shape[::-1], jnp.int32),
            turned,
            pltpu.SemaphoreType.DMA((2 * GROUPS + 2 + HALVES,)),
        ],
        compiler_params=pltpu.CompilerParams(vmem_limit_bytes=24 * MIB),
        cost_estimate=cost(10**9, 8 * 10**6),
    )(
        stay(jnp.transpose(emb, (1, 2, 0))),
        stay(cot.reshape(HALVES, fields, each // HALVES * tile, LANES)),
        stay(comp),
        stay(pairs.T),
        counts,
    )
    x = lax.all_to_all(x, "field", 0, 0)
    y, z = pl.pallas_call(
        functools.partial(block_kernel, width ** (-0.5), tile, width),
        out_shape=(
            jax.ShapeDtypeStruct((fields, each // HALVES * rows + tile, LANES), bf16),
            jax.ShapeDtypeStruct((fields, each // HALVES * rows, LANES), bf16),
        ),
        in_specs=[vmem],
        out_specs=(vmem, vmem),
        scratch_shapes=[pltpu.VMEM((embeds, embeds), f32), pltpu.VMEM((embeds, LANES), f32)]
        + [
            pltpu.VMEM((embeds, width), bf16),
            pltpu.VMEM((embeds, 2 * LANES), bf16),
            pltpu.VMEM((embeds, 2 * LANES), bf16),
        ]
        * SETS,
        compiler_params=params,
        cost_estimate=cost(4 * 10**9, 6 * 10**6),
    )(x)
    y = lax.all_to_all(y, "field", 0, 0)
    y, z = lax.optimization_barrier((y, z))
    z = lax.all_to_all(z, "field", 0, 0)
    grad = dp_sum(jnp.sum(y[:, each // HALVES * rows :].astype(f32), axis=0))
    weight_grad = grad / (samp_rows * lax.axis_size("dp"))

    mixed_out = jax.ShapeDtypeStruct((HALVES, fields, each // HALVES * tile, LANES), bf16)
    half_rows = (packed * samp_rows // HALVES, LANES)
    mixed, sorted_rows = pl.pallas_call(
        early_kernel,
        out_shape=(mixed_out, jax.ShapeDtypeStruct(half_rows, bf16)),
        in_specs=[vmem],
        out_specs=(hbm, vmem),
        scratch_shapes=[pltpu.SemaphoreType.DMA],
        compiler_params=params,
        cost_estimate=cost(10**8, 4 * 10**6),
    )(y)
    mixed, emb_grad = pl.pallas_call(
        late_kernel,
        out_shape=(mixed_out, jax.ShapeDtypeStruct((tile, width, samp_rows), bf16)),
        in_specs=[vmem, vmem, hbm],
        out_specs=(hbm, hbm),
        input_output_aliases={2: 0},
        scratch_shapes=[
            pltpu.VMEM(half_rows, f32),
            pltpu.VMEM(half_rows, f32),
            by_row,
            pltpu.SemaphoreType.DMA((2 * GROUPS + 1,)),
        ],
        compiler_params=params,
        cost_estimate=cost(10**9, 8 * 10**6),
    )(z, sorted_rows, mixed)
    return mixed.reshape(cot.shape), jnp.transpose(emb_grad, (2, 0, 1)), weight_grad


def solution(mesh):
    in_specs = (
        P("dp", "field", None),
        P("field", None),
        P("dp", "field", None),
        P("field", None),
        P("field"),
    )
    out_specs = (P("dp", "field", None), P("dp", "field", None), P("field", None))
    return jax.shard_map(
        per_device, mesh=mesh, in_specs=in_specs, out_specs=out_specs, check_vma=False
    )
```
